128 devices in a mesh: dp: 16 (over x, y), section: 2 (over z_hi), fsdp: 4 (over z_lo, core).
Axes of the slice: x: 4, y: 4, z: 4 (z_hi: 2, z_lo: 2; z = z_hi * 2 + z_lo), core: 2. Of those that a mesh axis runs over, the one named last changes fastest.
Arguments:
- block_input: bfloat16 [2, 16384, 960], P(None, ('dp', 'fsdp')), may hold values from -6 to 6
- cotangent: bfloat16 [2, 16384, 960], P(None, ('dp', 'fsdp')), may hold values from -6 to 6
- lengths: int32 [16, 2], P('dp'), may hold values from 512 to 1024, as said below
- w_query: bfloat16 [2, 960, 960], P('section', 'fsdp'), may hold values from -0.1875 to 0.1875
- w_key: bfloat16 [2, 960, 320], P('section', 'fsdp'), may hold values from -0.1875 to 0.1875
- w_value: bfloat16 [2, 960, 320], P('section', 'fsdp'), may hold values from -0.1875 to 0.1875
- w_out: bfloat16 [2, 960, 960], P('section', 'fsdp'), may hold values from -1.5 to 1.5
- w_gate: bfloat16 [2, 960, 2560], P('section', 'fsdp'), may hold values from -0.1875 to 0.1875
- w_up: bfloat16 [2, 960, 2560], P('section', 'fsdp'), may hold values from -0.1875 to 0.1875
- w_down: bfloat16 [2, 2560, 960], P('section', 'fsdp'), may hold values from -0.125 to 0.125
- gain_attn: bfloat16 [2, 960], P('section', 'fsdp'), may hold values from 0.5 to 1.5
- gain_mlp: bfloat16 [2, 960], P('section', 'fsdp'), may hold values from 0.5 to 1.5
Outputs:
- layer_out: bfloat16 [2, 2, 16384, 960], P('section', None, ('dp', 'fsdp'))
- input_grad: float32 [2, 2, 16384, 960], P('section', None, ('dp', 'fsdp'))
- query_grad: float32 [2, 960, 960], P('section', 'fsdp')
- key_grad: float32 [2, 960, 320], P('section', 'fsdp')
- value_grad: float32 [2, 960, 320], P('section', 'fsdp')
- out_grad: float32 [2, 960, 960], P('section', 'fsdp')
- gate_grad: float32 [2, 960, 2560], P('section', 'fsdp')
- up_grad: float32 [2, 960, 2560], P('section', 'fsdp')
- down_grad: float32 [2, 2560, 960], P('section', 'fsdp')
- attn_gain_grad: float32 [2, 960], P('section', 'fsdp')
- mlp_gain_grad: float32 [2, 960], P('section', 'fsdp')
The draws below stay inside these ranges and needn't reach their ends.
Inputs may be any that keep to these rules, and one draw needn't show every extreme that they name: Each entry is the live length of one sequence of 1024 slots, the rest padding; in every row of lengths one entry equals 1024.
All inputs are finite; a program needn't handle non-finite values.
Results may differ from the reference program's by a relative error of at most 0.03.
Values may be sent and summed in bfloat16 or wider, within the bound.
A program may use at most 320 MiB of HBM per device.

```python
import jax
import jax.numpy as jnp
from jax import lax

D = 960
HEADS = 15
KV_HEADS = 5
HEAD_DIM = 64
FF = 2560
MICRO = 2
SEQ = 1024
TOKENS = 16384
N_DP = 16


def draw_lengths(key, part):
    key = jax.random.fold_in(key, 7)
    first_key, second_key = jax.random.split(key)
    base = jax.random.randint(first_key, (N_DP, MICRO), SEQ // 2, SEQ + 1)
    chosen = jax.random.randint(second_key, (N_DP,), 0, MICRO)
    columns = jnp.arange(MICRO)[None, :]
    return jnp.where(columns == chosen[:, None], SEQ, base).astype(jnp.int32)


def shard_levels(key, extent, cuts, least, top_value):
    def one(position, parts):
        heights = jax.random.uniform(jax.random.fold_in(jax.random.fold_in(key, 6), position), (parts,), jnp.float32, least / len(cuts), top_value / len(cuts))
        return jnp.repeat(jnp.exp(heights), extent[position] // parts).reshape((-1,) + (1,) * (len(extent) - position - 1))

    gain = one(*cuts[0])
    for cut in cuts[1:]:
        gain = gain * one(*cut)
    return gain


def centred(own_key, dims, spread, bound, pieces=(), kind=jnp.bfloat16):
    gain = shard_levels(own_key, dims, pieces, -0.22, 0.18) if pieces else 1.0
    values = jax.random.normal(own_key, dims, jnp.float32) * spread * gain
    return jnp.minimum(jnp.maximum(values, -bound), bound).astype(kind)


def setup_inputs(seed: int = 0) -> dict:
    splits = jax.random.split(jax.random.key(seed), 13)
    return {
        "block_input": centred(splits[0], (MICRO, TOKENS, D), 1.0, 6.0, ((1, 64),)),
        "cotangent": centred(splits[1], (MICRO, TOKENS, D), 1.0, 6.0, ((1, 64),)),
        "lengths": draw_lengths(jax.random.fold_in(splits[12], 71), 0),
        "w_query": centred(splits[3], (2, D, D), D ** -0.5, 0.1875, ((0, 2), (1, 4))),
        "w_key": centred(splits[4], (2, D, KV_HEADS * HEAD_DIM), D ** -0.5, 0.1875, ((0, 2), (1, 4))),
        "w_value": centred(splits[5], (2, D, KV_HEADS * HEAD_DIM), D ** -0.5, 0.1875, ((0, 2), (1, 4))),
        "w_out": centred(splits[6], (2, D, D), (max(16 * D // SEQ, 1)) ** -0.5, 1.5, ((0, 2), (1, 4))),
        "w_gate": centred(splits[7], (2, D, FF), D ** -0.5, 0.1875, ((0, 2), (1, 4))),
        "w_up": centred(splits[8], (2, D, FF), D ** -0.5, 0.1875, ((0, 2), (1, 4))),
        "w_down": centred(splits[9], (2, FF, D), FF ** -0.5, 0.125, ((0, 2), (1, 4))),
        "gain_attn": jnp.clip(1.0 + 0.1 * jax.random.normal(splits[10], (2, D), jnp.float32), 0.5, 1.5).astype(jnp.bfloat16),
        "gain_mlp": jnp.clip(1.0 + 0.1 * jax.random.normal(splits[11], (2, D), jnp.float32), 0.5, 1.5).astype(jnp.bfloat16),
    }


norm_eps = 1e-05
rope_base = 10000.0
masked_score = -1e+30
highest = lax.Precision.HIGHEST

@jax.custom_vjp
def low(v):
    return lax.optimization_barrier(v.astype(jnp.bfloat16)).astype(jnp.float32)

@jax.custom_vjp
def low_back(v):
    return v

def low_keep(v):
    return (low(v), None)

def low_pass(kept, grad):
    return (grad,)

def back_keep(v):
    return (v, None)

def back_low(kept, grad):
    return (low(grad),)
low.defvjp(low_keep, low_pass)
low_back.defvjp(back_keep, back_low)

def rope_tables(places):
    half_dim = HEAD_DIM // 2
    frequencies = rope_base ** (-(jnp.arange(half_dim, dtype=jnp.float32) * 2.0) / HEAD_DIM)
    angles = places.astype(jnp.float32)[:, None] * frequencies[None, :]
    return (jnp.cos(angles), jnp.sin(angles))

def rotate_pairs(tensor, cosine, sines):
    half_dim = tensor.shape[-1] // 2
    first_half = tensor[..., :half_dim]
    second_half = tensor[..., half_dim:]
    cosine = cosine[:, None, :]
    sines = sines[:, None, :]
    return jnp.concatenate([first_half * cosine - second_half * sines, second_half * cosine + first_half * sines], axis=-1)

def decoder_layer(hidden, weights, cosine, sines, length):
    w_query, w_key, w_value, w_out, w_gate, w_up, w_down, gain_one, gain_two = weights
    row_count = hidden.shape[0]
    per_group = HEADS // KV_HEADS
    score_scale = HEAD_DIM ** (-0.5)
    inverse_one = lax.rsqrt(lax.optimization_barrier(jnp.mean(hidden * hidden, axis=-1, keepdims=True)) + norm_eps)
    normed_one = low(hidden * inverse_one * gain_one)
    queries = low_back(jnp.dot(normed_one, w_query, precision=highest))
    keys_flat = low_back(jnp.dot(normed_one, w_key, precision=highest))
    values_flat = low(low_back(jnp.dot(normed_one, w_value, precision=highest)))
    rot_queries = low(rotate_pairs(queries.reshape(row_count, HEADS, HEAD_DIM), cosine, sines))
    rot_queries = rot_queries.reshape(row_count, KV_HEADS, per_group, HEAD_DIM)
    rot_keys = low(rotate_pairs(keys_flat.reshape(row_count, KV_HEADS, HEAD_DIM), cosine, sines))
    values_all = values_flat.reshape(row_count, KV_HEADS, HEAD_DIM)
    scores = low_back(jnp.einsum('qgrd,kgd->grqk', rot_queries, rot_keys, precision=highest) * score_scale)
    places = jnp.arange(row_count)
    allowed = (places[None, :] <= places[:, None]) & (places[None, :] < length)
    masked = jnp.where(allowed, scores, masked_score)
    largest = lax.optimization_barrier(jnp.max(masked, axis=-1, keepdims=True))
    exp_scores = jnp.exp(masked - largest)
    probabilities = low(exp_scores / lax.optimization_barrier(jnp.sum(exp_scores, axis=-1, keepdims=True)))
    attended = jnp.einsum('grqk,kgd->qgrd', probabilities, values_all, precision=highest)
    attended = low_back(low(attended.reshape(row_count, HEADS * HEAD_DIM)))
    middle = hidden + low_back(jnp.dot(attended, w_out, precision=highest))
    inverse_two = lax.rsqrt(lax.optimization_barrier(jnp.mean(middle * middle, axis=-1, keepdims=True)) + norm_eps)
    normed_two = low(middle * inverse_two * gain_two)
    gate_proj = low_back(jnp.dot(normed_two, w_gate, precision=highest))
    up_proj = low_back(jnp.dot(normed_two, w_up, precision=highest))
    mixed_act = low(gate_proj * jax.nn.sigmoid(gate_proj) * up_proj)
    return middle + low_back(jnp.dot(mixed_act, w_down, precision=highest))

def two_layers(tokens_in, offset, first_weights, second_weights, cosine, sines, length):
    first_out = low(decoder_layer(tokens_in, first_weights, cosine, sines, length))
    second_in = low_back(first_out) + offset
    return (decoder_layer(second_in, second_weights, cosine, sines, length), first_out)

def reference(block_input, cotangent, lengths, w_query, w_key, w_value, w_out, w_gate, w_up, w_down, gain_attn, gain_mlp):
    stacked = (w_query, w_key, w_value, w_out, w_gate, w_up, w_down, gain_attn, gain_mlp)
    first_weights = tuple((item[0].astype(jnp.float32) for item in stacked))
    second_weights = tuple((item[1].astype(jnp.float32) for item in stacked))
    cosine, sines = rope_tables(jnp.arange(SEQ, dtype=jnp.int32))

    def to_sequences(array):
        return array.astype(jnp.float32).reshape(MICRO, N_DP, SEQ, D).transpose(1, 0, 2, 3).reshape(N_DP * MICRO, SEQ, D)

    def to_tokens(array):
        return array.reshape(N_DP, MICRO, SEQ, D).transpose(1, 0, 2, 3).reshape(MICRO, TOKENS, D)
    inputs_all = to_sequences(block_input)
    cotangents_all = to_sequences(cotangent)
    lengths_all = lengths.reshape(N_DP * MICRO).astype(jnp.int32)

    def one_sequence(totals, items):
        seq_input, seq_cot, length = items

        def forward(tokens_in, offset, first_set, second_set):
            return two_layers(tokens_in, offset, first_set, second_set, cosine, sines, length)
        output, pullback, first_out = jax.vjp(forward, seq_input, jnp.zeros_like(seq_input), first_weights, second_weights, has_aux=True)
        live = (jnp.arange(SEQ) < length).astype(jnp.float32)[:, None]
        grad_in, grad_second_in, grad_first, grad_second = pullback(seq_cot * live)
        totals = (jax.tree.map(jnp.add, totals[0], grad_first), jax.tree.map(jnp.add, totals[1], grad_second))
        return (totals, (first_out, output, grad_in, grad_second_in))
    zero_set = jax.tree.map(jnp.zeros_like, first_weights)
    totals, collected = lax.scan(one_sequence, (zero_set, zero_set), (inputs_all, cotangents_all, lengths_all))
    first_outs, outputs, grads_in, grads_second_in = collected
    layer_out = jnp.stack([to_tokens(first_outs), to_tokens(outputs)]).astype(jnp.bfloat16)
    input_grad = jnp.stack([to_tokens(grads_in), to_tokens(grads_second_in)])
    grads = tuple((jnp.stack([first_item, second_item]) for first_item, second_item in zip(totals[0], totals[1])))
    return (layer_out, input_grad, grads[0], grads[1], grads[2], grads[3], grads[4], grads[5], grads[6], grads[7], grads[8])
```

```python
import jax
import jax.numpy as jnp
from jax import lax
from jax.experimental import pallas as pl
from jax.experimental.pallas import tpu as pltpu
from jax.sharding import PartitionSpec as P

HEADS = 15
KV_HEADS = 5
GROUP = 3
HEAD_DIM = 64
D = 960
ROWS = 256
STRIP = 640
SEQ = 1024
norm_eps = 1e-05
rope_base = 10000.0
masked_score = -1e30
BF = jnp.bfloat16
F32 = jnp.float32


def dot(a, b):
    return jnp.dot(a, b, preferred_element_type=F32)


def dot_nt(a, b):
    return lax.dot_general(a, b, (((1,), (1,)), ((), ())), preferred_element_type=F32)


def lanes(rows=ROWS):
    return lax.broadcasted_iota(jnp.int32, (rows, 128), 1)


def turn(tile, cosine, signed, low_half):
    partner = jnp.where(low_half, pltpu.roll(tile, 96, 1), pltpu.roll(tile, 32, 1))
    return tile * cosine + partner * signed


def whole(shape):
    return pl.BlockSpec(shape, lambda *_: (0,) * len(shape))


def params(limit=56):
    return pltpu.CompilerParams(vmem_limit_bytes=limit * 2**20)


def front_body(hid, gain, w, cosine, signed, n1, q, kv):
    h = hid[...].astype(F32)
    inverse = lax.rsqrt(jnp.mean(h * h, axis=-1, keepdims=True) + norm_eps)
    n = (h * inverse * gain[...]).astype(BF)
    n1[...] = n
    proj = dot(n, w[0])
    lane = lanes()
    low = lane < 64
    half = lax.rem(lane, 64) < 32
    cos, sin = cosine[...], signed[...]
    tile = [proj[:, 128 * i : 128 * i + 128] for i in range(13)]
    turned = [turn(tile[i], cos, sin, half) if i < 3 or i > 4 else None for i in range(13)]
    for g in range(KV_HEADS):
        k_tile, v_tile = turned[g // 2], tile[(5 + g) // 2]
        if g % 2 == 0:
            both = jnp.where(low, k_tile, v_tile)
        else:
            both = pltpu.roll(jnp.where(low, v_tile, k_tile), 64, 1)
        kv[g] = both.astype(BF)
    for h in range(HEADS):
        t = turned[5 + h // 2] * (HEAD_DIM**-0.5)
        if h % 2:
            t = pltpu.roll(t, 64, 1)
        q[h // GROUP, h % GROUP * ROWS : (h % GROUP + 1) * ROWS] = jnp.where(low, t, 0.0).astype(BF)


def front(hid, gain, full, cosine, signed):
    return pl.pallas_call(
        front_body,
        grid=(1,),
        out_shape=(
            jax.ShapeDtypeStruct((ROWS, D), BF),
            jax.ShapeDtypeStruct((KV_HEADS, GROUP * ROWS, 128), BF),
            jax.ShapeDtypeStruct((KV_HEADS, ROWS, 128), BF),
        ),
        in_specs=[
            whole((ROWS, D)), whole((1, D)), whole((1, D, 1664)), whole((ROWS, 128)), whole((ROWS, 128)),
        ],
        out_specs=[whole((ROWS, D)), whole((KV_HEADS, GROUP * ROWS, 128)), whole((KV_HEADS, ROWS, 128))],
        compiler_params=params(),
        name="front",
    )(hid, gain, full, cosine, signed)


def allowed_keys(scal):
    key = lax.broadcasted_iota(jnp.int32, (SEQ, ROWS), 0)
    place = lax.broadcasted_iota(jnp.int32, (SEQ, ROWS), 1) + scal[0] * ROWS
    return (key <= place) & (key < scal[1])


def attend_body(scal, q, kv, out, lse):
    keys = kv[0]
    keys_t = keys.astype(F32).T.astype(BF)
    allowed = allowed_keys(scal)
    for r in range(GROUP):
        rows = slice(r * ROWS, (r + 1) * ROWS)
        s = jnp.where(allowed, dot_nt(keys, q[0, rows]), masked_score)
        top = jnp.max(s, axis=0, keepdims=True)
        e = jnp.exp(s - top)
        total = jnp.sum(e, axis=0, keepdims=True)
        o = dot(keys_t, e.astype(BF)) / total
        out[0, rows] = o.T.astype(BF)
        lse[0, r : r + 1] = top + jnp.log(total)


def attend(scal, q, kv):
    return pl.pallas_call(
        attend_body,
        grid_spec=pltpu.PrefetchScalarGridSpec(
            num_scalar_prefetch=1,
            grid=(KV_HEADS,),
            in_specs=[
                pl.BlockSpec((1, GROUP * ROWS, 128), lambda g, s: (g, 0, 0)),
                pl.BlockSpec((1, SEQ, 128), lambda g, s: (g, 0, 0)),
            ],
            out_specs=[
                pl.BlockSpec((1, GROUP * ROWS, 128), lambda g, s: (g, 0, 0)),
                pl.BlockSpec((1, 8, ROWS), lambda g, s: (g, 0, 0)),
            ],
        ),
        out_shape=(
            jax.ShapeDtypeStruct((KV_HEADS, GROUP * ROWS, 128), BF),
            jax.ShapeDtypeStruct((KV_HEADS, 8, ROWS), F32),
        ),
        compiler_params=params(),
        name="attend",
    )(scal, q, kv)


def rest_body(att, hid, gain, woa, wob, wg, wu, wd, out, middle, n2, gate, up, mixed, compact, acc):
    t = pl.program_id(0)

    @pl.when(t == 0)
    def _():
        low = lanes() < 64

        def head(h):
            return att[h // GROUP, h % GROUP * ROWS : (h % GROUP + 1) * ROWS].astype(F32)

        for h in range(0, HEADS - 1, 2):
            pair = jnp.where(low, pltpu.roll(head(h), 64, 1), head(h + 1))
            compact[:, 64 * h : 64 * h + 128] = pair.astype(BF)
        compact[:, 896:960] = pltpu.roll(head(HEADS - 1), 64, 1)[:, :64].astype(BF)
        a = compact[...]
        proj = jnp.concatenate([dot(a, woa[0]), dot(a, wob[0])], axis=1)[:, 64:]
        mid = hid[...].astype(F32) + proj
        middle[...] = mid
        inverse = lax.rsqrt(jnp.mean(mid * mid, axis=-1, keepdims=True) + norm_eps)
        n2[...] = (mid * inverse * gain[...]).astype(BF)
        acc[...] = mid

    n = n2[...]
    g = dot(n, wg[0])
    u = dot(n, wu[0])
    gate[...] = g.astype(BF)
    up[...] = u.astype(BF)
    mix = (g * jax.nn.sigmoid(g) * u).astype(BF)
    mixed[...] = mix
    acc[...] += dot_nt(mix, wd[0])

    @pl.when(t == pl.num_programs(0) - 1)
    def _():
        out[...] = acc[...].astype(BF)


def strip_of(m):
    return pl.BlockSpec((1, D, STRIP), lambda t, m=m: (m, 0, t))


def out_half(i):
    return pl.BlockSpec((1, D, 512), lambda t, i=i: (0, 0, i))


def column_strip():
    return pl.BlockSpec((ROWS, STRIP), lambda t: (0, t))


def rest(att, hid, gain, full):
    wide = jax.ShapeDtypeStruct((ROWS, 2560), BF)
    return pl.pallas_call(
        rest_body,
        grid=(4,),
        out_shape=(
            jax.ShapeDtypeStruct((ROWS, D), BF),
            jax.ShapeDtypeStruct((ROWS, D), F32),
            jax.ShapeDtypeStruct((ROWS, D), BF),
            wide, wide, wide,
            jax.ShapeDtypeStruct((ROWS, D), BF),
        ),
        in_specs=[
            whole((KV_HEADS, GROUP * ROWS, 128)), whole((ROWS, D)), whole((1, D)),
            out_half(3), out_half(4), strip_of(1), strip_of(2), strip_of(3),
        ],
        out_specs=[
            whole((ROWS, D)), whole((ROWS, D)), whole((ROWS, D)),
            column_strip(), column_strip(), column_strip(), whole((ROWS, D)),
        ],
        scratch_shapes=[pltpu.VMEM((ROWS, D), F32)],
        compiler_params=params(),
        name="rest",
    )(att, hid, gain, full, full, full, full, full)


def back_rest_body(g_out, mid_ref, gain, gate, up, woa, wob, wg, wu, wd, gg_out, gu_out, gm_out, gao_out, part, da, acc):
    t = pl.program_id(0)
    g = g_out[...]
    grad_mixed = dot(g, wd[0])
    ga = gate[...].astype(F32)
    sg = jax.nn.sigmoid(ga)
    scaled = grad_mixed * sg
    gg = (scaled * up[...].astype(F32) * (1.0 + ga * (1.0 - sg))).astype(BF)
    gu = (scaled * ga).astype(BF)
    gg_out[...] = gg
    gu_out[...] = gu
    term = dot_nt(gg, wg[0]) + dot_nt(gu, wu[0])

    @pl.when(t == 0)
    def _():
        acc[...] = term

    @pl.when(t > 0)
    def _():
        acc[...] += term

    @pl.when(t == pl.num_programs(0) - 1)
    def _():
        mid = mid_ref[...]
        inverse = lax.rsqrt(jnp.mean(mid * mid, axis=-1, keepdims=True) + norm_eps)
        unit = mid * inverse
        grad_normed = acc[...]
        part[...] = jnp.sum(grad_normed * unit, axis=0, keepdims=True)
        scaled_two = grad_normed * gain[...]
        gm = g.astype(F32) + inverse * (scaled_two - unit * jnp.mean(scaled_two * unit, axis=-1, keepdims=True))
        gm_out[...] = gm
        gao_out[...] = gm.astype(BF)
        shifted = jnp.concatenate([jnp.zeros((ROWS, 64), F32), gm], axis=1).astype(BF)
        att = dot_nt(shifted[:, :512], woa[0]) + dot_nt(shifted[:, 512:], wob[0])
        att = jnp.concatenate([att, jnp.zeros((ROWS, 64), F32)], axis=1)
        low = lanes() < 64
        for h in range(HEADS):
            tile = att[:, 128 * (h // 2) : 128 * (h // 2) + 128]
            if h % 2 == 0:
                tile = pltpu.roll(tile, 64, 1)
            da[h // GROUP, h % GROUP * ROWS : (h % GROUP + 1) * ROWS] = jnp.where(low, 0.0, tile).astype(BF)


def back_rest(g_out, mid, gain, gate, up, full):
    wide = jax.ShapeDtypeStruct((ROWS, 2560), BF)
    return pl.pallas_call(
        back_rest_body,
        grid=(4,),
        out_shape=(
            wide, wide,
            jax.ShapeDtypeStruct((ROWS, D), F32),
            jax.ShapeDtypeStruct((ROWS, D), BF),
            jax.ShapeDtypeStruct((1, D), F32),
            jax.ShapeDtypeStruct((KV_HEADS, GROUP * ROWS, 128), BF),
        ),
        in_specs=[
            whole((ROWS, D)), whole((ROWS, D)), whole((1, D)), column_strip(), column_strip(),
            out_half(3), out_half(4), strip_of(1), strip_of(2), strip_of(3),
        ],
        out_specs=[
            column_strip(), column_strip(), whole((ROWS, D)), whole((ROWS, D)), whole((1, D)),
            whole((KV_HEADS, GROUP * ROWS, 128)),
        ],
        scratch_shapes=[pltpu.VMEM((ROWS, D), F32)],
        compiler_params=params(),
        name="back_rest",
    )(g_out, mid, gain, gate, up, full, full, full, full, full)


def back_attend_body(scal, q, kv, lse, da, cosine, signed, dq, dkv):
    keys = kv[0]
    keys_t = keys.astype(F32).T.astype(BF)
    allowed = allowed_keys(scal)
    lane = lanes()
    half = lax.rem(lane, 64) < 32
    total = None
    for r in range(GROUP):
        rows = slice(r * ROWS, (r + 1) * ROWS)
        qr, dr = q[0, rows], da[0, rows]
        s = dot_nt(keys, qr)
        p = jnp.where(allowed, jnp.exp(s - lse[0, r : r + 1]), 0.0)
        dp = dot_nt(keys, dr)
        delta = jnp.sum(p * dp, axis=0, keepdims=True)
        ds = (p * (dp - delta)).astype(BF)
        term = dot(ds, qr) + dot(p.astype(BF), dr)
        total = term if total is None else total + term
        grad_q = (dot(keys_t, ds) * (HEAD_DIM**-0.5)).T
        dq[0, rows] = turn(grad_q, cosine[...], -signed[...], half).astype(BF)
    dkv[0] = total.astype(BF)


def back_attend(scal, q, kv, lse, da, cosine, signed):
    heads = pl.BlockSpec((1, GROUP * ROWS, 128), lambda g, s: (g, 0, 0))
    keys = pl.BlockSpec((1, SEQ, 128), lambda g, s: (g, 0, 0))
    table = pl.BlockSpec((ROWS, 128), lambda g, s: (0, 0))
    return pl.pallas_call(
        back_attend_body,
        grid_spec=pltpu.PrefetchScalarGridSpec(
            num_scalar_prefetch=1,
            grid=(KV_HEADS,),
            in_specs=[heads, keys, pl.BlockSpec((1, 8, ROWS), lambda g, s: (g, 0, 0)), heads, table, table],
            out_specs=[heads, keys],
        ),
        out_shape=(
            jax.ShapeDtypeStruct((KV_HEADS, GROUP * ROWS, 128), BF),
            jax.ShapeDtypeStruct((KV_HEADS, SEQ, 128), BF),
        ),
        compiler_params=params(),
        name="back_attend",
    )(scal, q, kv, lse, da, cosine, signed)


def back_front_body(dq, dkv, hid, gain, w, cosine, signed, gm, grad_in, packed, part):
    lane = lanes()
    low = lane < 64
    half = lax.rem(lane, 64) < 32
    cos, sin = cosine[...], -signed[...]
    both = [dkv[g] for g in range(KV_HEADS)]
    turned = [turn(b, cos, sin, half) for b in both]

    def merged(left, right):
        return jnp.where(low, left, right)

    def flip(v):
        return pltpu.roll(v, 64, 1)

    tiles = [
        merged(turned[0], flip(turned[1])),
        merged(turned[2], flip(turned[3])),
        merged(turned[4], both[0]),
        merged(flip(both[1]), both[2]),
        merged(flip(both[3]), both[4]),
    ]

    def head(h):
        return dq[h // GROUP, h % GROUP * ROWS : (h % GROUP + 1) * ROWS].astype(F32)

    for h in range(0, HEADS - 1, 2):
        tiles.append(merged(head(h), flip(head(h + 1))))
    tiles.append(merged(head(HEADS - 1), 0.0))
    for i, tile in enumerate(tiles):
        packed[:, 128 * i : 128 * i + 128] = tile.astype(BF)
    grad_normed = dot_nt(packed[...], w[0])
    h = hid[...].astype(F32)
    inverse = lax.rsqrt(jnp.mean(h * h, axis=-1, keepdims=True) + norm_eps)
    unit = h * inverse
    part[...] = jnp.sum(grad_normed * unit, axis=0, keepdims=True)
    scaled = grad_normed * gain[...]
    grad_in[...] = gm[...] + inverse * (scaled - unit * jnp.mean(scaled * unit, axis=-1, keepdims=True))


def back_front(dq, dkv, hid, gain, full, cosine, signed, gm):
    return pl.pallas_call(
        back_front_body,
        grid=(1,),
        out_shape=(
            jax.ShapeDtypeStruct((ROWS, D), F32),
            jax.ShapeDtypeStruct((ROWS, 1664), BF),
            jax.ShapeDtypeStruct((1, D), F32),
        ),
        in_specs=[
            whole((KV_HEADS, GROUP * ROWS, 128)), whole((KV_HEADS, ROWS, 128)), whole((ROWS, D)), whole((1, D)),
            whole((1, D, 1664)), whole((ROWS, 128)), whole((ROWS, 128)), whole((ROWS, D)),
        ],
        out_specs=[whole((ROWS, D)), whole((ROWS, 1664)), whole((1, D))],
        compiler_params=params(),
        name="back_front",
    )(dq, dkv, hid, gain, full, cosine, signed, gm)


def weight_body(scal, *refs):
    sets = [refs[3 * i : 3 * i + 3] for i in range(9)]
    n1, att, n2, gd, packed, gao, gg, gu, mixed = sets
    out, lhs, lhs_b = refs[27:]
    m, t = pl.program_id(0), pl.program_id(1)

    def each(fn):
        pl.when(scal[0] == 1)(lambda: fn(0))
        pl.when(scal[0] == 0)(lambda: fn(2))

    def flip_into(dst, trio):
        dst[:, ROWS:] = trio[1][...].astype(F32).T.astype(BF)

        def put(i):
            dst[:, :ROWS] = trio[i][...].astype(F32).T.astype(BF)

        each(put)

    for i, trio in enumerate((n1, n2, n2, gd)):
        if i == 2:
            continue

        @pl.when((m == i) & (t == 0))
        def _(i=i, trio=trio):
            flip_into(lhs, trio)
            if i == 0:
                flip_into(lhs_b, att)

    def product(left, trio, cols, dst):
        first = dot(left[:, ROWS:], trio[1][:, cols])

        def put(i):
            out[0, :, dst] = (first + dot(left[:, :ROWS], trio[i][:, cols])).astype(BF)

        each(put)

    everything = slice(0, STRIP)
    for tt in range(4):
        @pl.when((m == 0) & (t == tt))
        def _(tt=tt):
            if tt < 2:
                product(lhs, packed, slice(STRIP * tt, STRIP * tt + STRIP), everything)
            elif tt == 2:
                product(lhs, packed, slice(1280, 1600), slice(0, 320))
                product(lhs_b, gao, slice(0, 320), slice(320, 640))
            else:
                product(lhs_b, gao, slice(320, 960), everything)

    for i, trio in ((1, gg), (2, gu), (3, mixed)):
        @pl.when(m == i)
        def _(trio=trio):
            product(lhs, trio, everything, everything)


def weight_grads(scal, sets):
    def strips(i):
        return pl.BlockSpec((ROWS, STRIP), lambda m, t, s, i=i: (0, jnp.where(m == i, t, jnp.where(m < i, 0, 3))))

    def fixed(cols):
        return pl.BlockSpec((ROWS, cols), lambda m, t, s: (0, 0))

    specs = [fixed(D)] * 12 + [fixed(1664)] * 3 + [fixed(D)] * 3
    specs += [strips(1)] * 3 + [strips(2)] * 3 + [strips(3)] * 3
    return pl.pallas_call(
        weight_body,
        grid_spec=pltpu.PrefetchScalarGridSpec(
            num_scalar_prefetch=1,
            grid=(4, 4),
            in_specs=specs,
            out_specs=pl.BlockSpec((1, D, STRIP), lambda m, t, s: (m, 0, t)),
            scratch_shapes=[pltpu.VMEM((D, 2 * ROWS), BF), pltpu.VMEM((D, 2 * ROWS), BF)],
        ),
        out_shape=jax.ShapeDtypeStruct((4, D, 2560), BF),
        compiler_params=params(),
        name="weight_grads",
    )(scal, *[a for trio in sets for a in trio])


MESH = pl.DeviceIdType.MESH
SIDE = 4
OFFSETS = (1, 3, 2)
HALVES = ((0, 128), (128, 112))


class Spot:
    def __init__(self):
        d = lax.axis_index("dp")
        f = lax.axis_index("fsdp")
        self.x, self.y = d // SIDE, lax.rem(d, SIDE)
        self.zl, self.c = f // 2, lax.rem(f, 2)
        self.f = f
        self.core = {"fsdp": self.zl * 2 + 1 - self.c}
        self.z = {"fsdp": (1 - self.zl) * 2 + self.c}
        self.across = {"fsdp": (1 - self.zl) * 2 + 1 - self.c}

    def along_x(self, k):
        return {"dp": lax.rem(self.x + k, SIDE) * SIDE + self.y}

    def along_y(self, k):
        return {"dp": self.x * SIDE + lax.rem(self.y + k, SIDE)}

    def greet(self):
        barrier = pltpu.get_barrier_semaphore()
        ids = [self.core, self.z, self.across]
        for k in range(1, SIDE):
            ids += [self.along_x(k), self.along_y(k)]
        for who in ids:
            pl.semaphore_signal(barrier, inc=1, device_id=who, device_id_type=MESH)
        pl.semaphore_wait(barrier, len(ids))


class Mover:
    def __init__(self, send, recv):
        self.send, self.recv, self.pending = send, recv, []

    def push(self, src, dst, who):
        i = len(self.pending)
        copy = pltpu.make_async_remote_copy(
            src_ref=src, dst_ref=dst, send_sem=self.send.at[i], recv_sem=self.recv.at[i],
            device_id=who, device_id_type=MESH,
        )
        copy.start()
        self.pending.append(copy)
        return copy

    def finish(self):
        for copy in self.pending:
            copy.wait_send()


def region(stack, f, m, j, lo=0, size=240):
    tall = m // 3
    row = f + tall * (j - f)
    col = j + tall * (f - j)
    return stack.at[m, pl.ds(pl.multiple_of(row * 240 + lo, 16), size), pl.ds(pl.multiple_of(col * 640, 128), 640)]


def shard_parts(stack, packed, f):
    rows = pl.ds(pl.multiple_of(f * 240, 16), 240)
    parts = [(stack.at[m, rows], packed.at[m]) for m in range(3)]
    cols = pl.ds(pl.multiple_of(f * 640, 128), 640)
    for j in range(4):
        parts.append((stack.at[3, pl.ds(j * 240, 240), cols], packed.at[3, :, pl.ds(j * 640, 640)]))
    return parts


def gather_kernel(own, gains, full, gains_full, held, send, recv, local):
    spot = Spot()
    x, y, f = spot.x, spot.y, spot.f
    fz = (1 - spot.zl) * 2 + spot.c
    spot.greet()
    mover = Mover(send, recv)
    first = mover.push(own.at[x, :, pl.ds(pl.multiple_of(y * 640, 128), 640)], region(full, f, x, y), spot.z)
    waits = []
    for k in range(1, 4):
        who = {"fsdp": lax.rem(f + k, 4)}
        waits.append(mover.push(gains, gains_full.at[f], who))
    load = pltpu.make_async_copy(own, held, local.at[8])
    load.start()
    for there, here in shard_parts(full, own, f):
        waits.append(mover.push(here, there, spot.core))
    load.wait()
    locals_ = [pltpu.make_async_copy(gains, gains_full.at[f], local.at[0])]
    for i, (there, here) in enumerate(shard_parts(full, held, f)):
        locals_.append(pltpu.make_async_copy(here, there, local.at[1 + i]))
    for copy in locals_:
        copy.start()
    first.wait_recv()

    def onward(view):
        waits.append(mover.push(view, view, spot.core))

    stage_one = []
    for k in OFFSETS:
        a = region(full, fz, x, y, *HALVES[0])
        b = region(full, fz, x, y, *HALVES[1])
        stage_one.append((mover.push(a, a, spot.along_x(k)), mover.push(b, b, spot.along_y(k))))
    stage_two = []

    def second(m, j):
        a = region(full, fz, m, y, *HALVES[0])
        b = region(full, fz, x, j, *HALVES[1])
        for k in OFFSETS:
            stage_two.append((k, m, j, mover.push(a, a, spot.along_y(k)), mover.push(b, b, spot.along_x(k))))

    second(x, y)
    onward(region(full, fz, x, y))
    for k, (copy_a, copy_b) in zip(OFFSETS, stage_one):
        m, j = lax.rem(x + 4 - k, SIDE), lax.rem(y + 4 - k, SIDE)
        copy_a.wait_recv()
        copy_b.wait_recv()
        second(m, j)
        onward(region(full, fz, m, y, *HALVES[0]))
        onward(region(full, fz, x, j, *HALVES[1]))
    for k, m, j, copy_a, copy_b in stage_two:
        copy_a.wait_recv()
        onward(region(full, fz, m, lax.rem(y + 4 - k, SIDE), *HALVES[0]))
        copy_b.wait_recv()
        onward(region(full, fz, lax.rem(x + 4 - k, SIDE), j, *HALVES[1]))
    for copy in waits:
        copy.wait_recv()
    mover.finish()
    for copy in locals_:
        copy.wait()


def gather_weights(own, gains):
    n = 96
    return pl.pallas_call(
        gather_kernel,
        out_shape=(
            jax.ShapeDtypeStruct((4, 960, 2560), own.dtype),
            jax.ShapeDtypeStruct((4,) + gains.shape, gains.dtype),
        ),
        in_specs=[pl.BlockSpec(memory_space=pl.ANY), pl.BlockSpec(memory_space=pltpu.VMEM)],
        out_specs=[pl.BlockSpec(memory_space=pl.ANY), pl.BlockSpec(memory_space=pltpu.VMEM)],
        scratch_shapes=[
            pltpu.VMEM((4, 240, 2560), own.dtype),
            pltpu.SemaphoreType.DMA((n,)),
            pltpu.SemaphoreType.DMA((n,)),
            pltpu.SemaphoreType.DMA((9,)),
        ],
        compiler_params=pltpu.CompilerParams(collective_id=1, has_side_effects=True, vmem_limit_bytes=60 * 2**20),
        name="gather_weights",
    )(own, gains)


STEP = 16


def add_rows(out, rows, terms):
    def body(i, carry):
        sl = pl.ds(pl.multiple_of(i * STEP, STEP), STEP)
        total = terms[0](sl).astype(jnp.float32)
        for term in terms[1:]:
            total = total + term(sl).astype(jnp.float32)
        out(sl, total)
        return carry

    lax.fori_loop(0, rows // STEP, body, 0)


def reduce_kernel(grads, gains, out, gains_out, mine, theirs, rx, ry, ta, tb, rx2, ry2, ua, ub, rz,
                  g_core, g_mine, g_x, g_y, send, recv, local):
    spot = Spot()
    x, y, f = spot.x, spot.y, spot.f
    spot.greet()
    mover = Mover(send, recv)
    shards = (spot.zl, 1 - spot.zl)
    loads, core = [], []
    small = []
    for s, zl in enumerate(shards):
        keep, give = zl * 2 + spot.c, zl * 2 + 1 - spot.c
        core.append([mover.push(there, here, spot.core)
                     for there, here in shard_parts(grads, theirs.at[s], give)])
        part = []
        for i, (there, here) in enumerate(shard_parts(grads, mine.at[s], keep)):
            copy = pltpu.make_async_copy(there, here, local.at[s * 8 + i])
            copy.start()
            part.append(copy)
        loads.append(part)
        small.append(mover.push(gains.at[give], g_core.at[s], spot.core))
    for s, zl in enumerate(shards):
        small[s].wait_recv()
        g_mine[0, s] = gains[zl * 2 + spot.c] + g_core[s]
    gx = [mover.push(g_mine.at[0], g_x.at[i], spot.along_x(k)) for i, k in enumerate(OFFSETS)]

    def core_sum(s):
        for copy in loads[s]:
            copy.wait()
        for copy in core[s]:
            copy.wait_recv()
        for m in range(4):
            def put(sl, total, m=m):
                mine[s, m, sl] = total.astype(jnp.bfloat16)
            add_rows(put, 240, [lambda sl, m=m: mine[s, m, sl], lambda sl, m=m: theirs[s, m, sl]])

    core_sum(0)
    xs = [mover.push(mine.at[0, lax.rem(x + k, SIDE)], rx.at[i], spot.along_x(k)) for i, k in enumerate(OFFSETS)]
    core_sum(1)

    def strip(j):
        return pl.ds(pl.multiple_of(j * 640, 128), 640)

    ys = [mover.push(mine.at[1, :, :, strip(lax.rem(y + k, SIDE))], ry.at[i], spot.along_y(k))
          for i, k in enumerate(OFFSETS)]
    for copy in gx:
        copy.wait_recv()
    g_mine[1] = g_mine[0] + g_x[0] + g_x[1] + g_x[2]
    gy = [mover.push(g_mine.at[1], g_y.at[i], spot.along_y(k)) for i, k in enumerate(OFFSETS)]
    for copy in xs:
        copy.wait_recv()

    def put_ta(sl, total):
        ta[sl] = total.astype(jnp.bfloat16)
    add_rows(put_ta, 240, [lambda sl: mine[0, x, sl]] + [lambda sl, i=i: rx[i, sl] for i in range(3)])
    ys2 = [mover.push(ta.at[:, strip(lax.rem(y + k, SIDE))], ry2.at[i], spot.along_y(k)) for i, k in enumerate(OFFSETS)]
    for copy in ys:
        copy.wait_recv()
    for m in range(4):
        def put_tb(sl, total, m=m):
            tb[m, sl] = total.astype(jnp.bfloat16)
        add_rows(put_tb, 240, [lambda sl, m=m: mine[1, m, sl, strip(y)]] + [lambda sl, i=i, m=m: ry[i, m, sl] for i in range(3)])
    xs2 = [mover.push(tb.at[lax.rem(x + k, SIDE)], rx2.at[i], spot.along_x(k)) for i, k in enumerate(OFFSETS)]
    for copy in gy:
        copy.wait_recv()
    g_mine[2] = g_mine[1] + g_y[0] + g_y[1] + g_y[2]
    gz = mover.push(g_mine.at[2, 1], g_core.at[2], spot.z)
    for copy in xs2:
        copy.wait_recv()

    def put_ub(sl, total):
        ub[sl] = total.astype(jnp.bfloat16)
    add_rows(put_ub, 240, [lambda sl: tb[x, sl]] + [lambda sl, i=i: rx2[i, sl] for i in range(3)])
    zz = mover.push(ub, rz, spot.z)
    for copy in ys2:
        copy.wait_recv()
    zz.wait_recv()

    def put_ua(sl, total):
        ua[sl] = total.astype(jnp.bfloat16)
    add_rows(put_ua, 240, [lambda sl: ta[sl, strip(y)]] + [lambda sl, i=i: ry2[i, sl] for i in range(3)] + [lambda sl: rz[sl]])
    gz.wait_recv()
    gains_out[...] = g_mine[2, 0] + g_core[2]

    def spread_to(m, j, half):
        lo, size = HALVES[half]
        return out.at[m, pl.ds(lo, size), strip(j)]

    def finished(half):
        lo, size = HALVES[half]
        return ua.at[pl.ds(lo, size)]

    keep = pltpu.make_async_copy(ua, out.at[x, :, strip(y)], local.at[0])
    keep.start()
    stage_one = [(mover.push(finished(0), spread_to(x, y, 0), spot.along_x(k)),
                  mover.push(finished(1), spread_to(x, y, 1), spot.along_y(k))) for k in OFFSETS]
    stage_two = []

    def second(m, j, src_a, src_b):
        for k in OFFSETS:
            stage_two.append(mover.push(src_a, spread_to(m, y, 0), spot.along_y(k)))
            stage_two.append(mover.push(src_b, spread_to(x, j, 1), spot.along_x(k)))

    second(x, y, finished(0), finished(1))
    for k, (copy_a, copy_b) in zip(OFFSETS, stage_one):
        m, j = lax.rem(x + 4 - k, SIDE), lax.rem(y + 4 - k, SIDE)
        copy_a.wait_recv()
        copy_b.wait_recv()
        second(m, j, spread_to(m, y, 0), spread_to(x, j, 1))
    for copy in stage_two:
        copy.wait_recv()
    mover.finish()
    keep.wait()


def reduce_grads(grads, gains):
    n = 96
    bf = jnp.bfloat16
    vm = pltpu.VMEM
    return pl.pallas_call(
        reduce_kernel,
        out_shape=(
            jax.ShapeDtypeStruct((4, 240, 2560), bf),
            jax.ShapeDtypeStruct(gains.shape[1:], jnp.float32),
        ),
        in_specs=[pl.BlockSpec(memory_space=pl.ANY), pl.BlockSpec(memory_space=pltpu.VMEM)],
        out_specs=[pl.BlockSpec(memory_space=pl.ANY), pl.BlockSpec(memory_space=pltpu.VMEM)],
        scratch_shapes=[
            vm((2, 4, 240, 2560), bf), vm((2, 4, 240, 2560), bf),
            vm((3, 240, 2560), bf), vm((3, 4, 240, 640), bf),
            vm((240, 2560), bf), vm((4, 240, 640), bf),
            vm((3, 240, 640), bf), vm((3, 240, 640), bf),
            vm((240, 640), bf), vm((240, 640), bf), vm((240, 640), bf),
            vm((3, 8, 256), jnp.float32), vm((3, 2, 8, 256), jnp.float32),
            vm((3, 2, 8, 256), jnp.float32), vm((3, 2, 8, 256), jnp.float32),
            pltpu.SemaphoreType.DMA((n,)),
            pltpu.SemaphoreType.DMA((n,)),
            pltpu.SemaphoreType.DMA((16,)),
        ],
        compiler_params=pltpu.CompilerParams(collective_id=2, has_side_effects=True, vmem_limit_bytes=60 * 2**20),
        name="reduce_grads",
    )(grads, gains)


def pair_greet(spot):
    barrier = pltpu.get_barrier_semaphore()
    for who in (spot.core, spot.z):
        pl.semaphore_signal(barrier, inc=1, device_id=who, device_id_type=MESH)
    pl.semaphore_wait(barrier, 2)


def kv_rows(stack, f):
    return stack.at[:, pl.ds(pl.multiple_of(f * 256, 256), 256)]


def kv_gather_kernel(own, full, send, recv, local):
    spot = Spot()
    pair_greet(spot)
    mover = Mover(send, recv)
    fz = (1 - spot.zl) * 2 + spot.c
    across = mover.push(own, kv_rows(full, spot.f), spot.z)
    near = mover.push(own, kv_rows(full, spot.f), spot.core)
    keep = pltpu.make_async_copy(own, kv_rows(full, spot.f), local)
    keep.start()
    across.wait_recv()
    far = mover.push(kv_rows(full, fz), kv_rows(full, fz), spot.core)
    near.wait_recv()
    far.wait_recv()
    mover.finish()
    keep.wait()


def gather_keys(own):
    return pl.pallas_call(
        kv_gather_kernel,
        out_shape=jax.ShapeDtypeStruct((KV_HEADS, SEQ, 128), BF),
        in_specs=[pl.BlockSpec(memory_space=pltpu.VMEM)],
        out_specs=pl.BlockSpec(memory_space=pl.ANY),
        scratch_shapes=[pltpu.SemaphoreType.DMA((3,)), pltpu.SemaphoreType.DMA((3,)), pltpu.SemaphoreType.DMA],
        compiler_params=pltpu.CompilerParams(collective_id=3, has_side_effects=True, vmem_limit_bytes=56 * 2**20),
        name="gather_keys",
    )(own)


def kv_reduce_kernel(part, out, near, far, passed, send, recv):
    spot = Spot()
    pair_greet(spot)
    mover = Mover(send, recv)
    other = 1 - spot.zl
    first = mover.push(kv_rows(part, other * 2 + 1 - spot.c), near.at[0], spot.core)
    second = mover.push(kv_rows(part, spot.zl * 2 + 1 - spot.c), near.at[1], spot.core)

    def mine(zl):
        return kv_rows(part, zl * 2 + spot.c)[...].astype(F32)

    first.wait_recv()
    passed[...] = (mine(other) + near[0].astype(F32)).astype(BF)
    third = mover.push(passed, far, spot.z)
    second.wait_recv()
    out[...] = mine(spot.zl) + near[1].astype(F32)
    third.wait_recv()
    out[...] += far[...].astype(F32)
    mover.finish()


def reduce_keys(part):
    own = (KV_HEADS, 256, 128)
    return pl.pallas_call(
        kv_reduce_kernel,
        out_shape=jax.ShapeDtypeStruct(own, F32),
        in_specs=[pl.BlockSpec(memory_space=pltpu.VMEM)],
        out_specs=pl.BlockSpec(memory_space=pltpu.VMEM),
        scratch_shapes=[
            pltpu.VMEM((2,) + own, BF), pltpu.VMEM(own, BF), pltpu.VMEM(own, BF),
            pltpu.SemaphoreType.DMA((3,)), pltpu.SemaphoreType.DMA((3,)),
        ],
        compiler_params=pltpu.CompilerParams(collective_id=4, has_side_effects=True, vmem_limit_bytes=56 * 2**20),
        name="reduce_keys",
    )(part)


def from_behind(value, axis, steps):
    count = lax.axis_size(axis)
    leading, last = (max(0, -steps), min(count, count - steps))
    return lax.ppermute(value, axis, [(source, source + steps) for source in range(leading, last)])


def rope_tables(places):
    half_dim = HEAD_DIM // 2
    frequencies = rope_base ** (-(jnp.arange(half_dim, dtype=F32) * 2.0) / HEAD_DIM)
    angles = places.astype(F32)[:, None] * frequencies[None, :]
    cosine, sines = jnp.cos(angles), jnp.sin(angles)
    return jnp.tile(cosine, (1, 4)), jnp.tile(jnp.concatenate([-sines, sines], axis=1), (1, 2))


def shards(
    block_input, cotangent, lengths, w_query, w_key, w_value, w_out, w_gate, w_up, w_down, gain_attn, gain_mlp
):
    section = lax.axis_index("section")
    place = lax.axis_index("fsdp")
    is_first = section == 0
    places = place * ROWS + jnp.arange(ROWS, dtype=jnp.int32)
    cosine, signed = rope_tables(places)
    own_lengths = lengths[0]
    attn = jnp.concatenate([w_key[0], w_value[0], w_query[0], w_out[0]], axis=1)
    down = w_down[0].T.reshape(4, 240, STRIP).transpose(1, 0, 2).reshape(240, 2560)
    own = jnp.stack([attn, w_gate[0], w_up[0], down])
    gains = jnp.pad(jnp.concatenate([gain_attn, gain_mlp]), ((0, 14), (0, 16)))
    full, gains_full = gather_weights(own, gains)
    gain_one = gains_full[:, 0, :240].reshape(1, D).astype(F32)
    gain_two = gains_full[:, 1, :240].reshape(1, D).astype(F32)

    def scalars(slot):
        return jnp.stack([place.astype(jnp.int32), jnp.where(slot == 0, own_lengths[0], own_lengths[1])])

    received = jnp.zeros((ROWS, D), BF)
    kept, outs = [], []
    for step in range(3):
        hid = jnp.where(is_first, block_input[min(step, 1)], received)
        scal = scalars(jnp.clip(step - section, 0, 1))
        n1, q, kv = front(hid, gain_one, full, cosine, signed)
        kv_all = gather_keys(kv)
        att, lse = attend(scal, q, kv_all)
        out, mid, n2, gate, up, mixed, compact = rest(att, hid, gain_two, full)
        if step < 2:
            received = from_behind(out, "section", 1)
        outs.append(out)
        kept.append((hid, scal, n1, q, kv_all, lse, mid, n2, gate, up, mixed, compact))
    layer_out = jnp.where(is_first, jnp.stack(outs[:2]), jnp.stack(outs[1:]))[None]

    back_received = jnp.zeros((ROWS, D), BF)
    grads, parts, terms = [], [], []
    for step in range(3):
        hid, scal, n1, q, kv_all, lse, mid, n2, gate, up, mixed, compact = kept[2 - step]
        if step < 2:
            live = places < scal[1]
            cot = jnp.where(live[:, None], cotangent[1 - step], 0.0).astype(BF)
            if step == 0:
                g_out = jnp.where(is_first, 0.0, cot).astype(BF)
            else:
                g_out = jnp.where(is_first, back_received, cot)
        else:
            g_out = jnp.where(is_first, back_received, 0.0).astype(BF)
        gg, gu, gm, gao, part_two, da = back_rest(g_out, mid, gain_two, gate, up, full)
        dq, dkv = back_attend(scal, q, kv_all, lse, da, cosine, signed)
        dkv_own = reduce_keys(dkv)
        grad_in, packed, part_one = back_front(dq, dkv_own, hid, gain_one, full, cosine, signed, gm)
        if step < 2:
            back_received = from_behind(grad_in.astype(BF), "section", -1)
        grads.append(grad_in)
        parts.append((part_one, part_two))
        terms.append((n1, compact, n2, g_out, packed, gao, gg, gu, mixed))
    input_grad = jnp.where(is_first, jnp.stack([grads[2], grads[1]]), jnp.stack([grads[1], grads[0]]))[None]

    stacked = weight_grads(section.astype(jnp.int32)[None], list(zip(*terms)))
    sums = [parts[0][i] + parts[1][i] + parts[2][i] for i in range(2)]
    gain_parts = jnp.concatenate([v.reshape(4, 1, 240) for v in sums], axis=1)
    summed, gain_sums = reduce_grads(stacked, jnp.pad(gain_parts, ((0, 0), (0, 6), (0, 16))))
    wide = summed.astype(F32)
    down_grad = wide[3].reshape(240, 4, STRIP).transpose(1, 0, 2).reshape(D, STRIP).T
    return (
        layer_out,
        input_grad,
        wide[0, :, 640:1600][None],
        wide[0, :, :320][None],
        wide[0, :, 320:640][None],
        wide[0, :, 1600:][None],
        wide[1][None],
        wide[2][None],
        down_grad[None],
        gain_sums[0:1, :240],
        gain_sums[1:2, :240],
    )


def solution(mesh):
    tokens, two = ("dp", "fsdp"), P("section", "fsdp", None)
    return jax.shard_map(
        shards,
        mesh=mesh,
        in_specs=(P(None, tokens, None), P(None, tokens, None), P("dp", None)) + (two,) * 7 + (P("section", "fsdp"),) * 2,
        out_specs=(P("section", None, tokens, None),) * 2 + (two,) * 7 + (P("section", "fsdp"),) * 2,
        check_vma=False,
    )
```

```python
import functools

import jax
import jax.numpy as jnp
from jax import lax
from jax.experimental import pallas as pl
from jax.experimental.pallas import tpu as pltpu
from jax.sharding import PartitionSpec as P

HEADS = 15
KV_HEADS = 5
GROUP = 3
HEAD_DIM = 64
D = 960
ROWS = 256
STRIP = 640
SEQ = 1024
norm_eps = 1e-05
rope_base = 10000.0
masked_score = -1e30
BF = jnp.bfloat16
F32 = jnp.float32


def dot(a, b):
    return jnp.dot(a, b, preferred_element_type=F32)


def dot_nt(a, b):
    return lax.dot_general(a, b, (((1,), (1,)), ((), ())), preferred_element_type=F32)


def lanes(rows=ROWS):
    return lax.broadcasted_iota(jnp.int32, (rows, 128), 1)


def turn(tile, cosine, signed, low_half):
    partner = jnp.where(low_half, pltpu.roll(tile, 96, 1), pltpu.roll(tile, 32, 1))
    return tile * cosine + partner * signed


def whole(shape):
    return pl.BlockSpec(shape, lambda *_: (0,) * len(shape))


def params(limit=56):
    return pltpu.CompilerParams(vmem_limit_bytes=limit * 2**20)


def linked(collective_id, limit=56):
    return pltpu.CompilerParams(collective_id=collective_id, has_side_effects=True, vmem_limit_bytes=limit * 2**20)


VM = pl.BlockSpec(memory_space=pltpu.VMEM)
HBM = pl.BlockSpec(memory_space=pl.ANY)
SM = pl.BlockSpec(memory_space=pltpu.SMEM)


def shape(dims, kind):
    return jax.ShapeDtypeStruct(dims, kind)


def gain_row(gains, i):
    return jnp.concatenate([gains[f].astype(F32)[i : i + 1, :240] for f in range(4)], axis=1)


class Streams:
    def __init__(self, sems):
        self.sems, self.count, self.open = sems, 0, []

    def start(self, src, dst):
        copy = pltpu.make_async_copy(src, dst, self.sems.at[self.count])
        self.count += 1
        copy.start()
        return copy

    def emit(self, src, dst):
        self.open.append(self.start(src, dst))

    def finish(self):
        for copy in self.open:
            copy.wait()


def pack_body(k_t, v_t, wq, wo, gate, up, down_t, own):
    keys = jnp.concatenate([k_t[...].astype(F32), v_t[...].astype(F32)], axis=0).T
    own[0, :, :STRIP] = keys.astype(BF)
    own[0, :, STRIP:] = jnp.concatenate([wq[...].astype(F32), wo[...].astype(F32)], axis=1).astype(BF)
    own[1] = gate[...]
    own[2] = up[...]
    for j in range(4):
        own[3, :, STRIP * j : STRIP * j + STRIP] = down_t[240 * j : 240 * j + 240]


def pack(*weights):
    return pl.pallas_call(
        pack_body,
        out_shape=shape((4, 240, 2560), BF),
        in_specs=[VM] * 7,
        out_specs=VM,
        compiler_params=params(),
        name="pack",
    )(*weights)


def unpack_body(summed, q, k_t, v_t, out, gate, up, down_t):
    attn = summed[0].astype(F32)
    keys = attn[:, :STRIP].T
    k_t[...] = keys[:320]
    v_t[...] = keys[320:]
    q[...] = attn[:, STRIP:1600]
    out[...] = attn[:, 1600:]
    gate[...] = summed[1].astype(F32)
    up[...] = summed[2].astype(F32)
    for j in range(4):
        down_t[240 * j : 240 * j + 240] = summed[3, :, STRIP * j : STRIP * j + STRIP].astype(F32)


def unpack(summed):
    return pl.pallas_call(
        unpack_body,
        out_shape=tuple(
            shape(s, F32) for s in ((240, D), (320, 240), (320, 240), (240, D), (240, 2560), (240, 2560), (D, STRIP))
        ),
        in_specs=[VM],
        out_specs=[VM] * 7,
        compiler_params=params(),
        name="unpack",
    )(summed)


def key_bias(lens, slot, f):
    key = lax.broadcasted_iota(jnp.int32, (SEQ, ROWS), 0)
    place = lax.broadcasted_iota(jnp.int32, (SEQ, ROWS), 1) + f * ROWS
    return jnp.where((key <= place) & (key < lens[0, slot]), 0.0, masked_score)


def front_attend_body(step, lens, own_t, passed_on, gains, w, cosine, signed, hid, n1, q, kv_all, att, lse, bias, send, recv):
    spot = Spot()
    pair_greet(spot, None)
    section = lax.axis_index("section")
    f = spot.f
    slot = step // 2 if step != 1 else 1 - section

    @pl.when(section == 0)
    def _():
        hid[...] = own_t[...].astype(F32).T.astype(BF)

    @pl.when(section == 1)
    def _():
        hid[...] = passed_on[...]

    h = hid[...].astype(F32)
    inverse = lax.rsqrt(jnp.mean(h * h, axis=-1, keepdims=True) + norm_eps)
    n = (h * inverse * gain_row(gains, 0)).astype(BF)
    n1[...] = n
    lane = lanes()
    low = lane < 64
    half = lax.rem(lane, 64) < 32
    cos, sin = cosine[...], signed[...]
    proj = dot(n, w[0, :, :STRIP])
    tile = [proj[:, 128 * i : 128 * i + 128] for i in range(5)]
    turned = [turn(tile[i], cos, sin, half) for i in range(3)]
    mine = pl.ds(pl.multiple_of(f * ROWS, ROWS), ROWS)
    other = pl.ds(pl.multiple_of(((1 - spot.zl) * 2 + spot.c) * ROWS, ROWS), ROWS)
    mover = Mover(send, recv)
    across, near, far = [], [], []
    for g in range(KV_HEADS):
        k_tile, v_tile = turned[g // 2], tile[(5 + g) // 2]
        if g % 2 == 0:
            both = jnp.where(low, k_tile, v_tile)
        else:
            both = pltpu.roll(jnp.where(low, v_tile, k_tile), 64, 1)
        kv_all[g, mine] = both.astype(BF)
        block = kv_all.at[g, mine]
        across.append(mover.push(block, block, spot.z))
        near.append(mover.push(block, block, spot.core))
    proj = dot(n, w[0, :, STRIP:])
    for i in range(8):
        t = turn(proj[:, 128 * i : 128 * i + 128], cos, sin, half) * (HEAD_DIM**-0.5)
        for h in (2 * i, 2 * i + 1):
            if h < HEADS:
                part = pltpu.roll(t, 64, 1) if h % 2 else t
                q[h // GROUP, h % GROUP * ROWS : (h % GROUP + 1) * ROWS] = jnp.where(low, part, 0.0).astype(BF)
    bias[...] = key_bias(lens, slot, f)

    def onward(g):
        across[g].wait_recv()
        block = kv_all.at[g, other]
        far.append(mover.push(block, block, spot.core))

    onward(0)
    for g in range(KV_HEADS):
        if g + 1 < KV_HEADS:
            onward(g + 1)
        near[g].wait_recv()
        far[g].wait_recv()
        keys = kv_all[g]
        keys_t = keys.astype(F32).T.astype(BF)
        for r in range(GROUP):
            rows = slice(r * ROWS, (r + 1) * ROWS)
            s = dot_nt(keys, q[g, rows]) + bias[...]
            top = jnp.max(s, axis=0, keepdims=True)
            e = jnp.exp(s - top)
            total = jnp.sum(e, axis=0, keepdims=True)
            o = dot(keys_t, e.astype(BF)) / total
            att[g, rows] = o.T.astype(BF)
            lse[g, r : r + 1] = top + jnp.log(total)
    mover.finish()


def front_attend(step, lens, own_t, passed_on, gains, full, cosine, signed):
    heads = (KV_HEADS, GROUP * ROWS, 128)
    return pl.pallas_call(
        functools.partial(front_attend_body, step),
        grid=(1,),
        out_shape=(
            shape((ROWS, D), BF), shape((ROWS, D), BF), shape(heads, BF), shape((KV_HEADS, SEQ, 128), BF),
            shape(heads, BF), shape((KV_HEADS, 8, ROWS), F32),
        ),
        in_specs=[SM, VM, VM, VM, whole((1, D, 1664)), VM, VM],
        out_specs=[VM] * 6,
        scratch_shapes=[
            pltpu.VMEM((SEQ, ROWS), F32), pltpu.SemaphoreType.DMA((15,)), pltpu.SemaphoreType.DMA((15,)),
        ],
        compiler_params=linked(3 + step),
        name="front_attend",
    )(lens, own_t, passed_on, gains, full, cosine, signed)


def rest_body(relay, att, hid, gains, full, out_t, middle, n2, gate, up, mixed, compact, passed_on,
              wo, wg, wu, wd, mid_s, n2_s, gate_s, up_s, mixed_s, compact_s, out_s, sems, send, recv, ready):
    streams = Streams(sems)
    load_o = streams.start(full.at[0, :, pl.ds(1536, 1024)], wo)
    load_g = streams.start(full.at[1], wg)
    load_u = streams.start(full.at[2], wu)
    load_d = streams.start(full.at[3], wd)
    section = lax.axis_index("section")
    if relay:
        relay_greet(section, 0, ready)
    low = lanes() < 64

    def head(h):
        return att[h // GROUP, h % GROUP * ROWS : (h % GROUP + 1) * ROWS].astype(F32)

    for h in range(0, HEADS - 1, 2):
        pair = jnp.where(low, pltpu.roll(head(h), 64, 1), head(h + 1))
        compact_s[:, 64 * h : 64 * h + 128] = pair.astype(BF)
    compact_s[:, 896:960] = pltpu.roll(head(HEADS - 1), 64, 1)[:, :64].astype(BF)
    streams.emit(compact_s, compact)
    load_o.wait()
    mid = hid[...].astype(F32) + dot(compact_s[...], wo[...])[:, 64:]
    mid_s[...] = mid
    streams.emit(mid_s, middle)
    inverse = lax.rsqrt(jnp.mean(mid * mid, axis=-1, keepdims=True) + norm_eps)
    n2_s[...] = (mid * inverse * gain_row(gains, 1)).astype(BF)
    streams.emit(n2_s, n2)
    load_g.wait()
    load_u.wait()
    for i in range(2):
        cols = slice(1280 * i, 1280 * i + 1280)
        n = n2_s[...]
        g = dot(n, wg[:, cols])
        u = dot(n, wu[:, cols])
        gate_s[:, cols] = g.astype(BF)
        up_s[:, cols] = u.astype(BF)
        mixed_s[:, cols] = (g * jax.nn.sigmoid(g) * u).astype(BF)
    streams.emit(gate_s, gate)
    streams.emit(up_s, up)
    streams.emit(mixed_s, mixed)
    load_d.wait()
    y = mid_s[...] + dot_nt(mixed_s[...], wd[...])
    out_s[...] = y.astype(BF)
    if relay:
        relay_send(section, 0, out_s, passed_on, ready, send, recv)
    out_t[...] = y.T.astype(BF)
    if relay:
        relay_wait(section, 0, out_s, passed_on, send, recv)
    streams.finish()


def weight_slots():
    return [pltpu.VMEM((D, 1024), BF)] + [pltpu.VMEM((D, 2560), BF)] * 3


def rest(relay, att, hid, gains, full):
    wide, narrow = (ROWS, 2560), (ROWS, D)
    body = rest_body if relay else rest_alone
    outs = [shape((D, ROWS), BF), shape(narrow, F32), shape(narrow, BF)] + [shape(wide, BF)] * 3 + [shape(narrow, BF)]
    specs = [VM] + [HBM] * 6
    scratch = weight_slots() + [
        pltpu.VMEM(narrow, F32), pltpu.VMEM(narrow, BF), pltpu.VMEM(wide, BF), pltpu.VMEM(wide, BF),
        pltpu.VMEM(wide, BF), pltpu.VMEM(narrow, BF), pltpu.VMEM(narrow, BF), pltpu.SemaphoreType.DMA((10,)),
    ]
    if relay:
        outs.append(shape(narrow, BF))
        specs.append(VM)
        scratch += [pltpu.SemaphoreType.DMA, pltpu.SemaphoreType.DMA, pltpu.SemaphoreType.REGULAR]
    return pl.pallas_call(
        functools.partial(rest_body, True) if relay else rest_alone,
        out_shape=tuple(outs),
        in_specs=[VM, VM, VM, HBM],
        out_specs=specs,
        scratch_shapes=scratch,
        compiler_params=linked(6) if relay else params(),
        name="rest",
    )(att, hid, gains, full)


def rest_alone(*refs):
    ins, outs, scratch = refs[:4], refs[4:11], refs[11:]
    rest_body(False, *ins, *outs, None, *scratch, None, None, None)


def back_rest_body(step, lens, cot_t, passed_on, gains, mid_ref, gate, up, full,
                   gg_out, gu_out, gm_out, gao_out, part, da, g_out,
                   wo, wg, wu, wd, gate_s, up_s, gg_s, gu_s, gm_s, sems):
    streams = Streams(sems)
    load_d = streams.start(full.at[3], wd)
    load_gate = streams.start(gate, gate_s)
    load_up = streams.start(up, up_s)
    load_g = streams.start(full.at[1], wg)
    load_u = streams.start(full.at[2], wu)
    load_o = streams.start(full.at[0, :, pl.ds(1536, 1024)], wo)
    section = lax.axis_index("section")
    f = lax.axis_index("fsdp")

    @pl.when(section == 1)
    def _():
        if step < 2:
            place = lax.broadcasted_iota(jnp.int32, (D, ROWS), 1) + f * ROWS
            cot = jnp.where(place < lens[0, 1 - step], cot_t[...].astype(F32), 0.0)
            g_out[...] = cot.T.astype(BF)
        else:
            g_out[...] = jnp.zeros((ROWS, D), BF)

    @pl.when(section == 0)
    def _():
        if step > 0:
            g_out[...] = passed_on[...]
        else:
            g_out[...] = jnp.zeros((ROWS, D), BF)

    load_d.wait()
    load_gate.wait()
    load_up.wait()
    for i in range(2):
        cols = slice(1280 * i, 1280 * i + 1280)
        grad_mixed = dot(g_out[...], wd[:, cols])
        ga = gate_s[:, cols].astype(F32)
        sg = jax.nn.sigmoid(ga)
        scaled = grad_mixed * sg
        gg_s[:, cols] = (scaled * up_s[:, cols].astype(F32) * (1.0 + ga * (1.0 - sg))).astype(BF)
        gu_s[:, cols] = (scaled * ga).astype(BF)
    streams.emit(gg_s, gg_out)
    streams.emit(gu_s, gu_out)
    load_g.wait()
    load_u.wait()
    grad_normed = dot_nt(gg_s[...], wg[...]) + dot_nt(gu_s[...], wu[...])
    mid = mid_ref[...]
    inverse = lax.rsqrt(jnp.mean(mid * mid, axis=-1, keepdims=True) + norm_eps)
    unit = mid * inverse
    part[...] = jnp.sum(grad_normed * unit, axis=0, keepdims=True)
    scaled_two = grad_normed * gain_row(gains, 1)
    gm = g_out[...].astype(F32) + inverse * (
        scaled_two - unit * jnp.mean(scaled_two * unit, axis=-1, keepdims=True)
    )
    gm_s[...] = gm
    streams.emit(gm_s, gm_out)
    gao_out[...] = gm.astype(BF)
    shifted = jnp.concatenate([jnp.zeros((ROWS, 64), F32), gm], axis=1).astype(BF)
    load_o.wait()
    att = jnp.concatenate([dot_nt(shifted, wo[...]), jnp.zeros((ROWS, 64), F32)], axis=1)
    low = lanes() < 64
    for h in range(HEADS):
        tile = att[:, 128 * (h // 2) : 128 * (h // 2) + 128]
        if h % 2 == 0:
            tile = pltpu.roll(tile, 64, 1)
        da[h // GROUP, h % GROUP * ROWS : (h % GROUP + 1) * ROWS] = jnp.where(low, 0.0, tile).astype(BF)
    streams.finish()


def back_rest(step, lens, cot_t, passed_on, gains, mid, gate, up, full):
    wide, narrow = (ROWS, 2560), (ROWS, D)
    return pl.pallas_call(
        functools.partial(back_rest_body, step),
        out_shape=(
            shape(wide, BF), shape(wide, BF), shape(narrow, F32), shape(narrow, BF), shape((1, D), F32),
            shape((KV_HEADS, GROUP * ROWS, 128), BF), shape(narrow, BF),
        ),
        in_specs=[SM, VM, VM, VM, VM, HBM, HBM, HBM],
        out_specs=[HBM, HBM, HBM, VM, VM, VM, VM],
        scratch_shapes=weight_slots() + [pltpu.VMEM(wide, BF)] * 4 + [pltpu.VMEM(narrow, F32), pltpu.SemaphoreType.DMA((9,))],
        compiler_params=params(),
        name="back_rest",
    )(lens, cot_t, passed_on, gains, mid, gate, up, full)


def back_attend_body(step, relay, lens, q, kv, lse, da, cosine, signed, hid, gains, w, gm,
                     grad_t, packed, gain_part, passed_on,
                     bias, part, near, passed, far, own, dq, out_s, send, recv, ready):
    spot = Spot()
    section = lax.axis_index("section")
    pair_greet(spot, (section, 1, ready) if relay else None)
    slot = 1 - section if step == 1 else 1 - step // 2
    bias[...] = key_bias(lens, slot, spot.f)
    mover = Mover(send, recv)
    lane = lanes()
    low = lane < 64
    half = lax.rem(lane, 64) < 32
    cos, sin = cosine[...], -signed[...]

    def rows_of(zl, c):
        return pl.ds(pl.multiple_of((zl * 2 + c) * ROWS, ROWS), ROWS)

    there, here = 1 - spot.zl, spot.zl
    core, across = {}, {}

    def stage_one(g):
        core[g][0].wait_recv()
        passed[g] = (part[g, rows_of(there, spot.c)].astype(F32) + near[g, 0].astype(F32)).astype(BF)
        across[g] = mover.push(passed.at[g], far.at[g], spot.z)
        core[g][1].wait_recv()
        own[g] = part[g, rows_of(here, spot.c)].astype(F32) + near[g, 1].astype(F32)

    def stage_two(g):
        across[g].wait_recv()
        own[g] = own[g] + far[g].astype(F32)

    for g in range(KV_HEADS):
        keys = kv[g]
        keys_t = keys.astype(F32).T.astype(BF)
        total = None
        for r in range(GROUP):
            rows = slice(r * ROWS, (r + 1) * ROWS)
            qr, dr = q[g, rows], da[g, rows]
            p = jnp.exp(dot_nt(keys, qr) + bias[...] - lse[g, r : r + 1])
            dp = dot_nt(keys, dr)
            delta = jnp.sum(p * dp, axis=0, keepdims=True)
            ds = (p * (dp - delta)).astype(BF)
            term = dot(ds, qr) + dot(p.astype(BF), dr)
            total = term if total is None else total + term
            grad_q = (dot(keys_t, ds) * (HEAD_DIM**-0.5)).T
            dq[g, rows] = turn(grad_q, cos, sin, half).astype(BF)
        part[g] = total.astype(BF)
        core[g] = (
            mover.push(part.at[g, rows_of(there, 1 - spot.c)], near.at[g, 0], spot.core),
            mover.push(part.at[g, rows_of(here, 1 - spot.c)], near.at[g, 1], spot.core),
        )
        if g > 0:
            stage_one(g - 1)
        if g > 1:
            stage_two(g - 2)
    stage_one(KV_HEADS - 1)

    def merged(left, right):
        return jnp.where(low, left, right)

    def flip(v):
        return pltpu.roll(v, 64, 1)

    def head(h):
        return dq[h // GROUP, h % GROUP * ROWS : (h % GROUP + 1) * ROWS].astype(F32)

    for h in range(0, HEADS, 2):
        tile = merged(head(h), flip(head(h + 1)) if h + 1 < HEADS else 0.0)
        packed[:, STRIP + 64 * h : STRIP + 64 * h + 128] = tile.astype(BF)
    grad_normed = dot_nt(packed[:, STRIP:], w[0, :, STRIP:])
    hidden = hid[...].astype(F32)
    inverse = lax.rsqrt(jnp.mean(hidden * hidden, axis=-1, keepdims=True) + norm_eps)
    unit = hidden * inverse
    stage_two(KV_HEADS - 2)
    stage_two(KV_HEADS - 1)
    both = [own[g] for g in range(KV_HEADS)]
    turned = [turn(b, cos, sin, half) for b in both]
    tiles = [
        merged(turned[0], flip(turned[1])),
        merged(turned[2], flip(turned[3])),
        merged(turned[4], both[0]),
        merged(flip(both[1]), both[2]),
        merged(flip(both[3]), both[4]),
    ]
    for i, tile in enumerate(tiles):
        packed[:, 128 * i : 128 * i + 128] = tile.astype(BF)
    grad_normed = grad_normed + dot_nt(packed[:, :STRIP], w[0, :, :STRIP])
    gain_part[...] = jnp.sum(grad_normed * unit, axis=0, keepdims=True)
    scaled = grad_normed * gain_row(gains, 0)
    grad_in = gm[...] + inverse * (scaled - unit * jnp.mean(scaled * unit, axis=-1, keepdims=True))
    if relay:
        out_s[...] = grad_in.astype(BF)
        relay_send(section, 1, out_s, passed_on, ready, send.at[20], recv.at[20])
    grad_t[...] = grad_in.T
    mover.finish()
    if relay:
        relay_wait(section, 1, out_s, passed_on, send.at[20], recv.at[20])


def back_alone(step, *refs):
    back_attend_body(step, False, *refs[:14], None, *refs[14:21], None, *refs[21:], None)


def back_attend(step, lens, q, kv, lse, da, cosine, signed, hid, gains, full, gm):
    relay = step < 2
    narrow, own = (ROWS, D), (KV_HEADS, ROWS, 128)
    outs = [shape((D, ROWS), F32), shape((ROWS, 1664), BF), shape((1, D), F32)]
    scratch = [
        pltpu.VMEM((SEQ, ROWS), F32), pltpu.VMEM((KV_HEADS, SEQ, 128), BF), pltpu.VMEM((KV_HEADS, 2, ROWS, 128), BF),
        pltpu.VMEM(own, BF), pltpu.VMEM(own, BF), pltpu.VMEM(own, F32), pltpu.VMEM((KV_HEADS, GROUP * ROWS, 128), BF),
    ]
    if relay:
        outs.append(shape(narrow, BF))
        scratch.append(pltpu.VMEM(narrow, BF))
    scratch += [pltpu.SemaphoreType.DMA((21,)), pltpu.SemaphoreType.DMA((21,))]
    if relay:
        scratch.append(pltpu.SemaphoreType.REGULAR)
    return pl.pallas_call(
        functools.partial(back_attend_body, step, True) if relay else functools.partial(back_alone, step),
        grid=(1,),
        out_shape=tuple(outs),
        in_specs=[SM] + [VM] * 8 + [whole((1, D, 1664)), VM],
        out_specs=[VM] * len(outs),
        scratch_shapes=scratch,
        compiler_params=linked(7 + step),
        name="back_attend",
    )(lens, q, kv, lse, da, cosine, signed, hid, gains, full, gm)


def weight_body(scal, *refs):
    sets = [refs[3 * i : 3 * i + 3] for i in range(9)]
    n1, att, n2, gd, packed, gao, gg, gu, mixed = sets
    out, lhs, lhs_b = refs[27:]
    m, t = pl.program_id(0), pl.program_id(1)

    def each(fn):
        pl.when(scal[0] == 1)(lambda: fn(0))
        pl.when(scal[0] == 0)(lambda: fn(2))

    def flip_into(dst, trio):
        dst[:, ROWS:] = trio[1][...].astype(F32).T.astype(BF)

        def put(i):
            dst[:, :ROWS] = trio[i][...].astype(F32).T.astype(BF)

        each(put)

    for i, trio in enumerate((n1, n2, n2, gd)):
        if i == 2:
            continue

        @pl.when((m == i) & (t == 0))
        def _(i=i, trio=trio):
            flip_into(lhs, trio)
            if i == 0:
                flip_into(lhs_b, att)

    def product(left, trio, cols, dst):
        first = dot(left[:, ROWS:], trio[1][:, cols])

        def put(i):
            out[0, :, dst] = (first + dot(left[:, :ROWS], trio[i][:, cols])).astype(BF)

        each(put)

    everything = slice(0, 1280)
    @pl.when((m == 0) & (t == 0))
    def _():
        product(lhs, packed, slice(0, 1280), everything)

    @pl.when((m == 0) & (t == 1))
    def _():
        product(lhs, packed, slice(1280, 1600), slice(0, 320))
        product(lhs_b, gao, slice(0, 960), slice(320, 1280))

    for i, trio in ((1, gg), (2, gu), (3, mixed)):
        @pl.when(m == i)
        def _(trio=trio):
            product(lhs, trio, everything, everything)


def weight_grads(scal, sets):
    def strips(i):
        return pl.BlockSpec((ROWS, 1280), lambda m, t, s, i=i: (0, jnp.where(m == i, t, jnp.where(m < i, 0, 1))))

    def fixed(cols):
        return pl.BlockSpec((ROWS, cols), lambda m, t, s: (0, 0))

    specs = [fixed(D)] * 12 + [fixed(1664)] * 3 + [fixed(D)] * 3
    specs += [strips(1)] * 3 + [strips(2)] * 3 + [strips(3)] * 3
    return pl.pallas_call(
        weight_body,
        grid_spec=pltpu.PrefetchScalarGridSpec(
            num_scalar_prefetch=1,
            grid=(4, 2),
            in_specs=specs,
            out_specs=pl.BlockSpec((1, D, 1280), lambda m, t, s: (m, 0, t)),
            scratch_shapes=[pltpu.VMEM((D, 2 * ROWS), BF), pltpu.VMEM((D, 2 * ROWS), BF)],
        ),
        out_shape=jax.ShapeDtypeStruct((4, D, 2560), BF),
        compiler_params=params(),
        name="weight_grads",
    )(scal, *[a for trio in sets for a in trio])


MESH = pl.DeviceIdType.MESH
SIDE = 4
OFFSETS = (1, 3, 2)
HALVES = ((0, 128), (128, 112))


class Spot:
    def __init__(self):
        d = lax.axis_index("dp")
        f = lax.axis_index("fsdp")
        self.x, self.y = d // SIDE, lax.rem(d, SIDE)
        self.zl, self.c = f // 2, lax.rem(f, 2)
        self.f = f
        self.core = {"fsdp": self.zl * 2 + 1 - self.c}
        self.z = {"fsdp": (1 - self.zl) * 2 + self.c}
        self.across = {"fsdp": (1 - self.zl) * 2 + 1 - self.c}

    def along_x(self, k):
        return {"dp": lax.rem(self.x + k, SIDE) * SIDE + self.y}

    def along_y(self, k):
        return {"dp": self.x * SIDE + lax.rem(self.y + k, SIDE)}

    def greet(self):
        barrier = pltpu.get_barrier_semaphore()
        ids = [self.core, self.z, self.across]
        for k in range(1, SIDE):
            ids += [self.along_x(k), self.along_y(k)]
        for who in ids:
            pl.semaphore_signal(barrier, inc=1, device_id=who, device_id_type=MESH)
        pl.semaphore_wait(barrier, len(ids))


class Mover:
    def __init__(self, send, recv):
        self.send, self.recv, self.pending = send, recv, []

    def push(self, src, dst, who):
        i = len(self.pending)
        copy = pltpu.make_async_remote_copy(
            src_ref=src, dst_ref=dst, send_sem=self.send.at[i], recv_sem=self.recv.at[i],
            device_id=who, device_id_type=MESH,
        )
        copy.start()
        self.pending.append(copy)
        return copy

    def finish(self):
        for copy in self.pending:
            copy.wait_send()


def region(stack, f, m, j, lo=0, size=240):
    tall = m // 3
    row = f + tall * (j - f)
    col = j + tall * (f - j)
    return stack.at[m, pl.ds(pl.multiple_of(row * 240 + lo, 16), size), pl.ds(pl.multiple_of(col * 640, 128), 640)]


def shard_parts(stack, packed, f):
    rows = pl.ds(pl.multiple_of(f * 240, 16), 240)
    parts = [(stack.at[m, rows], packed.at[m]) for m in range(3)]
    cols = pl.ds(pl.multiple_of(f * 640, 128), 640)
    for j in range(4):
        parts.append((stack.at[3, pl.ds(j * 240, 240), cols], packed.at[3, :, pl.ds(j * 640, 640)]))
    return parts


def gather_kernel(own, gains, full, gains_full, held, send, recv, local):
    spot = Spot()
    x, y, f = spot.x, spot.y, spot.f
    fz = (1 - spot.zl) * 2 + spot.c
    spot.greet()
    mover = Mover(send, recv)
    first = mover.push(own.at[x, :, pl.ds(pl.multiple_of(y * 640, 128), 640)], region(full, f, x, y), spot.z)
    waits = []
    for k in range(1, 4):
        who = {"fsdp": lax.rem(f + k, 4)}
        waits.append(mover.push(gains, gains_full.at[f], who))
    load = pltpu.make_async_copy(own, held, local.at[8])
    load.start()
    for there, here in shard_parts(full, own, f):
        waits.append(mover.push(here, there, spot.core))
    load.wait()
    locals_ = [pltpu.make_async_copy(gains, gains_full.at[f], local.at[0])]
    for i, (there, here) in enumerate(shard_parts(full, held, f)):
        locals_.append(pltpu.make_async_copy(here, there, local.at[1 + i]))
    for copy in locals_:
        copy.start()
    first.wait_recv()

    def onward(view):
        waits.append(mover.push(view, view, spot.core))

    stage_one = []
    for k in OFFSETS:
        a = region(full, fz, x, y, *HALVES[0])
        b = region(full, fz, x, y, *HALVES[1])
        stage_one.append((mover.push(a, a, spot.along_x(k)), mover.push(b, b, spot.along_y(k))))
    stage_two = []

    def second(m, j):
        a = region(full, fz, m, y, *HALVES[0])
        b = region(full, fz, x, j, *HALVES[1])
        for k in OFFSETS:
            stage_two.append((k, m, j, mover.push(a, a, spot.along_y(k)), mover.push(b, b, spot.along_x(k))))

    second(x, y)
    onward(region(full, fz, x, y))
    for k, (copy_a, copy_b) in zip(OFFSETS, stage_one):
        m, j = lax.rem(x + 4 - k, SIDE), lax.rem(y + 4 - k, SIDE)
        copy_a.wait_recv()
        copy_b.wait_recv()
        second(m, j)
        onward(region(full, fz, m, y, *HALVES[0]))
        onward(region(full, fz, x, j, *HALVES[1]))
    for k, m, j, copy_a, copy_b in stage_two:
        copy_a.wait_recv()
        onward(region(full, fz, m, lax.rem(y + 4 - k, SIDE), *HALVES[0]))
        copy_b.wait_recv()
        onward(region(full, fz, lax.rem(x + 4 - k, SIDE), j, *HALVES[1]))
    for copy in waits:
        copy.wait_recv()
    mover.finish()
    for copy in locals_:
        copy.wait()


def gather_weights(own, gains):
    n = 96
    return pl.pallas_call(
        gather_kernel,
        out_shape=(
            jax.ShapeDtypeStruct((4, 960, 2560), own.dtype),
            jax.ShapeDtypeStruct((4,) + gains.shape, gains.dtype),
        ),
        in_specs=[pl.BlockSpec(memory_space=pl.ANY), pl.BlockSpec(memory_space=pltpu.VMEM)],
        out_specs=[pl.BlockSpec(memory_space=pl.ANY), pl.BlockSpec(memory_space=pltpu.VMEM)],
        scratch_shapes=[
            pltpu.VMEM((4, 240, 2560), own.dtype),
            pltpu.SemaphoreType.DMA((n,)),
            pltpu.SemaphoreType.DMA((n,)),
            pltpu.SemaphoreType.DMA((9,)),
        ],
        compiler_params=pltpu.CompilerParams(collective_id=1, has_side_effects=True, vmem_limit_bytes=60 * 2**20),
        name="gather_weights",
    )(own, gains)


STEP = 16


def add_rows(out, rows, terms):
    def body(i, carry):
        sl = pl.ds(pl.multiple_of(i * STEP, STEP), STEP)
        total = terms[0](sl).astype(jnp.float32)
        for term in terms[1:]:
            total = total + term(sl).astype(jnp.float32)
        out(sl, total)
        return carry

    lax.fori_loop(0, rows // STEP, body, 0)


def reduce_kernel(grads, gains, out, gains_out, mine, theirs, rx, ry, ta, tb, rx2, ry2, ua, ub, rz,
                  g_core, g_mine, g_x, g_y, send, recv, local):
    spot = Spot()
    x, y, f = spot.x, spot.y, spot.f
    spot.greet()
    mover = Mover(send, recv)
    shards = (spot.zl, 1 - spot.zl)
    loads, core = [], []
    small = []
    for s, zl in enumerate(shards):
        keep, give = zl * 2 + spot.c, zl * 2 + 1 - spot.c
        core.append([mover.push(there, here, spot.core)
                     for there, here in shard_parts(grads, theirs.at[s], give)])
        part = []
        for i, (there, here) in enumerate(shard_parts(grads, mine.at[s], keep)):
            copy = pltpu.make_async_copy(there, here, local.at[s * 8 + i])
            copy.start()
            part.append(copy)
        loads.append(part)
        small.append(mover.push(gains.at[give], g_core.at[s], spot.core))
    for s, zl in enumerate(shards):
        small[s].wait_recv()
        g_mine[0, s] = gains[zl * 2 + spot.c] + g_core[s]
    gx = [mover.push(g_mine.at[0], g_x.at[i], spot.along_x(k)) for i, k in enumerate(OFFSETS)]

    def core_sum(s):
        for copy in loads[s]:
            copy.wait()
        for copy in core[s]:
            copy.wait_recv()
        for m in range(4):
            def put(sl, total, m=m):
                mine[s, m, sl] = total.astype(jnp.bfloat16)
            add_rows(put, 240, [lambda sl, m=m: mine[s, m, sl], lambda sl, m=m: theirs[s, m, sl]])

    core_sum(0)
    xs = [mover.push(mine.at[0, lax.rem(x + k, SIDE)], rx.at[i], spot.along_x(k)) for i, k in enumerate(OFFSETS)]
    core_sum(1)

    def strip(j):
        return pl.ds(pl.multiple_of(j * 640, 128), 640)

    ys = [mover.push(mine.at[1, :, :, strip(lax.rem(y + k, SIDE))], ry.at[i], spot.along_y(k))
          for i, k in enumerate(OFFSETS)]
    for copy in gx:
        copy.wait_recv()
    g_mine[1] = g_mine[0] + g_x[0] + g_x[1] + g_x[2]
    gy = [mover.push(g_mine.at[1], g_y.at[i], spot.along_y(k)) for i, k in enumerate(OFFSETS)]
    for copy in xs:
        copy.wait_recv()

    def put_ta(sl, total):
        ta[sl] = total.astype(jnp.bfloat16)
    add_rows(put_ta, 240, [lambda sl: mine[0, x, sl]] + [lambda sl, i=i: rx[i, sl] for i in range(3)])
    ys2 = [mover.push(ta.at[:, strip(lax.rem(y + k, SIDE))], ry2.at[i], spot.along_y(k)) for i, k in enumerate(OFFSETS)]
    for copy in ys:
        copy.wait_recv()
    for m in range(4):
        def put_tb(sl, total, m=m):
            tb[m, sl] = total.astype(jnp.bfloat16)
        add_rows(put_tb, 240, [lambda sl, m=m: mine[1, m, sl, strip(y)]] + [lambda sl, i=i, m=m: ry[i, m, sl] for i in range(3)])
    xs2 = [mover.push(tb.at[lax.rem(x + k, SIDE)], rx2.at[i], spot.along_x(k)) for i, k in enumerate(OFFSETS)]
    for copy in gy:
        copy.wait_recv()
    g_mine[2] = g_mine[1] + g_y[0] + g_y[1] + g_y[2]
    gz = mover.push(g_mine.at[2, 1], g_core.at[2], spot.z)
    for copy in xs2:
        copy.wait_recv()

    def put_ub(sl, total):
        ub[sl] = total.astype(jnp.bfloat16)
    add_rows(put_ub, 240, [lambda sl: tb[x, sl]] + [lambda sl, i=i: rx2[i, sl] for i in range(3)])
    zz = mover.push(ub, rz, spot.z)
    for copy in ys2:
        copy.wait_recv()
    zz.wait_recv()

    def put_ua(sl, total):
        ua[sl] = total.astype(jnp.bfloat16)
    add_rows(put_ua, 240, [lambda sl: ta[sl, strip(y)]] + [lambda sl, i=i: ry2[i, sl] for i in range(3)] + [lambda sl: rz[sl]])
    gz.wait_recv()
    gains_out[...] = g_mine[2, 0] + g_core[2]

    def spread_to(m, j, half):
        lo, size = HALVES[half]
        return out.at[m, pl.ds(lo, size), strip(j)]

    def finished(half):
        lo, size = HALVES[half]
        return ua.at[pl.ds(lo, size)]

    keep = pltpu.make_async_copy(ua, out.at[x, :, strip(y)], local.at[0])
    keep.start()
    stage_one = [(mover.push(finished(0), spread_to(x, y, 0), spot.along_x(k)),
                  mover.push(finished(1), spread_to(x, y, 1), spot.along_y(k))) for k in OFFSETS]
    stage_two = []

    def second(m, j, src_a, src_b):
        for k in OFFSETS:
            stage_two.append(mover.push(src_a, spread_to(m, y, 0), spot.along_y(k)))
            stage_two.append(mover.push(src_b, spread_to(x, j, 1), spot.along_x(k)))

    second(x, y, finished(0), finished(1))
    for k, (copy_a, copy_b) in zip(OFFSETS, stage_one):
        m, j = lax.rem(x + 4 - k, SIDE), lax.rem(y + 4 - k, SIDE)
        copy_a.wait_recv()
        copy_b.wait_recv()
        second(m, j, spread_to(m, y, 0), spread_to(x, j, 1))
    for copy in stage_two:
        copy.wait_recv()
    mover.finish()
    keep.wait()


def reduce_grads(grads, gains):
    n = 96
    bf = jnp.bfloat16
    vm = pltpu.VMEM
    return pl.pallas_call(
        reduce_kernel,
        out_shape=(
            jax.ShapeDtypeStruct((4, 240, 2560), bf),
            jax.ShapeDtypeStruct(gains.shape[1:], jnp.float32),
        ),
        in_specs=[pl.BlockSpec(memory_space=pl.ANY), pl.BlockSpec(memory_space=pltpu.VMEM)],
        out_specs=[pl.BlockSpec(memory_space=pl.ANY), pl.BlockSpec(memory_space=pltpu.VMEM)],
        scratch_shapes=[
            vm((2, 4, 240, 2560), bf), vm((2, 4, 240, 2560), bf),
            vm((3, 240, 2560), bf), vm((3, 4, 240, 640), bf),
            vm((240, 2560), bf), vm((4, 240, 640), bf),
            vm((3, 240, 640), bf), vm((3, 240, 640), bf),
            vm((240, 640), bf), vm((240, 640), bf), vm((240, 640), bf),
            vm((3, 8, 256), jnp.float32), vm((3, 2, 8, 256), jnp.float32),
            vm((3, 2, 8, 256), jnp.float32), vm((3, 2, 8, 256), jnp.float32),
            pltpu.SemaphoreType.DMA((n,)),
            pltpu.SemaphoreType.DMA((n,)),
            pltpu.SemaphoreType.DMA((16,)),
        ],
        compiler_params=pltpu.CompilerParams(collective_id=2, has_side_effects=True, vmem_limit_bytes=60 * 2**20),
        name="reduce_grads",
    )(grads, gains)


def pair_greet(spot, relay):
    barrier = pltpu.get_barrier_semaphore()
    for who in (spot.core, spot.z):
        pl.semaphore_signal(barrier, inc=1, device_id=who, device_id_type=MESH)
    if relay is None:
        pl.semaphore_wait(barrier, 2)
        return
    section, sender, ready = relay
    beyond = {"section": 1 - section}

    @pl.when(section == sender)
    def _():
        pl.semaphore_signal(barrier, inc=1, device_id=beyond, device_id_type=MESH)
        pl.semaphore_wait(barrier, 2)

    @pl.when(section != sender)
    def _():
        pl.semaphore_wait(barrier, 3)
        pl.semaphore_signal(ready, inc=1, device_id=beyond, device_id_type=MESH)


def relay_greet(section, sender, ready):
    barrier = pltpu.get_barrier_semaphore()
    beyond = {"section": 1 - section}

    @pl.when(section == sender)
    def _():
        pl.semaphore_signal(barrier, inc=1, device_id=beyond, device_id_type=MESH)

    @pl.when(section != sender)
    def _():
        pl.semaphore_wait(barrier, 1)
        pl.semaphore_signal(ready, inc=1, device_id=beyond, device_id_type=MESH)


def relay_copy(section, src, dst, send, recv):
    return pltpu.make_async_remote_copy(
        src_ref=src, dst_ref=dst, send_sem=send, recv_sem=recv,
        device_id={"section": 1 - section}, device_id_type=MESH,
    )


def relay_send(section, sender, src, dst, ready, send, recv):
    @pl.when(section == sender)
    def _():
        pl.semaphore_wait(ready, 1)
        relay_copy(section, src, dst, send, recv).start()
        dst[...] = jnp.zeros(dst.shape, dst.dtype)


def relay_wait(section, sender, src, dst, send, recv):
    @pl.when(section == sender)
    def _():
        relay_copy(section, src, dst, send, recv).wait_send()

    @pl.when(section != sender)
    def _():
        relay_copy(section, src, dst, send, recv).wait_recv()


def rope_tables(place):
    lane = lax.broadcasted_iota(jnp.int32, (ROWS, 128), 1)
    rows = lax.broadcasted_iota(jnp.int32, (ROWS, 128), 0) + place * ROWS
    frequencies = rope_base ** (-((lane % 32).astype(F32) * 2.0) / HEAD_DIM)
    angles = rows.astype(F32) * frequencies
    return jnp.cos(angles), jnp.sin(angles) * jnp.where(lane % 64 < 32, -1.0, 1.0)


def shards(
    block_input, cotangent, lengths, w_query, w_key, w_value, w_out, w_gate, w_up, w_down, gain_attn, gain_mlp
):
    section = lax.axis_index("section")
    is_first = section == 0
    cosine, signed = rope_tables(lax.axis_index("fsdp"))
    own = pack(w_key[0].T, w_value[0].T, w_query[0], w_out[0], w_gate[0], w_up[0], w_down[0].T)
    gains = jnp.pad(jnp.concatenate([gain_attn, gain_mlp]), ((0, 14), (0, 16)))
    full, gains = gather_weights(own, gains)
    inputs_t = block_input.transpose(0, 2, 1)
    cot_t = cotangent.transpose(0, 2, 1)
    passed_on = jnp.zeros((ROWS, D), BF)
    kept, outs = [], []
    for step in range(3):
        hid, n1, q, kv_all, att, lse = front_attend(
            step, lengths, inputs_t[min(step, 1)], passed_on, gains, full, cosine, signed
        )
        out_t, mid, n2, gate, up, mixed, compact, *more = rest(step < 2, att, hid, gains, full)
        if more:
            passed_on = more[0]
        outs.append(out_t)
        kept.append((hid, n1, q, kv_all, lse, mid, n2, gate, up, mixed, compact))
    layer_out = jnp.where(is_first, jnp.stack(outs[:2]), jnp.stack(outs[1:])).transpose(0, 2, 1)[None]

    passed_on = jnp.zeros((ROWS, D), BF)
    grads, parts, terms = [], [], []
    for step in range(3):
        hid, n1, q, kv_all, lse, mid, n2, gate, up, mixed, compact = kept[2 - step]
        gg, gu, gm, gao, part_two, da, g_out = back_rest(
            step, lengths, cot_t[max(1 - step, 0)], passed_on, gains, mid, gate, up, full
        )
        grad_t, packed, part_one, *more = back_attend(
            step, lengths, q, kv_all, lse, da, cosine, signed, hid, gains, full, gm
        )
        if more:
            passed_on = more[0]
        grads.append(grad_t)
        parts.append((part_one, part_two))
        terms.append((n1, compact, n2, g_out, packed, gao, gg, gu, mixed))
    input_grad = jnp.where(is_first, jnp.stack([grads[2], grads[1]]), jnp.stack([grads[1], grads[0]]))
    input_grad = input_grad.transpose(0, 2, 1)[None]

    stacked = weight_grads(section.astype(jnp.int32)[None], list(zip(*terms)))
    sums = [parts[0][i] + parts[1][i] + parts[2][i] for i in range(2)]
    gain_parts = jnp.concatenate([v.reshape(4, 1, 240) for v in sums], axis=1)
    summed, gain_sums = reduce_grads(stacked, jnp.pad(gain_parts, ((0, 0), (0, 6), (0, 16))))
    query, key_t, value_t, out, gate, up, down_t = unpack(summed)
    return (
        layer_out,
        input_grad,
        query[None],
        key_t.T[None],
        value_t.T[None],
        out[None],
        gate[None],
        up[None],
        down_t.T[None],
        gain_sums[0:1, :240],
        gain_sums[1:2, :240],
    )


def solution(mesh):
    tokens, two = ("dp", "fsdp"), P("section", "fsdp", None)
    return jax.shard_map(
        shards,
        mesh=mesh,
        in_specs=(P(None, tokens, None), P(None, tokens, None), P("dp", None)) + (two,) * 7 + (P("section", "fsdp"),) * 2,
        out_specs=(P("section", None, tokens, None),) * 2 + (two,) * 7 + (P("section", "fsdp"),) * 2,
        check_vma=False,
    )
```

```python
import functools

import jax
import jax.numpy as jnp
from jax import lax
from jax.experimental import pallas as pl
from jax.experimental.pallas import tpu as pltpu
from jax.sharding import PartitionSpec as P

HEADS = 15
KV_HEADS = 5
GROUP = 3
HEAD_DIM = 64
D = 960
ROWS = 256
STRIP = 640
SEQ = 1024
norm_eps = 1e-05
rope_base = 10000.0
masked_score = -1e30
BF = jnp.bfloat16
F32 = jnp.float32


def dot(a, b):
    return jnp.dot(a, b, preferred_element_type=F32)


def dot_nt(a, b):
    return lax.dot_general(a, b, (((1,), (1,)), ((), ())), preferred_element_type=F32)


def lanes(rows=ROWS):
    return lax.broadcasted_iota(jnp.int32, (rows, 128), 1)


def turn(tile, cosine, signed, low_half):
    partner = jnp.where(low_half, pltpu.roll(tile, 96, 1), pltpu.roll(tile, 32, 1))
    return tile * cosine + partner * signed


def whole(shape):
    return pl.BlockSpec(shape, lambda *_: (0,) * len(shape))


def params(limit=56):
    return pltpu.CompilerParams(vmem_limit_bytes=limit * 2**20)


def linked(collective_id, limit=56):
    return pltpu.CompilerParams(collective_id=collective_id, has_side_effects=True, vmem_limit_bytes=limit * 2**20)


VM = pl.BlockSpec(memory_space=pltpu.VMEM)
HBM = pl.BlockSpec(memory_space=pl.ANY)
SM = pl.BlockSpec(memory_space=pltpu.SMEM)


def shape(dims, kind):
    return jax.ShapeDtypeStruct(dims, kind)


def gain_row(gains, i):
    return jnp.concatenate([gains[f].astype(F32)[i : i + 1, :240] for f in range(4)], axis=1)


class Streams:
    def __init__(self, sems):
        self.sems, self.count, self.open = sems, 0, []

    def start(self, src, dst):
        copy = pltpu.make_async_copy(src, dst, self.sems.at[self.count])
        self.count += 1
        copy.start()
        return copy

    def emit(self, src, dst):
        self.open.append(self.start(src, dst))

    def finish(self):
        for copy in self.open:
            copy.wait()


def pack_body(k_t, v_t, wq, wo, gate, up, down_t, own):
    keys = jnp.concatenate([k_t[...].astype(F32), v_t[...].astype(F32)], axis=0).T
    own[0, :, :STRIP] = keys.astype(BF)
    own[0, :, STRIP:] = jnp.concatenate([wq[...].astype(F32), wo[...].astype(F32)], axis=1).astype(BF)
    own[1] = gate[...]
    own[2] = up[...]
    for j in range(4):
        own[3, :, STRIP * j : STRIP * j + STRIP] = down_t[240 * j : 240 * j + 240]


def pack(*weights):
    return pl.pallas_call(
        pack_body,
        out_shape=shape((4, 240, 2560), BF),
        in_specs=[VM] * 7,
        out_specs=VM,
        compiler_params=params(),
        name="pack",
    )(*weights)


def unpack_body(summed, q, k_t, v_t, out, gate, up, down_t):
    attn = summed[0, :240].astype(F32)
    keys = attn[:, :STRIP].T
    k_t[...] = keys[:320]
    v_t[...] = keys[320:]
    q[...] = attn[:, STRIP:1600]
    out[...] = attn[:, 1600:]
    gate[...] = summed[1, :240].astype(F32)
    up[...] = summed[2, :240].astype(F32)
    for j in range(4):
        down_t[240 * j : 240 * j + 240] = summed[3, :240, STRIP * j : STRIP * j + STRIP].astype(F32)


def unpack(summed):
    return pl.pallas_call(
        unpack_body,
        out_shape=tuple(
            shape(s, F32) for s in ((240, D), (320, 240), (320, 240), (240, D), (240, 2560), (240, 2560), (D, STRIP))
        ),
        in_specs=[VM],
        out_specs=[VM] * 7,
        compiler_params=params(),
        name="unpack",
    )(summed)


def fill_bias(bias, lens, slot, f):
    key = lax.broadcasted_iota(jnp.int32, (SEQ, ROWS), 0)
    place = lax.broadcasted_iota(jnp.int32, (SEQ, ROWS), 1) + f * ROWS
    one = jnp.where((key <= place) & (key < lens[0, slot]), 0.0, masked_score)
    for r in range(GROUP):
        bias[:, r * ROWS : (r + 1) * ROWS] = one


HEADS_SHAPE = (KV_HEADS, GROUP * ROWS, 128)
KEYS_SHAPE = (KV_HEADS, SEQ, 128)
WIDE, NARROW = (ROWS, 2560), (ROWS, D)


def head_rows(h):
    return slice(h % GROUP * ROWS, (h % GROUP + 1) * ROWS)


def front_part(step, spot, mover, streams, lens, hid, gains, load_w, w, cosine, signed, n1, q, kv, att, lse, bias, outs):
    section = lax.axis_index("section")
    slot = step // 2 if step != 1 else 1 - section
    h = hid[...].astype(F32)
    inverse = lax.rsqrt(jnp.mean(h * h, axis=-1, keepdims=True) + norm_eps)
    n = (h * inverse * gain_row(gains, 0)).astype(BF)
    n1[...] = n
    streams.emit(hid, outs[0])
    streams.emit(n1, outs[1])
    low = lanes() < 64
    half = lax.rem(lanes(), 64) < 32
    cos, sin = cosine[...], signed[...]
    load_w.wait()
    proj = dot(n, w[:, :STRIP])
    tile = [proj[:, 128 * i : 128 * i + 128] for i in range(5)]
    turned = [turn(tile[i], cos, sin, half) for i in range(3)]
    mine = pl.ds(pl.multiple_of(spot.f * ROWS, ROWS), ROWS)
    other = pl.ds(pl.multiple_of(((1 - spot.zl) * 2 + spot.c) * ROWS, ROWS), ROWS)
    across, near, far = [], [], []
    for g in range(KV_HEADS):
        k_tile, v_tile = turned[g // 2], tile[(5 + g) // 2]
        if g % 2 == 0:
            both = jnp.where(low, k_tile, v_tile)
        else:
            both = pltpu.roll(jnp.where(low, v_tile, k_tile), 64, 1)
        kv[g, mine] = both.astype(BF)
        block = kv.at[g, mine]
        across.append(mover.push(block, block, spot.z))
        near.append(mover.push(block, block, spot.core))
    proj = dot(n, w[:, STRIP:])
    for i in range(8):
        t = turn(proj[:, 128 * i : 128 * i + 128], cos, sin, half) * (HEAD_DIM**-0.5)
        for h in (2 * i, 2 * i + 1):
            if h < HEADS:
                part = pltpu.roll(t, 64, 1) if h % 2 else t
                q[h // GROUP, head_rows(h)] = jnp.where(low, part, 0.0).astype(BF)
    streams.emit(q, outs[2])
    fill_bias(bias, lens, slot, spot.f)

    def onward(g):
        across[g].wait_recv()
        block = kv.at[g, other]
        far.append(mover.push(block, block, spot.core))

    onward(0)
    for g in range(KV_HEADS):
        if g + 1 < KV_HEADS:
            onward(g + 1)
        near[g].wait_recv()
        far[g].wait_recv()
        if g + 1 == KV_HEADS:
            streams.emit(kv, outs[3])
        keys = kv[g]
        keys_t = keys.astype(F32).T.astype(BF)
        s = dot_nt(keys, q[g]) + bias[...]
        top = jnp.max(s, axis=0, keepdims=True)
        e = jnp.exp(s - top)
        total = jnp.sum(e, axis=0, keepdims=True)
        att[g] = (dot(keys_t, e.astype(BF)) / total).T.astype(BF)
        log_total = top + jnp.log(total)
        for r in range(GROUP):
            lse[g, r : r + 1] = log_total[:, r * ROWS : (r + 1) * ROWS]


FRONT_OUTS = (
    shape(NARROW, BF), shape(NARROW, BF), shape(HEADS_SHAPE, BF), shape(KEYS_SHAPE, BF),
    shape(HEADS_SHAPE, BF), shape((KV_HEADS, 8, ROWS), F32),
)
FRONT_SPECS = [HBM] * 4 + [VM] * 2
FRONT_SLOTS = [
    pltpu.VMEM((D, 1664), BF), pltpu.VMEM(NARROW, BF), pltpu.VMEM(NARROW, BF), pltpu.VMEM(HEADS_SHAPE, BF),
    pltpu.VMEM(KEYS_SHAPE, BF), pltpu.VMEM((SEQ, GROUP * ROWS), F32),
]


def front_first_body(lens, own_t, gains, full, cosine, signed, o_hid, o_n1, o_q, o_kv, att, lse,
                     w, hid, n1, q, kv, bias, sems, send, recv):
    spot = Spot()
    pair_greet(spot, None)
    streams = Streams(sems)
    load_w = streams.start(full.at[0, :, pl.ds(0, 1664)], w)
    hid[...] = jnp.where(lax.axis_index("section") == 0, own_t[...].astype(F32).T, 0.0).astype(BF)
    mover = Mover(send, recv)
    front_part(0, spot, mover, streams, lens, hid, gains, load_w, w, cosine, signed, n1, q, kv, att, lse, bias,
               (o_hid, o_n1, o_q, o_kv))
    mover.finish()
    streams.finish()


def front_first(lens, own_t, gains, full, cosine, signed):
    return pl.pallas_call(
        front_first_body,
        out_shape=FRONT_OUTS,
        in_specs=[SM, VM, VM, HBM, VM, VM],
        out_specs=FRONT_SPECS,
        scratch_shapes=FRONT_SLOTS + [pltpu.SemaphoreType.DMA((5,)), pltpu.SemaphoreType.DMA((15,)), pltpu.SemaphoreType.DMA((15,))],
        compiler_params=linked(3),
        name="front_first",
    )(lens, own_t, gains, full, cosine, signed)


def load_weights(streams, full, wo, wg, wu, wd, order):
    views = {
        "o": (full.at[0, :, pl.ds(1536, 1024)], wo), "g": (full.at[1], wg), "u": (full.at[2], wu), "d": (full.at[3], wd),
    }
    return {k: streams.start(*views[k]) for k in order}


def rest_part(streams, loads, att, hid, gains, wo, wg, wu, wd, mid_s, n2_s, gate_s, up_s, mixed_s, compact_s, out_s, outs):
    low = lanes() < 64

    def head(h):
        return att[h // GROUP, head_rows(h)].astype(F32)

    for h in range(0, HEADS - 1, 2):
        pair = jnp.where(low, pltpu.roll(head(h), 64, 1), head(h + 1))
        compact_s[:, 64 * h : 64 * h + 128] = pair.astype(BF)
    compact_s[:, 896:960] = pltpu.roll(head(HEADS - 1), 64, 1)[:, :64].astype(BF)
    streams.emit(compact_s, outs[5])
    loads["o"].wait()
    mid = hid[...].astype(F32) + dot(compact_s[...], wo[...])[:, 64:]
    mid_s[...] = mid
    inverse = lax.rsqrt(jnp.mean(mid * mid, axis=-1, keepdims=True) + norm_eps)
    n2_s[...] = (mid * inverse * gain_row(gains, 1)).astype(BF)
    if outs[0] is not None:
        streams.emit(mid_s, outs[0])
    streams.emit(n2_s, outs[1])
    loads["g"].wait()
    loads["u"].wait()
    for i in range(2):
        cols = slice(1280 * i, 1280 * i + 1280)
        n = n2_s[...]
        g = dot(n, wg[:, cols])
        u = dot(n, wu[:, cols])
        gate_s[:, cols] = g.astype(BF)
        up_s[:, cols] = u.astype(BF)
        mixed_s[:, cols] = (g * jax.nn.sigmoid(g) * u).astype(BF)
    if outs[2] is not None:
        streams.emit(gate_s, outs[2])
        streams.emit(up_s, outs[3])
    streams.emit(mixed_s, outs[4])
    loads["d"].wait()
    y = mid_s[...] + dot_nt(mixed_s[...], wd[...])
    out_s[...] = y.astype(BF)
    return y


WEIGHT_SLOTS = [pltpu.VMEM((D, 1024), BF)] + [pltpu.VMEM((D, 2560), BF)] * 3
REST_SLOTS = [
    pltpu.VMEM(NARROW, F32), pltpu.VMEM(NARROW, BF), pltpu.VMEM(WIDE, BF), pltpu.VMEM(WIDE, BF),
    pltpu.VMEM(WIDE, BF), pltpu.VMEM(NARROW, BF), pltpu.VMEM(NARROW, BF),
]


def forward_body(step, lens, att, hid, own_t, gains, full, cosine, signed,
                 out_t, o_mid, o_n2, o_gate, o_up, o_mixed, o_compact, o_hid, o_n1, o_q, o_kv, att_next, lse,
                 wo, wg, wu, wd, mid_s, n2_s, gate_s, up_s, mixed_s, compact_s, out_s,
                 w, hid_s, n1, q, kv, bias, passed_on, sems, send, recv, ready):
    streams = Streams(sems)
    loads = load_weights(streams, full, wo, wg, wu, wd, "ogud")
    load_w = streams.start(full.at[0, :, pl.ds(0, 1664)], w)
    spot = Spot()
    section = lax.axis_index("section")
    pair_greet(spot, (section, 0, ready))
    y = rest_part(streams, loads, att, hid, gains, wo, wg, wu, wd, mid_s, n2_s, gate_s, up_s, mixed_s, compact_s, out_s,
                  (o_mid, o_n2, o_gate, o_up, o_mixed, o_compact))

    @pl.when(section == 0)
    def _():
        pl.semaphore_wait(ready, 1)
        relay_copy(section, out_s, passed_on, send.at[15], recv.at[15]).start()
        hid_s[...] = own_t[...].astype(F32).T.astype(BF)

    out_t[...] = y.T.astype(BF)

    @pl.when(section == 1)
    def _():
        relay_copy(section, out_s, passed_on, send.at[15], recv.at[15]).wait_recv()
        hid_s[...] = passed_on[...]

    mover = Mover(send, recv)
    front_part(step + 1, spot, mover, streams, lens, hid_s, gains, load_w, w, cosine, signed, n1, q, kv, att_next, lse, bias,
               (o_hid, o_n1, o_q, o_kv))
    mover.finish()

    @pl.when(section == 0)
    def _():
        relay_copy(section, out_s, passed_on, send.at[15], recv.at[15]).wait_send()

    streams.finish()


def forward(step, lens, att, hid, own_t, gains, full, cosine, signed):
    rest_outs = (shape((D, ROWS), BF), shape(NARROW, F32), shape(NARROW, BF)) + (shape(WIDE, BF),) * 3 + (shape(NARROW, BF),)
    return pl.pallas_call(
        functools.partial(forward_body, step),
        out_shape=rest_outs + FRONT_OUTS,
        in_specs=[SM, VM, VM, VM, VM, HBM, VM, VM],
        out_specs=[VM] + [HBM] * 6 + FRONT_SPECS,
        scratch_shapes=WEIGHT_SLOTS + REST_SLOTS + FRONT_SLOTS + [
            pltpu.VMEM(NARROW, BF), pltpu.SemaphoreType.DMA((16,)), pltpu.SemaphoreType.DMA((16,)),
            pltpu.SemaphoreType.DMA((16,)), pltpu.SemaphoreType.REGULAR,
        ],
        compiler_params=linked(4 + step, 60),
        name="forward",
    )(lens, att, hid, own_t, gains, full, cosine, signed)


def back_rest_part(streams, loads, g_out, gains, mid_ref, gate_s, up_s, gg_s, gu_s, gm_s, wo, wg, wu, wd, gao_out, part, da, outs):
    loads["d"].wait()
    for i in range(2):
        cols = slice(1280 * i, 1280 * i + 1280)
        grad_mixed = dot(g_out[...], wd[:, cols])
        ga = gate_s[:, cols].astype(F32)
        sg = jax.nn.sigmoid(ga)
        scaled = grad_mixed * sg
        gg_s[:, cols] = (scaled * up_s[:, cols].astype(F32) * (1.0 + ga * (1.0 - sg))).astype(BF)
        gu_s[:, cols] = (scaled * ga).astype(BF)
    streams.emit(gg_s, outs[0])
    streams.emit(gu_s, outs[1])
    loads["g"].wait()
    loads["u"].wait()
    grad_normed = dot_nt(gg_s[...], wg[...]) + dot_nt(gu_s[...], wu[...])
    mid = mid_ref[...]
    inverse = lax.rsqrt(jnp.mean(mid * mid, axis=-1, keepdims=True) + norm_eps)
    unit = mid * inverse
    part[...] = jnp.sum(grad_normed * unit, axis=0, keepdims=True)
    scaled_two = grad_normed * gain_row(gains, 1)
    gm = g_out[...].astype(F32) + inverse * (
        scaled_two - unit * jnp.mean(scaled_two * unit, axis=-1, keepdims=True)
    )
    gm_s[...] = gm
    streams.emit(gm_s, outs[2])
    gao_out[...] = gm.astype(BF)
    shifted = jnp.concatenate([jnp.zeros((ROWS, 64), F32), gm], axis=1).astype(BF)
    loads["o"].wait()
    att = jnp.concatenate([dot_nt(shifted, wo[...]), jnp.zeros((ROWS, 64), F32)], axis=1)
    low = lanes() < 64
    for h in range(HEADS):
        tile = att[:, 128 * (h // 2) : 128 * (h // 2) + 128]
        if h % 2 == 0:
            tile = pltpu.roll(tile, 64, 1)
        da[h // GROUP, head_rows(h)] = jnp.where(low, 0.0, tile).astype(BF)


def live_cotangent(step, lens, cot_t):
    place = lax.broadcasted_iota(jnp.int32, (D, ROWS), 1) + lax.axis_index("fsdp") * ROWS
    return jnp.where(place < lens[0, 1 - step], cot_t[...].astype(F32), 0.0).T.astype(BF)


BACK_OUTS = (
    shape(WIDE, BF), shape(WIDE, BF), shape(NARROW, F32), shape(NARROW, BF), shape((1, D), F32),
    shape(HEADS_SHAPE, BF), shape(NARROW, BF),
)
BACK_SPECS = [HBM] * 3 + [VM] * 4


def turn_back_body(lens, att, hid, cot_t, gains, full,
                   out_t, o_n2, o_mixed, o_compact, o_gg, o_gu, o_gm, gao, part, da, g_out,
                   wo, wg, wu, wd, mid_s, n2_s, gate_s, up_s, mixed_s, compact_s, out_s, gg_s, gu_s, gm_s, sems):
    streams = Streams(sems)
    loads = load_weights(streams, full, wo, wg, wu, wd, "ogud")
    y = rest_part(streams, loads, att, hid, gains, wo, wg, wu, wd, mid_s, n2_s, gate_s, up_s, mixed_s, compact_s, out_s,
                  (None, o_n2, None, None, o_mixed, o_compact))
    out_t[...] = y.T.astype(BF)
    g_out[...] = jnp.where(lax.axis_index("section") == 1, live_cotangent(0, lens, cot_t), 0.0).astype(BF)

    class Done:
        def wait(self):
            pass

    back_rest_part(streams, {k: Done() for k in "ogud"}, g_out, gains, mid_s, gate_s, up_s, gg_s, gu_s, gm_s,
                   wo, wg, wu, wd, gao, part, da, (o_gg, o_gu, o_gm))
    streams.finish()


def turn_back(lens, att, hid, cot_t, gains, full):
    return pl.pallas_call(
        turn_back_body,
        out_shape=(shape((D, ROWS), BF), shape(NARROW, BF), shape(WIDE, BF), shape(NARROW, BF)) + BACK_OUTS,
        in_specs=[SM, VM, VM, VM, VM, HBM],
        out_specs=[VM] + [HBM] * 3 + BACK_SPECS,
        scratch_shapes=WEIGHT_SLOTS + REST_SLOTS + [
            pltpu.VMEM(WIDE, BF), pltpu.VMEM(WIDE, BF), pltpu.VMEM(NARROW, F32), pltpu.SemaphoreType.DMA((12,)),
        ],
        compiler_params=params(60),
        name="turn_back",
    )(lens, att, hid, cot_t, gains, full)


def back_attend_part(step, spot, mover, lens, q, kv, lse, da, cosine, signed, hid, gains, load_w, w, gm, packed, gain_part,
                     bias, part, near, passed, far, own, dq):
    section = lax.axis_index("section")
    slot = 1 - section if step == 1 else 1 - step // 2
    fill_bias(bias, lens, slot, spot.f)
    low = lanes() < 64
    half = lax.rem(lanes(), 64) < 32
    cos, sin = cosine[...], -signed[...]

    def rows_of(zl, c):
        return pl.ds(pl.multiple_of((zl * 2 + c) * ROWS, ROWS), ROWS)

    there, here = 1 - spot.zl, spot.zl
    core, across = {}, {}

    def stage_one(g):
        core[g][0].wait_recv()
        passed[g] = (part[g, rows_of(there, spot.c)].astype(F32) + near[g, 0].astype(F32)).astype(BF)
        across[g] = mover.push(passed.at[g], far.at[g], spot.z)
        core[g][1].wait_recv()
        own[g] = part[g, rows_of(here, spot.c)].astype(F32) + near[g, 1].astype(F32)

    def stage_two(g):
        across[g].wait_recv()
        own[g] = own[g] + far[g].astype(F32)

    for g in range(KV_HEADS):
        keys = kv[g]
        keys_t = keys.astype(F32).T.astype(BF)
        logs = jnp.concatenate([lse[g, r : r + 1] for r in range(GROUP)], axis=1)
        p = jnp.exp(dot_nt(keys, q[g]) + bias[...] - logs)
        dp = dot_nt(keys, da[g])
        delta = jnp.sum(p * dp, axis=0, keepdims=True)
        ds = (p * (dp - delta)).astype(BF)
        part[g] = (dot(ds, q[g]) + dot(p.astype(BF), da[g])).astype(BF)
        core[g] = (
            mover.push(part.at[g, rows_of(there, 1 - spot.c)], near.at[g, 0], spot.core),
            mover.push(part.at[g, rows_of(here, 1 - spot.c)], near.at[g, 1], spot.core),
        )
        grad_q = (dot(keys_t, ds) * (HEAD_DIM**-0.5)).T
        for r in range(GROUP):
            rows = slice(r * ROWS, (r + 1) * ROWS)
            dq[g, rows] = turn(grad_q[rows], cos, sin, half).astype(BF)
        if g > 0:
            stage_one(g - 1)
        if g > 1:
            stage_two(g - 2)

    def merged(left, right):
        return jnp.where(low, left, right)

    def flip(v):
        return pltpu.roll(v, 64, 1)

    def head(h):
        return dq[h // GROUP, head_rows(h)].astype(F32)

    for h in range(0, HEADS, 2):
        tile = merged(head(h), flip(head(h + 1)) if h + 1 < HEADS else 0.0)
        packed[:, STRIP + 64 * h : STRIP + 64 * h + 128] = tile.astype(BF)
    stage_one(KV_HEADS - 1)
    load_w.wait()
    grad_normed = dot_nt(packed[:, STRIP:], w[:, STRIP:])
    hidden = hid[...].astype(F32)
    inverse = lax.rsqrt(jnp.mean(hidden * hidden, axis=-1, keepdims=True) + norm_eps)
    unit = hidden * inverse
    stage_two(KV_HEADS - 2)
    stage_two(KV_HEADS - 1)
    both = [own[g] for g in range(KV_HEADS)]
    turned = [turn(b, cos, sin, half) for b in both]
    tiles = [
        merged(turned[0], flip(turned[1])),
        merged(turned[2], flip(turned[3])),
        merged(turned[4], both[0]),
        merged(flip(both[1]), both[2]),
        merged(flip(both[3]), both[4]),
    ]
    for i, tile in enumerate(tiles):
        packed[:, 128 * i : 128 * i + 128] = tile.astype(BF)
    grad_normed = grad_normed + dot_nt(packed[:, :STRIP], w[:, :STRIP])
    gain_part[...] = jnp.sum(grad_normed * unit, axis=0, keepdims=True)
    scaled = grad_normed * gain_row(gains, 0)
    return gm[...] + inverse * (scaled - unit * jnp.mean(scaled * unit, axis=-1, keepdims=True))


OWN_SHAPE = (KV_HEADS, ROWS, 128)
ATTEND_SLOTS = [
    pltpu.VMEM((SEQ, GROUP * ROWS), F32), pltpu.VMEM(KEYS_SHAPE, BF), pltpu.VMEM((KV_HEADS, 2, ROWS, 128), BF),
    pltpu.VMEM(OWN_SHAPE, BF), pltpu.VMEM(OWN_SHAPE, BF), pltpu.VMEM(OWN_SHAPE, F32), pltpu.VMEM(HEADS_SHAPE, BF),
    pltpu.VMEM((D, 1664), BF),
]
ATTEND_OUTS = (shape((D, ROWS), F32), shape((ROWS, 1664), BF), shape((1, D), F32))


def backward_body(step, lens, q, kv, lse, da, cosine, signed, hid, gains, full, gm, cot_t, mid, gate, up,
                  grad_t, packed, gain_part, o_gg, o_gu, o_gm, gao, part_two, da_next, g_out,
                  bias, part, near, passed, far, own, dq, w, wo, wg, wu, wd, gate_s, up_s, gg_s, gu_s, gm_s,
                  out_s, passed_on, sems, send, recv, ready):
    streams = Streams(sems)
    load_w = streams.start(full.at[0, :, pl.ds(0, 1664)], w)
    loads = load_weights(streams, full, wo, wg, wu, wd, "dguo")
    load_gate = streams.start(gate, gate_s)
    load_up = streams.start(up, up_s)
    spot = Spot()
    section = lax.axis_index("section")
    pair_greet(spot, (section, 1, ready))
    mover = Mover(send, recv)
    grad_in = back_attend_part(step, spot, mover, lens, q, kv, lse, da, cosine, signed, hid, gains, load_w, w, gm,
                               packed, gain_part, bias, part, near, passed, far, own, dq)
    out_s[...] = grad_in.astype(BF)

    @pl.when(section == 1)
    def _():
        pl.semaphore_wait(ready, 1)
        relay_copy(section, out_s, passed_on, send.at[15], recv.at[15]).start()
        if step == 0:
            g_out[...] = live_cotangent(1, lens, cot_t)
        else:
            g_out[...] = jnp.zeros(NARROW, BF)

    grad_t[...] = grad_in.T

    @pl.when(section == 0)
    def _():
        relay_copy(section, out_s, passed_on, send.at[15], recv.at[15]).wait_recv()
        g_out[...] = passed_on[...]

    load_gate.wait()
    load_up.wait()
    back_rest_part(streams, loads, g_out, gains, mid, gate_s, up_s, gg_s, gu_s, gm_s, wo, wg, wu, wd, gao, part_two, da_next,
                   (o_gg, o_gu, o_gm))
    mover.finish()

    @pl.when(section == 1)
    def _():
        relay_copy(section, out_s, passed_on, send.at[15], recv.at[15]).wait_send()

    streams.finish()


def backward(step, lens, q, kv, lse, da, cosine, signed, hid, gains, full, gm, cot_t, mid, gate, up):
    return pl.pallas_call(
        functools.partial(backward_body, step),
        out_shape=ATTEND_OUTS + BACK_OUTS,
        in_specs=[SM] + [VM] * 8 + [HBM, VM, VM, VM, HBM, HBM],
        out_specs=[VM] * 3 + BACK_SPECS,
        scratch_shapes=ATTEND_SLOTS + WEIGHT_SLOTS + [pltpu.VMEM(WIDE, BF)] * 4 + [
            pltpu.VMEM(NARROW, F32), pltpu.VMEM(NARROW, BF), pltpu.VMEM(NARROW, BF), pltpu.SemaphoreType.DMA((10,)),
            pltpu.SemaphoreType.DMA((16,)), pltpu.SemaphoreType.DMA((16,)), pltpu.SemaphoreType.REGULAR,
        ],
        compiler_params=linked(6 + step, 62),
        name="backward",
    )(lens, q, kv, lse, da, cosine, signed, hid, gains, full, gm, cot_t, mid, gate, up)


def back_last_body(lens, q, kv, lse, da, cosine, signed, hid, gains, full, gm,
                   grad_t, packed, gain_part, bias, part, near, passed, far, own, dq, w, sems, send, recv):
    streams = Streams(sems)
    load_w = streams.start(full.at[0, :, pl.ds(0, 1664)], w)
    spot = Spot()
    pair_greet(spot, None)
    mover = Mover(send, recv)
    grad_in = back_attend_part(2, spot, mover, lens, q, kv, lse, da, cosine, signed, hid, gains, load_w, w, gm,
                               packed, gain_part, bias, part, near, passed, far, own, dq)
    grad_t[...] = grad_in.T
    mover.finish()


def back_last(lens, q, kv, lse, da, cosine, signed, hid, gains, full, gm):
    return pl.pallas_call(
        back_last_body,
        out_shape=ATTEND_OUTS,
        in_specs=[SM] + [VM] * 8 + [HBM, VM],
        out_specs=[VM] * 3,
        scratch_shapes=ATTEND_SLOTS + [pltpu.SemaphoreType.DMA((1,)), pltpu.SemaphoreType.DMA((15,)), pltpu.SemaphoreType.DMA((15,))],
        compiler_params=linked(8, 60),
        name="back_last",
    )(lens, q, kv, lse, da, cosine, signed, hid, gains, full, gm)


MESH = pl.DeviceIdType.MESH
SIDE = 4
OFFSETS = (1, 3, 2)
HALVES = ((0, 128), (128, 112))


class Spot:
    def __init__(self):
        d = lax.axis_index("dp")
        f = lax.axis_index("fsdp")
        self.x, self.y = d // SIDE, lax.rem(d, SIDE)
        self.zl, self.c = f // 2, lax.rem(f, 2)
        self.f = f
        self.core = {"fsdp": self.zl * 2 + 1 - self.c}
        self.z = {"fsdp": (1 - self.zl) * 2 + self.c}
        self.across = {"fsdp": (1 - self.zl) * 2 + 1 - self.c}

    def along_x(self, k):
        return {"dp": lax.rem(self.x + k, SIDE) * SIDE + self.y}

    def along_y(self, k):
        return {"dp": self.x * SIDE + lax.rem(self.y + k, SIDE)}

    def greet(self):
        barrier = pltpu.get_barrier_semaphore()
        ids = [self.core, self.z, self.across]
        for k in range(1, SIDE):
            ids += [self.along_x(k), self.along_y(k)]
        for who in ids:
            pl.semaphore_signal(barrier, inc=1, device_id=who, device_id_type=MESH)
        pl.semaphore_wait(barrier, len(ids))


class Mover:
    def __init__(self, send, recv):
        self.send, self.recv, self.pending = send, recv, []

    def push(self, src, dst, who):
        i = len(self.pending)
        copy = pltpu.make_async_remote_copy(
            src_ref=src, dst_ref=dst, send_sem=self.send.at[i], recv_sem=self.recv.at[i],
            device_id=who, device_id_type=MESH,
        )
        copy.start()
        self.pending.append(copy)
        return copy

    def finish(self):
        for copy in self.pending:
            copy.wait_send()


def region(stack, f, m, j, lo=0, size=240):
    tall = m // 3
    row = f + tall * (j - f)
    col = j + tall * (f - j)
    return stack.at[m, pl.ds(pl.multiple_of(row * 240 + lo, 16), size), pl.ds(pl.multiple_of(col * 640, 128), 640)]


def shard_parts(stack, packed, f):
    rows = pl.ds(pl.multiple_of(f * 240, 16), 240)
    parts = [(stack.at[m, rows], packed.at[m]) for m in range(3)]
    cols = pl.ds(pl.multiple_of(f * 640, 128), 640)
    for j in range(4):
        parts.append((stack.at[3, pl.ds(j * 240, 240), cols], packed.at[3, :, pl.ds(j * 640, 640)]))
    return parts


def gather_kernel(own, gains, full, gains_full, held, send, recv, local):
    spot = Spot()
    x, y, f = spot.x, spot.y, spot.f
    fz = (1 - spot.zl) * 2 + spot.c
    spot.greet()
    mover = Mover(send, recv)
    first = mover.push(own.at[x, :, pl.ds(pl.multiple_of(y * 640, 128), 640)], region(full, f, x, y), spot.z)
    waits = []
    for k in range(1, 4):
        who = {"fsdp": lax.rem(f + k, 4)}
        waits.append(mover.push(gains, gains_full.at[f], who))
    load = pltpu.make_async_copy(own, held, local.at[8])
    load.start()
    for there, here in shard_parts(full, own, f):
        waits.append(mover.push(here, there, spot.core))
    load.wait()
    locals_ = [pltpu.make_async_copy(gains, gains_full.at[f], local.at[0])]
    for i, (there, here) in enumerate(shard_parts(full, held, f)):
        locals_.append(pltpu.make_async_copy(here, there, local.at[1 + i]))
    for copy in locals_:
        copy.start()
    first.wait_recv()

    def onward(view):
        waits.append(mover.push(view, view, spot.core))

    stage_one = []
    for k in OFFSETS:
        a = region(full, fz, x, y, *HALVES[0])
        b = region(full, fz, x, y, *HALVES[1])
        stage_one.append((mover.push(a, a, spot.along_x(k)), mover.push(b, b, spot.along_y(k))))
    stage_two = []

    def second(m, j):
        a = region(full, fz, m, y, *HALVES[0])
        b = region(full, fz, x, j, *HALVES[1])
        for k in OFFSETS:
            stage_two.append((k, m, j, mover.push(a, a, spot.along_y(k)), mover.push(b, b, spot.along_x(k))))

    second(x, y)
    onward(region(full, fz, x, y))
    for k, (copy_a, copy_b) in zip(OFFSETS, stage_one):
        m, j = lax.rem(x + 4 - k, SIDE), lax.rem(y + 4 - k, SIDE)
        copy_a.wait_recv()
        copy_b.wait_recv()
        second(m, j)
        onward(region(full, fz, m, y, *HALVES[0]))
        onward(region(full, fz, x, j, *HALVES[1]))
    for k, m, j, copy_a, copy_b in stage_two:
        copy_a.wait_recv()
        onward(region(full, fz, m, lax.rem(y + 4 - k, SIDE), *HALVES[0]))
        copy_b.wait_recv()
        onward(region(full, fz, lax.rem(x + 4 - k, SIDE), j, *HALVES[1]))
    for copy in waits:
        copy.wait_recv()
    mover.finish()
    for copy in locals_:
        copy.wait()


def gather_weights(own, gains):
    n = 96
    return pl.pallas_call(
        gather_kernel,
        out_shape=(
            jax.ShapeDtypeStruct((4, 960, 2560), own.dtype),
            jax.ShapeDtypeStruct((4,) + gains.shape, gains.dtype),
        ),
        in_specs=[pl.BlockSpec(memory_space=pl.ANY), pl.BlockSpec(memory_space=pltpu.VMEM)],
        out_specs=[pl.BlockSpec(memory_space=pl.ANY), pl.BlockSpec(memory_space=pltpu.VMEM)],
        scratch_shapes=[
            pltpu.VMEM((4, 240, 2560), own.dtype),
            pltpu.SemaphoreType.DMA((n,)),
            pltpu.SemaphoreType.DMA((n,)),
            pltpu.SemaphoreType.DMA((9,)),
        ],
        compiler_params=pltpu.CompilerParams(collective_id=1, has_side_effects=True, vmem_limit_bytes=60 * 2**20),
        name="gather_weights",
    )(own, gains)


STEP = 16


def add_rows(out, rows, terms):
    def body(i, carry):
        sl = pl.ds(pl.multiple_of(i * STEP, STEP), STEP)
        total = terms[0](sl).astype(F32)
        for term in terms[1:]:
            total = total + term(sl).astype(F32)
        out(sl, total.astype(BF))
        return carry

    lax.fori_loop(0, rows // STEP, body, 0)


def dot_tn(a, b):
    return lax.dot_general(a, b, (((0,), (0,)), ((), ())), preferred_element_type=F32)


ORDER = (3, 2, 1, 0)


def finish_body(*refs):
    n1, att, n2, gd, packed, gao, gg, gu, mixed = (refs[3 * i : 3 * i + 3] for i in range(9))
    (gains, out, gains_out, stack, theirs, left, left_b, right, right_p, right_q, hx, hy, rx, ry, ta, tb, rx2, ry2,
     ua, ub, rz, g_core, g_mine, g_x, g_y, send, recv, local) = refs[27:]
    spot = Spot()
    x, y = spot.x, spot.y
    section = lax.axis_index("section")
    fa, fb = spot.zl * 2 + spot.c, (1 - spot.zl) * 2 + spot.c
    pa, pb = spot.zl * 2 + 1 - spot.c, (1 - spot.zl) * 2 + 1 - spot.c

    loads = [0]

    def load(trio, dst):
        i = loads[0]
        loads[0] += 2
        fixed = pltpu.make_async_copy(trio[1], dst.at[pl.ds(ROWS, ROWS)], local.at[i])
        fixed.start()
        early = pltpu.make_async_copy(trio[0], dst.at[pl.ds(0, ROWS)], local.at[i + 1])
        late = pltpu.make_async_copy(trio[2], dst.at[pl.ds(0, ROWS)], local.at[i + 1])
        pl.when(section == 1)(early.start)
        pl.when(section == 0)(late.start)

        def wait():
            fixed.wait()
            pl.when(section == 1)(early.wait)
            pl.when(section == 0)(late.wait)

        return wait

    waits = {3: [load(gd, left.at[0]), load(mixed, right.at[0])], 2: [load(n2, left.at[1]), load(gu, right.at[1])]}
    spot.greet()
    mover = Mover(send, recv)
    small = [mover.push(gains.at[p], g_core.at[i], spot.core) for i, p in enumerate((pa, pb))]
    stack[:, :, pl.ds(240, 16)] = jnp.zeros((4, 4, 16, 2560), BF)

    def compute(m):
        for wait in waits[m]:
            wait()
        if m == 0:
            v = dot_tn(left[0], right_p[:, :1280])
            v2 = jnp.concatenate([dot_tn(left[0], right_p[:, 1280:1600]), dot_tn(left_b[...], right_q[...])], axis=1)
            for i, value in enumerate((v, v2)):
                for f in range(4):
                    stack[0, f, pl.ds(0, 240), pl.ds(1280 * i, 1280)] = value[240 * f : 240 * f + 240].astype(BF)
            return
        lhs, rhs = {3: (0, 0), 2: (1, 1), 1: (1, 0)}[m]
        for i in range(2):
            v = dot_tn(left[lhs], right[rhs, :, pl.ds(1280 * i, 1280)])
            for f in range(4):
                if m < 3:
                    stack[m, f, pl.ds(0, 240), pl.ds(1280 * i, 1280)] = v[240 * f : 240 * f + 240].astype(BF)
                elif f // 2 == i:
                    for j in range(4):
                        cols = slice(STRIP * (f % 2), STRIP * (f % 2) + STRIP)
                        stack[3, f, pl.ds(0, 240), pl.ds(STRIP * j, STRIP)] = v[240 * j : 240 * j + 240, cols].astype(BF)
        if m == 3:
            waits[1] = [load(gg, right.at[0])]
            waits[0] = [load(n1, left.at[0]), load(att, left_b), load(packed, right_p), load(gao, right_q)]

    def chunk(p, lo=0, size=64):
        return pl.ds(pl.multiple_of(lax.rem(p, SIDE) * 64 + lo, 16), size)

    def strip(p):
        return pl.ds(pl.multiple_of(lax.rem(p, SIDE) * STRIP, 128), STRIP)

    flights = {}

    def send_core(m):
        flights["core", m] = (
            mover.push(stack.at[m, pa], theirs.at[m, 0], spot.core), mover.push(stack.at[m, pb], theirs.at[m, 1], spot.core)
        )

    def await_all(*key):
        for copy in flights[key]:
            copy.wait_recv()

    def stage_one(m):
        await_all("core", m)
        for i, f in enumerate((fa, fb)):
            def put(sl, v, f=f):
                stack[m, f, sl] = v
            add_rows(put, 256, [lambda sl, f=f: stack[m, f, sl], lambda sl, i=i: theirs[m, i, sl]])
        flights["half", m] = (
            mover.push(stack.at[m, fa, chunk(x + 2, 0, 32)], hx.at[0, m], spot.along_x(1)),
            mover.push(stack.at[m, fa, chunk(x + 2, 32, 32)], hx.at[1, m], spot.along_x(3)),
            mover.push(stack.at[m, fb, pl.ds(0, 128), strip(y + 2)], hy.at[0, m], spot.along_y(1)),
            mover.push(stack.at[m, fb, pl.ds(128, 128), strip(y + 2)], hy.at[1, m], spot.along_y(3)),
        )

    def stage_two(m):
        await_all("half", m)
        for i, k in ((0, 1), (1, 3)):
            base = lax.rem(x + k, SIDE) * 64 + 32 * i

            def rows(sl, base=base):
                return pl.ds(pl.multiple_of(base + sl.start, 16), STEP)

            def put(sl, v, rows=rows):
                stack[m, fa, rows(sl)] = v
            add_rows(put, 32, [lambda sl, rows=rows: stack[m, fa, rows(sl)], lambda sl, i=i: hx[i, m, sl]])

            def low(sl, i=i):
                return pl.ds(pl.multiple_of(128 * i + sl.start, 16), STEP)

            def put(sl, v, low=low, k=k):
                stack[m, fb, low(sl), strip(y + k)] = v
            add_rows(put, 128, [lambda sl, low=low, k=k: stack[m, fb, low(sl), strip(y + k)], lambda sl, i=i: hy[i, m, sl]])
        flights["next", m] = tuple(
            copy
            for i, k in ((0, 1), (1, 3))
            for copy in (
                mover.push(stack.at[m, fa, chunk(x + k)], rx.at[i, m], spot.along_x(k)),
                mover.push(stack.at[m, fb, :, strip(y + k)], ry.at[i, m], spot.along_y(k)),
            )
        )

    def stage_three(m):
        await_all("next", m)
        base = x * 64

        def put(sl, v):
            ta[m, sl] = v
        own = lambda sl: stack[m, fa, pl.ds(pl.multiple_of(base + sl.start, 16), STEP)]
        add_rows(put, 64, [own, lambda sl: rx[0, m, sl], lambda sl: rx[1, m, sl]])

        def put(sl, v):
            tb[m, sl] = v
        add_rows(put, 256, [lambda sl: stack[m, fb, sl, strip(y)], lambda sl: ry[0, m, sl], lambda sl: ry[1, m, sl]])
        flights["second", m] = tuple(
            copy
            for i, k in enumerate(OFFSETS)
            for copy in (
                mover.push(ta.at[m, :, strip(y + k)], ry2.at[i, m], spot.along_y(k)),
                mover.push(tb.at[m, chunk(x + k)], rx2.at[i, m], spot.along_x(k)),
            )
        )

    def stage_four(m):
        await_all("second", m)
        base = x * 64

        def put(sl, v):
            ub[m, sl] = v
        own = lambda sl: tb[m, pl.ds(pl.multiple_of(base + sl.start, 16), STEP)]
        add_rows(put, 64, [own] + [lambda sl, i=i: rx2[i, m, sl] for i in range(3)])
        flights["z", m] = (mover.push(ub.at[m], rz.at[m], spot.z),)

        def put(sl, v):
            ua[m, sl] = v
        add_rows(put, 64, [lambda sl: ta[m, sl, strip(y)]] + [lambda sl, i=i: ry2[i, m, sl] for i in range(3)])

    def stage_five(m):
        await_all("z", m)

        def put(sl, v):
            ua[m, sl] = v
        add_rows(put, 64, [lambda sl: ua[m, sl], lambda sl: rz[m, sl]])

    def gains_step(t):
        if t == 1:
            for i, f in enumerate((fa, fb)):
                small[i].wait_recv()
                g_mine[0, i] = gains[f] + g_core[i]
            flights["gx"] = [mover.push(g_mine.at[0], g_x.at[i], spot.along_x(k)) for i, k in enumerate(OFFSETS)]
        if t == 3:
            for copy in flights["gx"]:
                copy.wait_recv()
            g_mine[1] = g_mine[0] + g_x[0] + g_x[1] + g_x[2]
            flights["gy"] = [mover.push(g_mine.at[1], g_y.at[i], spot.along_y(k)) for i, k in enumerate(OFFSETS)]
        if t == 5:
            for copy in flights["gy"]:
                copy.wait_recv()
            g_mine[2] = g_mine[1] + g_y[0] + g_y[1] + g_y[2]
            flights["gz"] = mover.push(g_mine.at[2, 1], g_core.at[2], spot.z)
        if t == 8:
            flights["gz"].wait_recv()
            gains_out[...] = g_mine[2, 0] + g_core[2]

    def place(ms, p, q):
        return out.at[pl.ds(*ms), chunk(p), strip(q)]

    spreads = []

    def spread(first, src):
        both, one, two = ((0, 2), (0, 1), (1, 1)) if first == 0 else ((2, 2), (2, 1), (3, 1))
        if first == 0:
            inner, outer = spot.along_x, spot.along_y
            view = lambda ms, a, b: place(ms, x + a, y + b)
        else:
            inner, outer = spot.along_y, spot.along_x
            view = lambda ms, a, b: place(ms, x + b, y + a)
        own = src.at[pl.ds(*both)]

        def begin():
            up = mover.push(own, view(both, 0, 0), inner(1))
            down = mover.push(own, view(both, 0, 0), inner(3))
            wide = {0: [mover.push(own, view(both, 0, 0), outer(k)) for k in (1, 3)]}
            yield
            up.wait_recv()
            down.wait_recv()
            r1, r3 = view(one, 3, 0), view(two, 1, 0)
            far = (mover.push(r1, r1, inner(1)), mover.push(r3, r3, inner(3)))
            for a in (3, 1):
                r = view(both, a, 0)
                wide[a] = [mover.push(r, r, outer(k)) for k in (1, 3)]
            yield
            ends = []

            def pass_on(a):
                wide[a][0].wait_recv()
                wide[a][1].wait_recv()
                r1, r3 = view(one, a, 3), view(two, a, 1)
                ends.extend((mover.push(r1, r1, outer(1)), mover.push(r3, r3, outer(3))))

            pass_on(0)
            for copy in far:
                copy.wait_recv()
            r = view(both, 2, 0)
            wide[2] = [mover.push(r, r, outer(k)) for k in (1, 3)]
            yield
            pass_on(3)
            pass_on(1)
            yield
            pass_on(2)
            for copy in ends:
                copy.wait_recv()
            yield

        return begin()

    stages = (stage_one, stage_two, stage_three, stage_four, stage_five)
    b_side = None
    for t in range(9):
        if t < 4:
            compute(ORDER[t])
            send_core(ORDER[t])
        gains_step(t)
        for s, stage in enumerate(stages):
            i = t - 1 - s
            if 0 <= i < 4:
                stage(ORDER[i])
        if t == 6:
            keep_b = pltpu.make_async_copy(ua.at[pl.ds(2, 2)], place((2, 2), x, y), local.at[0])
            keep_b.start()
            b_side = spread(2, ua)
            next(b_side)
    keep_a = pltpu.make_async_copy(ua.at[pl.ds(0, 2)], place((0, 2), x, y), local.at[1])
    keep_a.start()
    a_side = spread(0, ua)
    next(a_side)
    for _ in range(4):
        next(b_side)
        next(a_side)
    mover.finish()
    keep_a.wait()
    keep_b.wait()


def finish(sets, gains):
    vm = pltpu.VMEM
    n = 128
    return pl.pallas_call(
        finish_body,
        out_shape=(shape((4, 256, 2560), BF), shape(gains.shape[1:], F32)),
        in_specs=[HBM] * 27 + [VM],
        out_specs=[HBM, VM],
        scratch_shapes=[
            vm((4, 4, 256, 2560), BF), vm((4, 2, 256, 2560), BF),
            vm((2, 2 * ROWS, D), BF), vm((2 * ROWS, D), BF), vm((2, 2 * ROWS, 2560), BF), vm((2 * ROWS, 1664), BF), vm((2 * ROWS, D), BF),
            vm((2, 4, 32, 2560), BF), vm((2, 4, 128, STRIP), BF), vm((2, 4, 64, 2560), BF), vm((2, 4, 256, STRIP), BF),
            vm((4, 64, 2560), BF), vm((4, 256, STRIP), BF), vm((3, 4, 64, STRIP), BF), vm((3, 4, 64, STRIP), BF),
            vm((4, 64, STRIP), BF), vm((4, 64, STRIP), BF), vm((4, 64, STRIP), BF),
            vm((3, 8, 256), F32), vm((3, 2, 8, 256), F32), vm((3, 2, 8, 256), F32), vm((3, 2, 8, 256), F32),
            pltpu.SemaphoreType.DMA((n,)), pltpu.SemaphoreType.DMA((n,)), pltpu.SemaphoreType.DMA((20,)),
        ],
        compiler_params=linked(2, 63),
        name="finish",
    )(*[a for trio in sets for a in trio], gains)


def pair_greet(spot, relay):
    barrier = pltpu.get_barrier_semaphore()
    for who in (spot.core, spot.z):
        pl.semaphore_signal(barrier, inc=1, device_id=who, device_id_type=MESH)
    if relay is None:
        pl.semaphore_wait(barrier, 2)
        return
    section, sender, ready = relay
    beyond = {"section": 1 - section}

    @pl.when(section == sender)
    def _():
        pl.semaphore_signal(barrier, inc=1, device_id=beyond, device_id_type=MESH)
        pl.semaphore_wait(barrier, 2)

    @pl.when(section != sender)
    def _():
        pl.semaphore_wait(barrier, 3)
        pl.semaphore_signal(ready, inc=1, device_id=beyond, device_id_type=MESH)


def relay_copy(section, src, dst, send, recv):
    return pltpu.make_async_remote_copy(
        src_ref=src, dst_ref=dst, send_sem=send, recv_sem=recv,
        device_id={"section": 1 - section}, device_id_type=MESH,
    )


def rope_tables(place):
    lane = lax.broadcasted_iota(jnp.int32, (ROWS, 128), 1)
    rows = lax.broadcasted_iota(jnp.int32, (ROWS, 128), 0) + place * ROWS
    frequencies = rope_base ** (-((lane % 32).astype(F32) * 2.0) / HEAD_DIM)
    angles = rows.astype(F32) * frequencies
    return jnp.cos(angles), jnp.sin(angles) * jnp.where(lane % 64 < 32, -1.0, 1.0)


def shards(
    block_input, cotangent, lengths, w_query, w_key, w_value, w_out, w_gate, w_up, w_down, gain_attn, gain_mlp
):
    section = lax.axis_index("section")
    is_first = section == 0
    cosine, signed = rope_tables(lax.axis_index("fsdp"))
    own = pack(w_key[0].T, w_value[0].T, w_query[0], w_out[0], w_gate[0], w_up[0], w_down[0].T)
    gains = jnp.pad(jnp.concatenate([gain_attn, gain_mlp]), ((0, 14), (0, 16)))
    full, gains = gather_weights(own, gains)
    inputs_t = block_input.transpose(0, 2, 1)
    cot_t = cotangent.transpose(0, 2, 1)
    kept, outs = [], []
    hid, n1, q, kv, att, lse = front_first(lengths, inputs_t[0], gains, full, cosine, signed)
    for step in range(2):
        here = (hid, n1, q, kv, lse)
        out_t, mid, n2, gate, up, mixed, compact, hid, n1, q, kv, att, lse = forward(
            step, lengths, att, hid, inputs_t[1], gains, full, cosine, signed
        )
        outs.append(out_t)
        kept.append(here + (mid, n2, gate, up, mixed, compact))
    out_t, n2, mixed, compact, gg, gu, gm, gao, part_two, da, g_out = turn_back(lengths, att, hid, cot_t[1], gains, full)
    outs.append(out_t)
    kept.append((hid, n1, q, kv, lse, None, n2, None, None, mixed, compact))
    layer_out = jnp.where(is_first, jnp.stack(outs[:2]), jnp.stack(outs[1:])).transpose(0, 2, 1)[None]

    grads, parts, terms = [], [], []
    for step in range(3):
        hid, n1, q, kv, lse, _, n2, _, _, mixed, compact = kept[2 - step]
        before = (n1, compact, n2, g_out)
        after = (gao, gg, gu, mixed)
        if step < 2:
            mid, gate, up = (kept[1 - step][i] for i in (5, 7, 8))
            grad_t, packed, part_one, gg, gu, gm, gao, next_two, da, g_out = backward(
                step, lengths, q, kv, lse, da, cosine, signed, hid, gains, full, gm, cot_t[0], mid, gate, up
            )
        else:
            grad_t, packed, part_one = back_last(lengths, q, kv, lse, da, cosine, signed, hid, gains, full, gm)
        grads.append(grad_t)
        parts.append((part_one, part_two))
        part_two = next_two
        terms.append(before + (packed,) + after)
    input_grad = jnp.where(is_first, jnp.stack([grads[2], grads[1]]), jnp.stack([grads[1], grads[0]]))
    input_grad = input_grad.transpose(0, 2, 1)[None]

    sums = [parts[0][i] + parts[1][i] + parts[2][i] for i in range(2)]
    gain_parts = jnp.concatenate([v.reshape(4, 1, 240) for v in sums], axis=1)
    summed, gain_sums = finish(list(zip(*terms)), jnp.pad(gain_parts, ((0, 0), (0, 6), (0, 16))))
    query, key_t, value_t, out, gate, up, down_t = unpack(summed)
    return (
        layer_out,
        input_grad,
        query[None],
        key_t.T[None],
        value_t.T[None],
        out[None],
        gate[None],
        up[None],
        down_t.T[None],
        gain_sums[0:1, :240],
        gain_sums[1:2, :240],
    )


def solution(mesh):
    tokens, two = ("dp", "fsdp"), P("section", "fsdp", None)
    return jax.shard_map(
        shards,
        mesh=mesh,
        in_specs=(P(None, tokens, None), P(None, tokens, None), P("dp", None)) + (two,) * 7 + (P("section", "fsdp"),) * 2,
        out_specs=(P("section", None, tokens, None),) * 2 + (two,) * 7 + (P("section", "fsdp"),) * 2,
        check_vma=False,
    )
```

```python
import functools

import jax
import jax.numpy as jnp
from jax import lax
from jax.experimental import pallas as pl
from jax.experimental.pallas import tpu as pltpu
from jax.sharding import PartitionSpec as P

HEADS = 15
KV_HEADS = 5
GROUP = 3
HEAD_DIM = 64
D = 960
ROWS = 256
STRIP = 640
SEQ = 1024
norm_eps = 1e-05
rope_base = 10000.0
masked_score = -1e30
BF = jnp.bfloat16
F32 = jnp.float32


def dot(a, b):
    return jnp.dot(a, b, preferred_element_type=F32)


def dot_nt(a, b):
    return lax.dot_general(a, b, (((1,), (1,)), ((), ())), preferred_element_type=F32)


def lanes(rows=ROWS):
    return lax.broadcasted_iota(jnp.int32, (rows, 128), 1)


def turn(tile, cosine, signed, low_half):
    partner = jnp.where(low_half, pltpu.roll(tile, 96, 1), pltpu.roll(tile, 32, 1))
    return tile * cosine + partner * signed


def whole(shape):
    return pl.BlockSpec(shape, lambda *_: (0,) * len(shape))


def params(limit=56):
    return pltpu.CompilerParams(vmem_limit_bytes=limit * 2**20)


def linked(collective_id, limit=56):
    return pltpu.CompilerParams(collective_id=collective_id, has_side_effects=True, vmem_limit_bytes=limit * 2**20)


VM = pl.BlockSpec(memory_space=pltpu.VMEM)
HBM = pl.BlockSpec(memory_space=pl.ANY)
SM = pl.BlockSpec(memory_space=pltpu.SMEM)


def shape(dims, kind):
    return jax.ShapeDtypeStruct(dims, kind)


def gain_row(gains, i):
    return jnp.concatenate([gains[f].astype(F32)[i : i + 1, :240] for f in range(4)], axis=1)


class Several:
    def __init__(self, copies):
        self.copies = copies

    def wait(self):
        for copy in self.copies:
            copy.wait()


class Streams:
    def __init__(self, sems):
        self.sems, self.count, self.open = sems, 0, []

    def start(self, src, dst):
        copy = pltpu.make_async_copy(src, dst, self.sems.at[self.count])
        self.count += 1
        copy.start()
        return copy

    def emit(self, src, dst):
        self.open.append(self.start(src, dst))

    def finish(self):
        for copy in self.open:
            copy.wait()


def unpack_body(summed, *refs):
    layer_outs, grads = refs[:3], refs[3:6]
    q, k_t, v_t, out, gate, up, down_t, layer_out, input_grad = refs[6:15]
    raw, gate_s, up_s, down_s, layer_s, grad_s, sems = refs[15:]
    streams = Streams(sems)
    loads = [streams.start(summed.at[m, pl.ds(0, 240)], raw.at[m]) for m in range(4)]
    section = lax.axis_index("section")
    for i in range(2):
        for sources, slot in ((layer_outs, layer_s), (grads, grad_s)):
            first, second = (i, i + 1) if slot is layer_s else (2 - i, 1 - i)
            sem = sems.at[streams.count]
            streams.count += 1
            copies = [pltpu.make_async_copy(sources[k], slot.at[i], sem) for k in (first, second)]
            pl.when(section == 0)(copies[0].start)
            pl.when(section == 1)(copies[1].start)
            loads.append(copies[0])
    for m, slot, place in ((1, gate_s, gate), (2, up_s, up)):
        loads[m].wait()
        slot[...] = raw[m].astype(F32)
        streams.emit(slot, place)
    loads[3].wait()
    for j in range(4):
        down_s[240 * j : 240 * j + 240] = raw[3, :, STRIP * j : STRIP * j + STRIP].astype(F32)
    streams.emit(down_s, down_t)
    for load in loads[4:]:
        load.wait()
    streams.emit(layer_s, layer_out)
    streams.emit(grad_s, input_grad)
    loads[0].wait()
    attn = raw[0].astype(F32)
    keys = attn[:, :STRIP].T
    k_t[...] = keys[:320]
    v_t[...] = keys[320:]
    q[...] = attn[:, STRIP:1600]
    out[...] = attn[:, 1600:]
    streams.finish()


def unpack(summed, layer_outs, grads):
    dims = ((240, D), (320, 240), (320, 240), (240, D), (240, 2560), (240, 2560), (D, STRIP))
    return pl.pallas_call(
        unpack_body,
        out_shape=tuple(shape(s, F32) for s in dims) + (shape((2, D, ROWS), BF), shape((2, D, ROWS), F32)),
        in_specs=[HBM] * 7,
        out_specs=[VM] * 4 + [HBM] * 5,
        scratch_shapes=[
            pltpu.VMEM((4, 240, 2560), BF), pltpu.VMEM((240, 2560), F32), pltpu.VMEM((240, 2560), F32),
            pltpu.VMEM((D, STRIP), F32), pltpu.VMEM((2, D, ROWS), BF), pltpu.VMEM((2, D, ROWS), F32),
            pltpu.SemaphoreType.DMA((13,)),
        ],
        compiler_params=params(),
        name="unpack",
    )(summed, *layer_outs, *grads)


def fill_bias(bias, lens, slot, f):
    key = lax.broadcasted_iota(jnp.int32, (SEQ, ROWS), 0)
    place = lax.broadcasted_iota(jnp.int32, (SEQ, ROWS), 1) + f * ROWS
    one = jnp.where((key <= place) & (key < lens[0, slot]), 0.0, masked_score)
    for r in range(GROUP):
        bias[:, r * ROWS : (r + 1) * ROWS] = one


HEADS_SHAPE = (KV_HEADS, GROUP * ROWS, 128)
KEYS_SHAPE = (KV_HEADS, SEQ, 128)
WIDE, NARROW = (ROWS, 2560), (ROWS, D)


def head_rows(h):
    return slice(h % GROUP * ROWS, (h % GROUP + 1) * ROWS)


def front_part(step, spot, mover, streams, lens, hid, gains, load_w, w, cosine, signed, n1, q, kv, att, lse, bias, outs,
               between=None):
    section = lax.axis_index("section")
    slot = step // 2 if step != 1 else 1 - section
    h = hid[...].astype(F32)
    inverse = lax.rsqrt(jnp.mean(h * h, axis=-1, keepdims=True) + norm_eps)
    n = (h * inverse * gain_row(gains, 0)).astype(BF)
    n1[...] = n
    streams.emit(hid, outs[0])
    streams.emit(n1, outs[1])
    low = lanes() < 64
    half = lax.rem(lanes(), 64) < 32
    cos, sin = cosine[...], signed[...]
    load_w.wait()
    proj = dot(n, w[:, :STRIP])
    tile = [proj[:, 128 * i : 128 * i + 128] for i in range(5)]
    turned = [turn(tile[i], cos, sin, half) for i in range(3)]
    mine = pl.ds(pl.multiple_of(spot.f * ROWS, ROWS), ROWS)
    other = pl.ds(pl.multiple_of(((1 - spot.zl) * 2 + spot.c) * ROWS, ROWS), ROWS)
    across, near, far = [], [], []
    for g in range(KV_HEADS):
        k_tile, v_tile = turned[g // 2], tile[(5 + g) // 2]
        if g % 2 == 0:
            both = jnp.where(low, k_tile, v_tile)
        else:
            both = pltpu.roll(jnp.where(low, v_tile, k_tile), 64, 1)
        kv[g, mine] = both.astype(BF)
        block = kv.at[g, mine]
        across.append(mover.push(block, block, spot.z))
        near.append(mover.push(block, block, spot.core))
    proj = dot(n, w[:, STRIP:])
    for i in range(8):
        t = turn(proj[:, 128 * i : 128 * i + 128], cos, sin, half) * (HEAD_DIM**-0.5)
        for h in (2 * i, 2 * i + 1):
            if h < HEADS:
                part = pltpu.roll(t, 64, 1) if h % 2 else t
                q[h // GROUP, head_rows(h)] = jnp.where(low, part, 0.0).astype(BF)
    streams.emit(q, outs[2])
    fill_bias(bias, lens, slot, spot.f)

    def onward(g):
        across[g].wait_recv()
        block = kv.at[g, other]
        far.append(mover.push(block, block, spot.core))

    onward(0)
    for g in range(KV_HEADS):
        if g + 1 < KV_HEADS:
            onward(g + 1)
        near[g].wait_recv()
        far[g].wait_recv()
        if g + 1 == KV_HEADS:
            streams.emit(kv, outs[3])
        keys = kv[g]
        keys_t = keys.astype(F32).T.astype(BF)
        s = dot_nt(keys, q[g]) + bias[...]
        top = jnp.max(s, axis=0, keepdims=True)
        e = jnp.exp(s - top)
        total = jnp.sum(e, axis=0, keepdims=True)
        att[g] = (dot(keys_t, e.astype(BF)) / total).T.astype(BF)
        log_total = top + jnp.log(total)
        for r in range(GROUP):
            lse[g, r : r + 1] = log_total[:, r * ROWS : (r + 1) * ROWS]
        if between and g in between:
            between[g]()


FRONT_OUTS = (
    shape(NARROW, BF), shape(NARROW, BF), shape(HEADS_SHAPE, BF), shape(KEYS_SHAPE, BF),
    shape(HEADS_SHAPE, BF), shape((KV_HEADS, 8, ROWS), F32),
)
FRONT_SPECS = [HBM] * 4 + [VM] * 2
FRONT_SLOTS = [
    pltpu.VMEM((D, 1664), BF), pltpu.VMEM(NARROW, BF), pltpu.VMEM(NARROW, BF), pltpu.VMEM(HEADS_SHAPE, BF),
    pltpu.VMEM(KEYS_SHAPE, BF), pltpu.VMEM((SEQ, GROUP * ROWS), F32),
]


def front_first_body(lens, own_t, gains, attn_w, ff_in, cosine, signed, ff_w, o_hid, o_n1, o_q, o_kv, att, lse,
                     w, hid, n1, q, kv, bias, sems, send, recv):
    spot = Spot()
    spot.greet()
    streams = Streams(sems)
    load_w = load_columns(streams, attn_w, 0, w)
    mover = Mover(send, recv)
    fz = (1 - spot.zl) * 2 + spot.c
    arrived = []

    def view(part, a, b):
        return ff_w.at[(pl.ds(0, 3), fz) + chunk_at(moved(spot.x, a), part) + (strip_at(moved(spot.y, b)),)]

    def onward(ref):
        arrived.append(mover.push(ref, ref, spot.core))

    sides = [ring_outer(mover, spot, which, (32 * which, 32), view, onward) for which in (0, 1)]

    def progress():
        for side in sides:
            next(side)

    progress()
    hid[...] = jnp.where(lax.axis_index("section") == 0, own_t[0].astype(F32).T, 0.0).astype(BF)
    front_part(0, spot, mover, streams, lens, hid, gains, load_w, w, cosine, signed, n1, q, kv, att, lse, bias,
               (o_hid, o_n1, o_q, o_kv), {2: progress})
    progress()
    for copy in arrived:
        copy.wait_recv()
    mover.finish()
    streams.finish()


def front_first(lens, own_t, gains, attn_w, ff_w, cosine, signed):
    n = 96
    return pl.pallas_call(
        front_first_body,
        out_shape=(shape(ff_w.shape, BF),) + FRONT_OUTS,
        in_specs=[SM, VM, VM, HBM, HBM, VM, VM],
        out_specs=[HBM] + FRONT_SPECS,
        input_output_aliases={4: 0},
        scratch_shapes=FRONT_SLOTS + [pltpu.SemaphoreType.DMA((8,)), pltpu.SemaphoreType.DMA((n,)), pltpu.SemaphoreType.DMA((n,))],
        compiler_params=linked(3),
        name="front_first",
    )(lens, own_t, gains, attn_w, ff_w, cosine, signed)


def load_columns(streams, attn, start, dst):
    size = dst.shape[1]
    return Several([
        streams.start(attn.at[f, pl.ds(0, 240), pl.ds(start, size)], dst.at[pl.ds(240 * f, 240)]) for f in range(4)
    ])


def load_weights(streams, attn, ff, wo, wg, wu, wd, order):
    def load(k):
        if k == "o":
            return load_columns(streams, attn, 1536, wo)
        if k == "d":
            return Several([
                streams.start(
                    ff.at[2, f, pl.ds(0, 240), pl.ds(STRIP * j, STRIP)], wd.at[pl.ds(240 * j, 240), pl.ds(STRIP * f, STRIP)]
                )
                for f in range(4) for j in range(4)
            ])
        m, dst = (0, wg) if k == "g" else (1, wu)
        return Several([streams.start(ff.at[m, f, pl.ds(0, 240)], dst.at[pl.ds(240 * f, 240)]) for f in range(4)])

    return {k: load(k) for k in order}


def rest_part(streams, loads, att, hid, gains, wo, wg, wu, wd, mid_s, n2_s, gate_s, up_s, mixed_s, compact_s, out_s, outs):
    low = lanes() < 64

    def head(h):
        return att[h // GROUP, head_rows(h)].astype(F32)

    for h in range(0, HEADS - 1, 2):
        pair = jnp.where(low, pltpu.roll(head(h), 64, 1), head(h + 1))
        compact_s[:, 64 * h : 64 * h + 128] = pair.astype(BF)
    compact_s[:, 896:960] = pltpu.roll(head(HEADS - 1), 64, 1)[:, :64].astype(BF)
    streams.emit(compact_s, outs[5])
    loads["o"].wait()
    mid = hid[...].astype(F32) + dot(compact_s[...], wo[...])[:, 64:]
    mid_s[...] = mid
    inverse = lax.rsqrt(jnp.mean(mid * mid, axis=-1, keepdims=True) + norm_eps)
    n2_s[...] = (mid * inverse * gain_row(gains, 1)).astype(BF)
    if outs[0] is not None:
        streams.emit(mid_s, outs[0])
    streams.emit(n2_s, outs[1])
    loads["g"].wait()
    loads["u"].wait()
    for i in range(2):
        cols = slice(1280 * i, 1280 * i + 1280)
        n = n2_s[...]
        g = dot(n, wg[:, cols])
        u = dot(n, wu[:, cols])
        gate_s[:, cols] = g.astype(BF)
        up_s[:, cols] = u.astype(BF)
        mixed_s[:, cols] = (g * jax.nn.sigmoid(g) * u).astype(BF)
    if outs[2] is not None:
        streams.emit(gate_s, outs[2])
        streams.emit(up_s, outs[3])
    streams.emit(mixed_s, outs[4])
    loads["d"].wait()
    y = mid_s[...] + dot_nt(mixed_s[...], wd[...])
    out_s[...] = y.astype(BF)
    return y


WEIGHT_SLOTS = [pltpu.VMEM((D, 1024), BF)] + [pltpu.VMEM((D, 2560), BF)] * 3
REST_SLOTS = [
    pltpu.VMEM(NARROW, F32), pltpu.VMEM(NARROW, BF), pltpu.VMEM(WIDE, BF), pltpu.VMEM(WIDE, BF),
    pltpu.VMEM(WIDE, BF), pltpu.VMEM(NARROW, BF), pltpu.VMEM(NARROW, BF),
]


def forward_body(step, lens, att, hid, own_t, gains, attn_w, ff_w, cosine, signed,
                 out_t, o_mid, o_n2, o_gate, o_up, o_mixed, o_compact, o_hid, o_n1, o_q, o_kv, att_next, lse,
                 wo, wg, wu, wd, mid_s, n2_s, gate_s, up_s, mixed_s, compact_s, out_s,
                 w, hid_s, n1, q, kv, bias, passed_on, sems, front_sems, send, recv, ready):
    streams = Streams(sems)
    loads = load_weights(streams, attn_w, ff_w, wo, wg, wu, wd, "ogud")
    load_w = load_columns(streams, attn_w, 0, w)
    spot = Spot()
    section = lax.axis_index("section")
    pair_greet(spot, (section, 0, ready))
    y = rest_part(streams, loads, att, hid, gains, wo, wg, wu, wd, mid_s, n2_s, gate_s, up_s, mixed_s, compact_s, out_s,
                  (o_mid, o_n2, o_gate, o_up, o_mixed, o_compact))

    @pl.when(section == 0)
    def _():
        pl.semaphore_wait(ready, 1)
        relay_copy(section, out_s, passed_on, send.at[15], recv.at[15]).start()
        hid_s[...] = own_t[1].astype(F32).T.astype(BF)

    out_t[...] = y.T.astype(BF)

    @pl.when(section == 1)
    def _():
        relay_copy(section, out_s, passed_on, send.at[15], recv.at[15]).wait_recv()
        hid_s[...] = passed_on[...]

    def attention():
        mover = Mover(send, recv)
        inner = Streams(front_sems)
        front_part(step + 1, spot, mover, inner, lens, hid_s, gains, load_w, w, cosine, signed, n1, q, kv, att_next, lse, bias,
                   (o_hid, o_n1, o_q, o_kv))
        mover.finish()
        inner.finish()

    if step == 0:
        attention()
    else:
        pl.when(section == 1)(attention)

        @pl.when(section == 0)
        def _():
            inner = Streams(front_sems)
            load_w.wait()
            for slot, place in ((hid_s, o_hid), (n1, o_n1), (q, o_q), (kv, o_kv)):
                slot[...] = jnp.zeros(slot.shape, slot.dtype)
                inner.emit(slot, place)
            att_next[...] = jnp.zeros(att_next.shape, BF)
            lse[...] = jnp.zeros(lse.shape, F32)
            inner.finish()

    @pl.when(section == 0)
    def _():
        relay_copy(section, out_s, passed_on, send.at[15], recv.at[15]).wait_send()

    streams.finish()


def forward(step, lens, att, hid, own_t, gains, attn_w, ff_w, cosine, signed):
    rest_outs = (shape((D, ROWS), BF), shape(NARROW, F32), shape(NARROW, BF)) + (shape(WIDE, BF),) * 3 + (shape(NARROW, BF),)
    return pl.pallas_call(
        functools.partial(forward_body, step),
        out_shape=rest_outs + FRONT_OUTS,
        in_specs=[SM, VM, VM, VM, VM, HBM, HBM, VM, VM],
        out_specs=[VM] + [HBM] * 6 + FRONT_SPECS,
        scratch_shapes=WEIGHT_SLOTS + REST_SLOTS + FRONT_SLOTS + [
            pltpu.VMEM(NARROW, BF), pltpu.SemaphoreType.DMA((42,)), pltpu.SemaphoreType.DMA((4,)), pltpu.SemaphoreType.DMA((16,)),
            pltpu.SemaphoreType.DMA((16,)), pltpu.SemaphoreType.REGULAR,
        ],
        compiler_params=linked(4 + step, 60),
        name="forward",
    )(lens, att, hid, own_t, gains, attn_w, ff_w, cosine, signed)


def back_rest_part(streams, loads, g_out, gains, mid_ref, gate_s, up_s, gg_s, gu_s, gm_s, wo, wg, wu, wd, gao_out, part, da, outs):
    loads["d"].wait()
    for i in range(2):
        cols = slice(1280 * i, 1280 * i + 1280)
        grad_mixed = dot(g_out[...], wd[:, cols])
        ga = gate_s[:, cols].astype(F32)
        sg = jax.nn.sigmoid(ga)
        scaled = grad_mixed * sg
        gg_s[:, cols] = (scaled * up_s[:, cols].astype(F32) * (1.0 + ga * (1.0 - sg))).astype(BF)
        gu_s[:, cols] = (scaled * ga).astype(BF)
    streams.emit(gg_s, outs[0])
    streams.emit(gu_s, outs[1])
    loads["g"].wait()
    loads["u"].wait()
    grad_normed = dot_nt(gg_s[...], wg[...]) + dot_nt(gu_s[...], wu[...])
    mid = mid_ref[...]
    inverse = lax.rsqrt(jnp.mean(mid * mid, axis=-1, keepdims=True) + norm_eps)
    unit = mid * inverse
    part[...] = jnp.sum(grad_normed * unit, axis=0, keepdims=True)
    scaled_two = grad_normed * gain_row(gains, 1)
    gm = g_out[...].astype(F32) + inverse * (
        scaled_two - unit * jnp.mean(scaled_two * unit, axis=-1, keepdims=True)
    )
    gm_s[...] = gm
    streams.emit(gm_s, outs[2])
    gao_out[...] = gm.astype(BF)
    shifted = jnp.concatenate([jnp.zeros((ROWS, 64), F32), gm], axis=1).astype(BF)
    loads["o"].wait()
    att = jnp.concatenate([dot_nt(shifted, wo[...]), jnp.zeros((ROWS, 64), F32)], axis=1)
    low = lanes() < 64
    for h in range(HEADS):
        tile = att[:, 128 * (h // 2) : 128 * (h // 2) + 128]
        if h % 2 == 0:
            tile = pltpu.roll(tile, 64, 1)
        da[h // GROUP, head_rows(h)] = jnp.where(low, 0.0, tile).astype(BF)


def live_cotangent(step, lens, cot_t):
    place = lax.broadcasted_iota(jnp.int32, (D, ROWS), 1) + lax.axis_index("fsdp") * ROWS
    return jnp.where(place < lens[0, 1 - step], cot_t[1 - step].astype(F32), 0.0).T.astype(BF)


BACK_OUTS = (
    shape(WIDE, BF), shape(WIDE, BF), shape(NARROW, F32), shape(NARROW, BF), shape((1, D), F32),
    shape(HEADS_SHAPE, BF), shape(NARROW, BF),
)
BACK_SPECS = [HBM] * 3 + [VM] * 4


def turn_back_body(lens, att, hid, cot_t, gains, attn_w, ff_w,
                   out_t, o_n2, o_mixed, o_compact, o_gg, o_gu, o_gm, gao, part, da, g_out,
                   wo, wg, wu, wd, mid_s, n2_s, gate_s, up_s, mixed_s, compact_s, out_s, gg_s, gu_s, gm_s, sems):
    streams = Streams(sems)
    loads = load_weights(streams, attn_w, ff_w, wo, wg, wu, wd, "ogud")
    y = rest_part(streams, loads, att, hid, gains, wo, wg, wu, wd, mid_s, n2_s, gate_s, up_s, mixed_s, compact_s, out_s,
                  (None, o_n2, None, None, o_mixed, o_compact))
    out_t[...] = y.T.astype(BF)
    g_out[...] = jnp.where(lax.axis_index("section") == 1, live_cotangent(0, lens, cot_t), 0.0).astype(BF)

    class Done:
        def wait(self):
            pass

    back_rest_part(streams, {k: Done() for k in "ogud"}, g_out, gains, mid_s, gate_s, up_s, gg_s, gu_s, gm_s,
                   wo, wg, wu, wd, gao, part, da, (o_gg, o_gu, o_gm))
    streams.finish()


def turn_back(lens, att, hid, cot_t, gains, attn_w, ff_w):
    return pl.pallas_call(
        turn_back_body,
        out_shape=(shape((D, ROWS), BF), shape(NARROW, BF), shape(WIDE, BF), shape(NARROW, BF)) + BACK_OUTS,
        in_specs=[SM, VM, VM, VM, VM, HBM, HBM],
        out_specs=[VM] + [HBM] * 3 + BACK_SPECS,
        scratch_shapes=WEIGHT_SLOTS + REST_SLOTS + [
            pltpu.VMEM(WIDE, BF), pltpu.VMEM(WIDE, BF), pltpu.VMEM(NARROW, F32), pltpu.SemaphoreType.DMA((36,)),
        ],
        compiler_params=params(60),
        name="turn_back",
    )(lens, att, hid, cot_t, gains, attn_w, ff_w)


def back_attend_part(step, spot, mover, lens, q, kv, lse, da, cosine, signed, hid, gains, load_w, w, gm, packed, gain_part,
                     bias, part, near, passed, far, own, dq, between=None):
    section = lax.axis_index("section")
    slot = 1 - section if step == 1 else 1 - step // 2
    fill_bias(bias, lens, slot, spot.f)
    low = lanes() < 64
    half = lax.rem(lanes(), 64) < 32
    cos, sin = cosine[...], -signed[...]

    def rows_of(zl, c):
        return pl.ds(pl.multiple_of((zl * 2 + c) * ROWS, ROWS), ROWS)

    there, here = 1 - spot.zl, spot.zl
    core, across = {}, {}

    def stage_one(g):
        core[g][0].wait_recv()
        passed[g] = (part[g, rows_of(there, spot.c)].astype(F32) + near[g, 0].astype(F32)).astype(BF)
        across[g] = mover.push(passed.at[g], far.at[g], spot.z)
        core[g][1].wait_recv()
        own[g] = part[g, rows_of(here, spot.c)].astype(F32) + near[g, 1].astype(F32)

    def stage_two(g):
        across[g].wait_recv()
        own[g] = own[g] + far[g].astype(F32)

    for g in range(KV_HEADS):
        keys = kv[g]
        keys_t = keys.astype(F32).T.astype(BF)
        logs = jnp.concatenate([lse[g, r : r + 1] for r in range(GROUP)], axis=1)
        p = jnp.exp(dot_nt(keys, q[g]) + bias[...] - logs)
        dp = dot_nt(keys, da[g])
        delta = jnp.sum(p * dp, axis=0, keepdims=True)
        ds = (p * (dp - delta)).astype(BF)
        part[g] = (dot(ds, q[g]) + dot(p.astype(BF), da[g])).astype(BF)
        core[g] = (
            mover.push(part.at[g, rows_of(there, 1 - spot.c)], near.at[g, 0], spot.core),
            mover.push(part.at[g, rows_of(here, 1 - spot.c)], near.at[g, 1], spot.core),
        )
        grad_q = (dot(keys_t, ds) * (HEAD_DIM**-0.5)).T
        for r in range(GROUP):
            rows = slice(r * ROWS, (r + 1) * ROWS)
            dq[g, rows] = turn(grad_q[rows], cos, sin, half).astype(BF)
        if g > 0:
            stage_one(g - 1)
        if g > 1:
            stage_two(g - 2)
        if between and g in between:
            between[g]()

    def merged(left, right):
        return jnp.where(low, left, right)

    def flip(v):
        return pltpu.roll(v, 64, 1)

    def head(h):
        return dq[h // GROUP, head_rows(h)].astype(F32)

    for h in range(0, HEADS, 2):
        tile = merged(head(h), flip(head(h + 1)) if h + 1 < HEADS else 0.0)
        packed[:, STRIP + 64 * h : STRIP + 64 * h + 128] = tile.astype(BF)
    stage_one(KV_HEADS - 1)
    load_w.wait()
    grad_normed = dot_nt(packed[:, STRIP:], w[:, STRIP:])
    hidden = hid[...].astype(F32)
    inverse = lax.rsqrt(jnp.mean(hidden * hidden, axis=-1, keepdims=True) + norm_eps)
    unit = hidden * inverse
    stage_two(KV_HEADS - 2)
    stage_two(KV_HEADS - 1)
    both = [own[g] for g in range(KV_HEADS)]
    turned = [turn(b, cos, sin, half) for b in both]
    tiles = [
        merged(turned[0], flip(turned[1])),
        merged(turned[2], flip(turned[3])),
        merged(turned[4], both[0]),
        merged(flip(both[1]), both[2]),
        merged(flip(both[3]), both[4]),
    ]
    for i, tile in enumerate(tiles):
        packed[:, 128 * i : 128 * i + 128] = tile.astype(BF)
    grad_normed = grad_normed + dot_nt(packed[:, :STRIP], w[:, :STRIP])
    gain_part[...] = jnp.sum(grad_normed * unit, axis=0, keepdims=True)
    scaled = grad_normed * gain_row(gains, 0)
    return gm[...] + inverse * (scaled - unit * jnp.mean(scaled * unit, axis=-1, keepdims=True))


OWN_SHAPE = (KV_HEADS, ROWS, 128)
ATTEND_SLOTS = [
    pltpu.VMEM((SEQ, GROUP * ROWS), F32), pltpu.VMEM(KEYS_SHAPE, BF), pltpu.VMEM((KV_HEADS, 2, ROWS, 128), BF),
    pltpu.VMEM(OWN_SHAPE, BF), pltpu.VMEM(OWN_SHAPE, BF), pltpu.VMEM(OWN_SHAPE, F32), pltpu.VMEM(HEADS_SHAPE, BF),
    pltpu.VMEM((D, 1664), BF),
]
ATTEND_OUTS = (shape((D, ROWS), F32), shape((ROWS, 1664), BF), shape((1, D), F32))


def backward_body(step, lens, q, kv, lse, da, cosine, signed, hid, gains, attn_w, ff_w, gm, cot_t, mid, gate, up,
                  grad_t, packed, gain_part, o_gg, o_gu, o_gm, gao, part_two, da_next, g_out,
                  bias, part, near, passed, far, own, dq, w, wo, wg, wu, wd, gate_s, up_s, gg_s, gu_s, gm_s,
                  out_s, passed_on, sems, send, recv, ready):
    streams = Streams(sems)
    load_w = load_columns(streams, attn_w, 0, w)
    loads = load_weights(streams, attn_w, ff_w, wo, wg, wu, wd, "dguo")
    load_gate = streams.start(gate, gate_s)
    load_up = streams.start(up, up_s)
    spot = Spot()
    section = lax.axis_index("section")
    pair_greet(spot, (section, 1, ready))
    mover = Mover(send, recv)
    grad_in = back_attend_part(step, spot, mover, lens, q, kv, lse, da, cosine, signed, hid, gains, load_w, w, gm,
                               packed, gain_part, bias, part, near, passed, far, own, dq)
    out_s[...] = grad_in.astype(BF)

    @pl.when(section == 1)
    def _():
        pl.semaphore_wait(ready, 1)
        relay_copy(section, out_s, passed_on, send.at[15], recv.at[15]).start()
        if step == 0:
            g_out[...] = live_cotangent(1, lens, cot_t)
        else:
            g_out[...] = jnp.zeros(NARROW, BF)

    grad_t[...] = grad_in.T

    @pl.when(section == 0)
    def _():
        relay_copy(section, out_s, passed_on, send.at[15], recv.at[15]).wait_recv()
        g_out[...] = passed_on[...]

    load_gate.wait()
    load_up.wait()
    back_rest_part(streams, loads, g_out, gains, mid, gate_s, up_s, gg_s, gu_s, gm_s, wo, wg, wu, wd, gao, part_two, da_next,
                   (o_gg, o_gu, o_gm))
    mover.finish()

    @pl.when(section == 1)
    def _():
        relay_copy(section, out_s, passed_on, send.at[15], recv.at[15]).wait_send()

    streams.finish()


def backward(step, lens, q, kv, lse, da, cosine, signed, hid, gains, attn_w, ff_w, gm, cot_t, mid, gate, up):
    return pl.pallas_call(
        functools.partial(backward_body, step),
        out_shape=ATTEND_OUTS + BACK_OUTS,
        in_specs=[SM] + [VM] * 8 + [HBM, HBM, VM, VM, VM, HBM, HBM],
        out_specs=[VM] * 3 + BACK_SPECS,
        scratch_shapes=ATTEND_SLOTS + WEIGHT_SLOTS + [pltpu.VMEM(WIDE, BF)] * 4 + [
            pltpu.VMEM(NARROW, F32), pltpu.VMEM(NARROW, BF), pltpu.VMEM(NARROW, BF), pltpu.SemaphoreType.DMA((40,)),
            pltpu.SemaphoreType.DMA((16,)), pltpu.SemaphoreType.DMA((16,)), pltpu.SemaphoreType.REGULAR,
        ],
        compiler_params=linked(6 + step, 62),
        name="backward",
    )(lens, q, kv, lse, da, cosine, signed, hid, gains, attn_w, ff_w, gm, cot_t, mid, gate, up)


MESH = pl.DeviceIdType.MESH
SIDE = 4
OFFSETS = (1, 3, 2)
HALVES = ((0, 128), (128, 112))


class Spot:
    def __init__(self):
        d = lax.axis_index("dp")
        f = lax.axis_index("fsdp")
        self.x, self.y = d // SIDE, lax.rem(d, SIDE)
        self.zl, self.c = f // 2, lax.rem(f, 2)
        self.f = f
        self.core = {"fsdp": self.zl * 2 + 1 - self.c}
        self.z = {"fsdp": (1 - self.zl) * 2 + self.c}
        self.across = {"fsdp": (1 - self.zl) * 2 + 1 - self.c}

    def along_x(self, k):
        return {"dp": lax.rem(self.x + k, SIDE) * SIDE + self.y}

    def along_y(self, k):
        return {"dp": self.x * SIDE + lax.rem(self.y + k, SIDE)}

    def greet(self):
        self.call()
        self.hear()

    def call(self):
        barrier = pltpu.get_barrier_semaphore()
        ids = [self.core, self.z, self.across]
        for k in range(1, SIDE):
            ids += [self.along_x(k), self.along_y(k)]
        for who in ids:
            pl.semaphore_signal(barrier, inc=1, device_id=who, device_id_type=MESH)

    def hear(self):
        pl.semaphore_wait(pltpu.get_barrier_semaphore(), 9)


class Mover:
    def __init__(self, send, recv):
        self.send, self.recv, self.pending, self.count = send, recv, [], 0

    def push(self, src, dst, who):
        i = self.count
        self.count += 1
        copy = pltpu.make_async_remote_copy(
            src_ref=src, dst_ref=dst, send_sem=self.send.at[i], recv_sem=self.recv.at[i],
            device_id=who, device_id_type=MESH,
        )
        copy.start()
        self.pending.append(copy)
        return copy

    def finish(self):
        for copy in self.pending:
            copy.wait_send()


def ring_axes(spot, which, view):
    if which == 0:
        return spot.along_x, spot.along_y, view
    return spot.along_y, spot.along_x, lambda part, a, b: view(part, b, a)


def ring_inner(mover, spot, which, rows, view):
    inner, outer, at = ring_axes(spot, which, view)
    lo, size = rows
    both, one, two = rows, (lo, size // 2), (lo + size // 2, size // 2)
    own = at(both, 0, 0)
    near = [mover.push(own, own, inner(k)) for k in (1, 3)]
    yield
    for copy in near:
        copy.wait_recv()
    far = [mover.push(at(one, 3, 0), at(one, 3, 0), inner(1)), mover.push(at(two, 1, 0), at(two, 1, 0), inner(3))]
    yield
    for copy in far:
        copy.wait_recv()
    yield


def ring_outer(mover, spot, which, rows, view, onward):
    inner, outer, at = ring_axes(spot, which, view)
    lo, size = rows
    both, one, two = rows, (lo, size // 2), (lo + size // 2, size // 2)
    line = at(both, None, 0)
    near = [mover.push(line, line, outer(k)) for k in (1, 3)]
    onward(line)
    yield
    for copy in near:
        copy.wait_recv()
    far = [mover.push(at(one, None, 3), at(one, None, 3), outer(1)), mover.push(at(two, None, 1), at(two, None, 1), outer(3))]
    onward(at(both, None, 3))
    onward(at(both, None, 1))
    yield
    for copy in far:
        copy.wait_recv()
    onward(at(both, None, 2))
    yield


def chunk_at(p, part):
    return pl.ds(0, 4) if p is None else pl.ds(lax.rem(p, SIDE), 1), pl.ds(*part)


def strip_at(p):
    return pl.ds(0, 2560) if p is None else pl.ds(pl.multiple_of(lax.rem(p, SIDE) * STRIP, 128), STRIP)


def moved(p, a):
    return None if a is None else p + a


def chunk_rows(p, lo=0, size=64):
    return pl.ds(pl.multiple_of(lax.rem(p, SIDE) * 64 + lo, 16), size)


def strip_cols(p):
    return pl.ds(pl.multiple_of(lax.rem(p, SIDE) * STRIP, 128), STRIP)


def first_body(k_t, v_t, wq, wo, gain_a, gain_b, gate, up, down_t, attn_full, ff_full, gains_full,
               own, ff, gains, sems, send, recv):
    streams = Streams(sems)
    loads = [
        streams.start(gate, ff.at[0, pl.ds(0, 240)]),
        streams.start(up, ff.at[1, pl.ds(0, 240)]),
    ]
    for j in range(4):
        loads.append(streams.start(down_t.at[pl.ds(240 * j, 240)], ff.at[2, pl.ds(0, 240), pl.ds(STRIP * j, STRIP)]))
    spot = Spot()
    x, y, f = spot.x, spot.y, spot.f
    fz = (1 - spot.zl) * 2 + spot.c
    spot.call()
    keys = jnp.concatenate([k_t[...].astype(F32), v_t[...].astype(F32)], axis=0).T
    both = jnp.concatenate([wq[...].astype(F32), wo[...].astype(F32)], axis=1)
    for i in range(4):
        size = 64 if i < 3 else 48
        own[i, :size, :STRIP] = keys[64 * i : 64 * i + size].astype(BF)
        own[i, :size, STRIP:] = both[64 * i : 64 * i + size].astype(BF)
    own[3, 48:64] = jnp.zeros((16, 2560), BF)
    ff[:, pl.ds(240, 16)] = jnp.zeros((3, 16, 2560), BF)
    gains[...] = jnp.zeros((8, 256), F32)
    gains[0:1, 0:240] = gain_a[...].astype(F32)
    gains[1:2, 0:240] = gain_b[...].astype(F32)
    spot.hear()
    mover = Mover(send, recv)
    here = chunk_at(x, (0, 64)) + (strip_at(y),)
    first = mover.push(own.at[here], attn_full.at[(f,) + here], spot.z)
    waits = [mover.push(gains, gains_full.at[f], {"fsdp": lax.rem(f + k, 4)}) for k in range(1, 4)]
    waits.append(mover.push(own, attn_full.at[f], spot.core))
    streams.emit(own, attn_full.at[f])
    gains_full[f] = gains[...]

    def view(part, a, b):
        return attn_full.at[(fz,) + chunk_at(moved(x, a), part) + (strip_at(moved(y, b)),)]

    def onward(ref):
        waits.append(mover.push(ref, ref, spot.core))

    def ff_view(part, a, b):
        return ff_full.at[(pl.ds(0, 3), fz) + chunk_at(moved(x, a), part) + (strip_at(moved(y, b)),)]

    parts = (0, (0, 32)), (1, (32, 32))
    sides = [ring_inner(mover, spot, *part, view) for part in parts]
    first.wait_recv()
    for side in sides:
        next(side)
    for load in loads:
        load.wait()
    block = (pl.ds(0, 3), chunk_rows(x), strip_at(y))
    there = (pl.ds(0, 3), f, lax.rem(x, SIDE), pl.ds(0, 64), strip_at(y))
    second = mover.push(ff.at[block], ff_full.at[there], spot.z)
    for i in range(4):
        waits.append(mover.push(ff.at[:, pl.ds(64 * i, 64)], ff_full.at[:, f, i], spot.core))
        streams.emit(ff.at[:, pl.ds(64 * i, 64)], ff_full.at[:, f, i])
    for _ in range(2):
        for side in sides:
            next(side)
    sides = [ring_outer(mover, spot, *part, view, onward) for part in parts]
    for side in sides:
        next(side)
    second.wait_recv()
    ff_sides = [ring_inner(mover, spot, *part, ff_view) for part in parts]
    for _ in range(2):
        for side in ff_sides:
            next(side)
        for side in sides:
            next(side)
    for side in ff_sides:
        next(side)
    for copy in waits:
        copy.wait_recv()
    mover.finish()
    streams.finish()


def first_weights(*weights):
    n = 96
    return pl.pallas_call(
        first_body,
        out_shape=(shape((4, 4, 64, 2560), BF), shape((3, 4, 4, 64, 2560), BF), shape((4, 8, 256), F32)),
        in_specs=[VM] * 6 + [HBM] * 3,
        out_specs=[HBM, HBM, VM],
        scratch_shapes=[
            pltpu.VMEM((4, 64, 2560), BF), pltpu.VMEM((3, 256, 2560), BF), pltpu.VMEM((8, 256), F32),
            pltpu.SemaphoreType.DMA((12,)), pltpu.SemaphoreType.DMA((n,)), pltpu.SemaphoreType.DMA((n,)),
        ],
        compiler_params=linked(1),
        name="first_weights",
    )(*weights)


STEP = 16


def add_rows(out, rows, terms):
    def body(i, carry):
        sl = pl.ds(pl.multiple_of(i * STEP, STEP), STEP)
        total = terms[0](sl).astype(F32)
        for term in terms[1:]:
            total = total + term(sl).astype(F32)
        out(sl, total.astype(BF))
        return carry

    lax.fori_loop(0, rows // STEP, body, 0)


def dot_tn(a, b):
    return lax.dot_general(a, b, (((0,), (0,)), ((), ())), preferred_element_type=F32)


class Sums:
    def __init__(self, spot, mover, **slots):
        self.spot, self.mover, self.flights = spot, mover, {}
        self.__dict__.update(slots)

    def land(self, *key):
        for copy in self.flights[key]:
            copy.wait_recv()

    def chunk(self, k, lo=0, size=64):
        return chunk_rows(self.spot.x + k, lo, size)

    def strip(self, k):
        return strip_cols(self.spot.y + k)

    def to_core(self, m):
        spot, push = self.spot, self.mover.push
        pa, pb = spot.zl * 2 + 1 - spot.c, (1 - spot.zl) * 2 + 1 - spot.c
        self.flights["core", m] = (
            push(self.stage.at[pa], self.own.at[m, 0], spot.core), push(self.stage.at[pb], self.own.at[m, 1], spot.core)
        )

    def core_sent(self, m):
        for copy in self.flights["core", m]:
            copy.wait_send()
            self.mover.pending = [item for item in self.mover.pending if item is not copy]

    def one(self, m):
        self.land("core", m)
        spot, push, own = self.spot, self.mover.push, self.own
        for i, f in enumerate((spot.zl * 2 + spot.c, (1 - spot.zl) * 2 + spot.c)):
            def put(sl, v, i=i):
                own[m, i, sl] = v
            add_rows(put, 256, [lambda sl, i=i: own[m, i, sl], lambda sl, f=f: self.stage[f, sl]])
        self.flights["half", m] = (
            push(own.at[m, 0, self.chunk(2, 0, 32)], self.hx.at[0, m], spot.along_x(1)),
            push(own.at[m, 0, self.chunk(2, 32, 32)], self.hx.at[1, m], spot.along_x(3)),
            push(own.at[m, 1, pl.ds(0, 128), self.strip(2)], self.hy.at[0, m], spot.along_y(1)),
            push(own.at[m, 1, pl.ds(128, 128), self.strip(2)], self.hy.at[1, m], spot.along_y(3)),
        )

    def two(self, m):
        self.land("half", m)
        spot, own = self.spot, self.own
        for i, k in ((0, 1), (1, 3)):
            base = lax.rem(spot.x + k, SIDE) * 64 + 32 * i

            def rows(sl, base=base):
                return pl.ds(pl.multiple_of(base + sl.start, 16), STEP)

            def put(sl, v, rows=rows):
                own[m, 0, rows(sl)] = v
            add_rows(put, 32, [lambda sl, rows=rows: own[m, 0, rows(sl)], lambda sl, i=i: self.hx[i, m, sl]])

            def low(sl, i=i):
                return pl.ds(pl.multiple_of(128 * i + sl.start, 16), STEP)

            def put(sl, v, low=low, k=k):
                own[m, 1, low(sl), self.strip(k)] = v
            add_rows(put, 128, [lambda sl, low=low, k=k: own[m, 1, low(sl), self.strip(k)], lambda sl, i=i: self.hy[i, m, sl]])

    def next(self, m):
        spot, push, own = self.spot, self.mover.push, self.own
        self.flights["next", m] = tuple(
            copy
            for i, k in ((0, 1), (1, 3))
            for copy in (
                push(own.at[m, 0, self.chunk(k)], self.rx.at[i, m], spot.along_x(k)),
                push(own.at[m, 1, :, self.strip(k)], self.ry.at[i, m], spot.along_y(k)),
            )
        )

    def three(self, m, ta, tb):
        self.land("next", m)
        own, base = self.own, self.spot.x * 64

        def put(sl, v):
            ta[sl] = v
        first = lambda sl: own[m, 0, pl.ds(pl.multiple_of(base + sl.start, 16), STEP)]
        add_rows(put, 64, [first, lambda sl: self.rx[0, m, sl], lambda sl: self.rx[1, m, sl]])

        def put(sl, v):
            tb[sl] = v
        add_rows(put, 256, [lambda sl: own[m, 1, sl, self.strip(0)], lambda sl: self.ry[0, m, sl], lambda sl: self.ry[1, m, sl]])

    def cross(self, m):
        spot, push = self.spot, self.mover.push
        self.flights["second", m] = tuple(
            copy
            for i, k in enumerate(OFFSETS)
            for copy in (
                push(self.ta.at[m, :, self.strip(k)], self.ry2.at[i, m], spot.along_y(k)),
                push(self.tb.at[m, self.chunk(k)], self.rx2.at[i, m], spot.along_x(k)),
            )
        )

    def four(self, m):
        self.land("second", m)
        ta, tb, ua, ub, base = self.ta, self.tb, self.ua, self.ub, self.spot.x * 64

        def put(sl, v):
            ub[m, sl] = v
        first = lambda sl: tb[m, pl.ds(pl.multiple_of(base + sl.start, 16), STEP)]
        add_rows(put, 64, [first] + [lambda sl, i=i: self.rx2[i, m, sl] for i in range(3)])
        self.flights["z", m] = (self.mover.push(ub.at[m], self.rz.at[m], self.spot.z),)

        def put(sl, v):
            ua[m, sl] = v
        add_rows(put, 64, [lambda sl: ta[m, sl, self.strip(0)]] + [lambda sl, i=i: self.ry2[i, m, sl] for i in range(3)])

    def five(self, m):
        self.land("z", m)
        ua = self.ua

        def put(sl, v):
            ua[m, sl] = v
        add_rows(put, 64, [lambda sl: ua[m, sl], lambda sl: self.rz[m, sl]])


class Live:
    def __init__(self, sems):
        self.sems, self.count = sems, 0

    def load(self, trio, dst):
        i = self.count
        self.count += 2
        section = lax.axis_index("section")
        fixed = pltpu.make_async_copy(trio[1], dst.at[pl.ds(ROWS, ROWS)], self.sems.at[i])
        fixed.start()
        early = pltpu.make_async_copy(trio[0], dst.at[pl.ds(0, ROWS)], self.sems.at[i + 1])
        late = pltpu.make_async_copy(trio[2], dst.at[pl.ds(0, ROWS)], self.sems.at[i + 1])
        pl.when(section == 1)(early.start)
        pl.when(section == 0)(late.start)

        def wait():
            fixed.wait()
            pl.when(section == 1)(early.wait)
            pl.when(section == 0)(late.wait)

        return wait


def wide_gradient(stage, tall, left, right):
    for i in range(2):
        v = dot_tn(left[...], right[:, pl.ds(1280 * i, 1280)])
        for f in range(4):
            if not tall:
                stage[f, pl.ds(0, 240), pl.ds(1280 * i, 1280)] = v[240 * f : 240 * f + 240].astype(BF)
            elif f // 2 == i:
                for j in range(4):
                    cols = slice(STRIP * (f % 2), STRIP * (f % 2) + STRIP)
                    stage[f, pl.ds(0, 240), pl.ds(STRIP * j, STRIP)] = v[240 * j : 240 * j + 240, cols].astype(BF)


def back_last_body(lens, q, kv, lse, da, cosine, signed, hid, gains, attn_w, gm, *refs):
    gd, mixed, n2, gu, gg = (refs[3 * i : 3 * i + 3] for i in range(5))
    (grad_t, packed, gain_part, ta_out, tb_out, own_out, bias, part, near, passed, far, own_keys, dq, w,
     stage, own, hx, hy, rx, ry, ta, tb, left, right, sems, live_sems, send, recv) = refs[15:]
    spot = Spot()
    spot.call()
    streams = Streams(sems)
    live = Live(live_sems)
    waits = {0: [live.load(gd, left.at[0]), live.load(mixed, right.at[0])]}
    load_w = load_columns(streams, attn_w, 0, w)
    waits[1] = [live.load(n2, left.at[1]), live.load(gu, right.at[1])]
    stage[:, pl.ds(240, 16)] = jnp.zeros((4, 16, 2560), BF)
    spot.hear()
    mover = Mover(send, recv)
    sums = Sums(spot, mover, stage=stage, own=own, hx=hx, hy=hy, rx=rx, ry=ry)

    def compute(k):
        for wait in waits[k]:
            wait()
        wide_gradient(stage, k == 0, left.at[min(k, 1)], right.at[k % 2])
        if k == 0:
            waits[2] = [live.load(gg, right.at[0])]
        sums.to_core(k)

    def three(k):
        sums.three(k, ta.at[k], tb.at[k])
        streams.emit(ta.at[k], ta_out.at[k])
        streams.emit(tb.at[k], tb_out.at[k])

    def after_one():
        sums.one(0)
        sums.core_sent(0)
        compute(1)

    def after_two():
        sums.one(1)
        sums.two(0)
        sums.next(0)
        sums.core_sent(1)
        compute(2)

    def after_three():
        sums.one(2)
        sums.two(1)
        sums.next(1)

    def after_four():
        three(0)

    compute(0)
    grad_in = back_attend_part(2, spot, mover, lens, q, kv, lse, da, cosine, signed, hid, gains, load_w, w, gm,
                               packed, gain_part, bias, part, near, passed, far, own_keys, dq,
                               {1: after_one, 2: after_two, 3: after_three, 4: after_four})
    sums.two(2)
    streams.emit(own.at[2], own_out)
    grad_t[...] = grad_in.T
    three(1)
    mover.finish()
    streams.finish()


def back_last(lens, q, kv, lse, da, cosine, signed, hid, gains, attn_w, gm, sets):
    vm, n = pltpu.VMEM, 64
    return pl.pallas_call(
        back_last_body,
        out_shape=ATTEND_OUTS + (shape((2, 64, 2560), BF), shape((2, 256, STRIP), BF), shape((2, 256, 2560), BF)),
        in_specs=[SM] + [VM] * 8 + [HBM, VM] + [HBM] * 15,
        out_specs=[VM] * 3 + [HBM] * 3,
        scratch_shapes=ATTEND_SLOTS + [
            vm((4, 256, 2560), BF), vm((3, 2, 256, 2560), BF), vm((2, 3, 32, 2560), BF), vm((2, 3, 128, STRIP), BF),
            vm((2, 2, 64, 2560), BF), vm((2, 2, 256, STRIP), BF), vm((2, 64, 2560), BF), vm((2, 256, STRIP), BF),
            vm((2, 2 * ROWS, D), BF), vm((2, 2 * ROWS, 2560), BF),
            pltpu.SemaphoreType.DMA((10,)), pltpu.SemaphoreType.DMA((10,)), pltpu.SemaphoreType.DMA((n,)), pltpu.SemaphoreType.DMA((n,)),
        ],
        compiler_params=linked(8, 63),
        name="back_last",
    )(lens, q, kv, lse, da, cosine, signed, hid, gains, attn_w, gm, *[a for trio in sets for a in trio])


def finish_body(*refs):
    n1, att, packed, gao = (refs[3 * i : 3 * i + 3] for i in range(4))
    ta_in, tb_in, own_in = refs[12:15]
    parts = refs[15:21]
    (out, gains_out, gains, stage, own, left, left_b, right_p, right_q, hx, hy, rx, ry, ta, tb, rx2, ry2,
     ua, ub, rz, g_core, g_mine, g_x, g_y, send, recv, local, live_sems) = refs[21:]
    spot = Spot()
    spot.call()
    x, y = spot.x, spot.y
    live = Live(live_sems)
    brought = [pltpu.make_async_copy(own_in, own.at[1], local.at[2])]
    for k in range(2):
        brought.append(pltpu.make_async_copy(ta_in.at[k], ta.at[3 - k], local.at[3 + 2 * k]))
        brought.append(pltpu.make_async_copy(tb_in.at[k], tb.at[3 - k], local.at[4 + 2 * k]))
    for copy in brought:
        copy.start()
    waits = [live.load(n1, left), live.load(packed, right_p), live.load(att, left_b), live.load(gao, right_q)]
    stage[:, pl.ds(240, 16)] = jnp.zeros((4, 16, 2560), BF)
    gains[...] = jnp.zeros((4, 8, 256), F32)
    for i in range(2):
        total = parts[i][...] + parts[2 + i][...] + parts[4 + i][...]
        for f in range(4):
            gains[f, i : i + 1, 0:240] = total[:, 240 * f : 240 * f + 240]
    spot.hear()
    mover = Mover(send, recv)
    sums = Sums(spot, mover, stage=stage, own=own, hx=hx, hy=hy, rx=rx, ry=ry, ta=ta, tb=tb, rx2=rx2, ry2=ry2, ua=ua, ub=ub, rz=rz)
    pa, pb = spot.zl * 2 + 1 - spot.c, (1 - spot.zl) * 2 + 1 - spot.c
    small = [mover.push(gains.at[p], g_core.at[i], spot.core) for i, p in enumerate((pa, pb))]
    for copy in brought:
        copy.wait()
    sums.cross(3)
    sums.next(1)
    sums.cross(2)
    for wait in waits:
        wait()
    v = dot_tn(left[...], right_p[:, :1280])
    v2 = jnp.concatenate([dot_tn(left[...], right_p[:, 1280:1600]), dot_tn(left_b[...], right_q[...])], axis=1)
    for i, value in enumerate((v, v2)):
        for f in range(4):
            stage[f, pl.ds(0, 240), pl.ds(1280 * i, 1280)] = value[240 * f : 240 * f + 240].astype(BF)
    sums.to_core(0)
    for i, f in enumerate((spot.zl * 2 + spot.c, (1 - spot.zl) * 2 + spot.c)):
        small[i].wait_recv()
        g_mine[0, i] = gains[f] + g_core[i]
    gx = [mover.push(g_mine.at[0], g_x.at[i], spot.along_x(k)) for i, k in enumerate(OFFSETS)]

    def spread(ms):
        keep = pltpu.make_async_copy(ua.at[ms], out.at[ms, x, :, strip_at(y)], local.at[0])
        keep.start()
        keep.wait()

        def view(part, a, b):
            return out.at[(ms,) + chunk_at(moved(x, a), part) + (strip_at(moved(y, b)),)]

        def steps():
            rows = (0, (0, 32)), (1, (32, 32))
            sides = [ring_inner(mover, spot, *part, view) for part in rows]
            for _ in range(3):
                for side in sides:
                    next(side)
                yield
            sides = [ring_outer(mover, spot, *part, view, lambda ref: None) for part in rows]
            for _ in range(3):
                for side in sides:
                    next(side)
                yield

        return steps()

    sums.four(3)
    sums.one(0)
    sums.four(2)
    sums.three(1, ta.at[1], tb.at[1])
    sums.cross(1)
    for copy in gx:
        copy.wait_recv()
    g_mine[1] = g_mine[0] + g_x[0] + g_x[1] + g_x[2]
    gy = [mover.push(g_mine.at[1], g_y.at[i], spot.along_y(k)) for i, k in enumerate(OFFSETS)]
    sums.two(0)
    sums.next(0)
    sums.five(3)
    sums.five(2)
    sums.four(1)
    for copy in gy:
        copy.wait_recv()
    g_mine[2] = g_mine[1] + g_y[0] + g_y[1] + g_y[2]
    gz = mover.push(g_mine.at[2, 1], g_core.at[2], spot.z)
    sums.five(1)
    wide = spread(pl.ds(1, 3))
    next(wide)
    sums.three(0, ta.at[0], tb.at[0])
    sums.cross(0)
    next(wide)
    sums.four(0)
    next(wide)
    next(wide)
    sums.five(0)
    last = spread(pl.ds(0, 1))
    next(last)
    gz.wait_recv()
    gains_out[...] = g_mine[2, 0] + g_core[2]
    for _ in range(3):
        next(last)
    next(wide)
    next(last)
    next(wide)
    next(last)
    mover.finish()


def finish(sets, begun, parts):
    vm, n = pltpu.VMEM, 128
    return pl.pallas_call(
        finish_body,
        out_shape=(shape((4, 4, 64, 2560), BF), shape((8, 256), F32)),
        in_specs=[HBM] * 15 + [VM] * 6,
        out_specs=[HBM, VM],
        scratch_shapes=[
            vm((4, 8, 256), F32), vm((4, 256, 2560), BF), vm((2, 2, 256, 2560), BF),
            vm((2 * ROWS, D), BF), vm((2 * ROWS, D), BF), vm((2 * ROWS, 1664), BF), vm((2 * ROWS, D), BF),
            vm((2, 1, 32, 2560), BF), vm((2, 1, 128, STRIP), BF), vm((2, 2, 64, 2560), BF), vm((2, 2, 256, STRIP), BF),
            vm((4, 64, 2560), BF), vm((4, 256, STRIP), BF), vm((3, 4, 64, STRIP), BF), vm((3, 4, 64, STRIP), BF),
            vm((4, 64, STRIP), BF), vm((4, 64, STRIP), BF), vm((4, 64, STRIP), BF),
            vm((3, 8, 256), F32), vm((3, 2, 8, 256), F32), vm((3, 2, 8, 256), F32), vm((3, 2, 8, 256), F32),
            pltpu.SemaphoreType.DMA((n,)), pltpu.SemaphoreType.DMA((n,)), pltpu.SemaphoreType.DMA((7,)), pltpu.SemaphoreType.DMA((8,)),
        ],
        compiler_params=linked(2, 60),
        name="finish",
    )(*[a for trio in sets for a in trio], *begun, *[v for pair in parts for v in pair])


def pair_greet(spot, relay):
    barrier = pltpu.get_barrier_semaphore()
    for who in (spot.core, spot.z):
        pl.semaphore_signal(barrier, inc=1, device_id=who, device_id_type=MESH)
    if relay is None:
        pl.semaphore_wait(barrier, 2)
        return
    section, sender, ready = relay
    beyond = {"section": 1 - section}

    @pl.when(section == sender)
    def _():
        pl.semaphore_signal(barrier, inc=1, device_id=beyond, device_id_type=MESH)
        pl.semaphore_wait(barrier, 2)

    @pl.when(section != sender)
    def _():
        pl.semaphore_wait(barrier, 3)
        pl.semaphore_signal(ready, inc=1, device_id=beyond, device_id_type=MESH)


def relay_copy(section, src, dst, send, recv):
    return pltpu.make_async_remote_copy(
        src_ref=src, dst_ref=dst, send_sem=send, recv_sem=recv,
        device_id={"section": 1 - section}, device_id_type=MESH,
    )


def rope_tables(place):
    lane = lax.broadcasted_iota(jnp.int32, (ROWS, 128), 1)
    rows = lax.broadcasted_iota(jnp.int32, (ROWS, 128), 0) + place * ROWS
    frequencies = rope_base ** (-((lane % 32).astype(F32) * 2.0) / HEAD_DIM)
    angles = rows.astype(F32) * frequencies
    return jnp.cos(angles), jnp.sin(angles) * jnp.where(lane % 64 < 32, -1.0, 1.0)


def shards(
    block_input, cotangent, lengths, w_query, w_key, w_value, w_out, w_gate, w_up, w_down, gain_attn, gain_mlp
):
    cosine, signed = rope_tables(lax.axis_index("fsdp"))
    attn_w, ff_part, gains = first_weights(
        w_key[0].T, w_value[0].T, w_query[0], w_out[0], gain_attn, gain_mlp, w_gate[0], w_up[0], w_down[0].T
    )
    inputs_t = block_input.transpose(0, 2, 1)
    cot_t = cotangent.transpose(0, 2, 1)
    kept, outs = [], []
    attn_w = attn_w.reshape(4, 256, 2560)
    ff_w, hid, n1, q, kv, att, lse = front_first(lengths, inputs_t, gains, attn_w, ff_part, cosine, signed)
    ff_w = ff_w.reshape(3, 4, 256, 2560)
    for step in range(2):
        here = (hid, n1, q, kv, lse)
        out_t, mid, n2, gate, up, mixed, compact, hid, n1, q, kv, att, lse = forward(
            step, lengths, att, hid, inputs_t, gains, attn_w, ff_w, cosine, signed
        )
        outs.append(out_t)
        kept.append(here + (mid, n2, gate, up, mixed, compact))
    out_t, n2, mixed, compact, gg, gu, gm, gao, part_two, da, g_out = turn_back(
        lengths, att, hid, cot_t, gains, attn_w, ff_w
    )
    outs.append(out_t)
    kept.append((hid, n1, q, kv, lse, None, n2, None, None, mixed, compact))
    grads, parts, terms = [], [], []
    for step in range(3):
        hid, n1, q, kv, lse, _, n2, _, _, mixed, compact = kept[2 - step]
        before = (n1, compact, n2, g_out)
        after = (gao, gg, gu, mixed)
        if step < 2:
            mid, gate, up = (kept[1 - step][i] for i in (5, 7, 8))
            grad_t, packed, part_one, gg, gu, gm, gao, next_two, da, g_out = backward(
                step, lengths, q, kv, lse, da, cosine, signed, hid, gains, attn_w, ff_w, gm, cot_t, mid, gate, up
            )
        else:
            live = [(*(terms[k][i] for k in (0, 1)), (before + (None,) + after)[i]) for i in (3, 8, 2, 7, 6)]
            grad_t, packed, part_one, *begun = back_last(
                lengths, q, kv, lse, da, cosine, signed, hid, gains, attn_w, gm, live
            )
        grads.append(grad_t)
        parts.append((part_one, part_two))
        part_two = next_two
        terms.append(before + (packed,) + after)
    live = list(zip(*terms))
    summed, gain_sums = finish([live[i] for i in (0, 1, 4, 5)], begun, parts)
    query, key_t, value_t, out, gate, up, down_t, layer_out, input_grad = unpack(summed.reshape(4, 256, 2560), outs, grads)
    return (
        layer_out.transpose(0, 2, 1)[None],
        input_grad.transpose(0, 2, 1)[None],
        query[None],
        key_t.T[None],
        value_t.T[None],
        out[None],
        gate[None],
        up[None],
        down_t.T[None],
        gain_sums[0:1, :240],
        gain_sums[1:2, :240],
    )


def solution(mesh):
    tokens, two = ("dp", "fsdp"), P("section", "fsdp", None)
    return jax.shard_map(
        shards,
        mesh=mesh,
        in_specs=(P(None, tokens, None), P(None, tokens, None), P("dp", None)) + (two,) * 7 + (P("section", "fsdp"),) * 2,
        out_specs=(P("section", None, tokens, None),) * 2 + (two,) * 7 + (P("section", "fsdp"),) * 2,
        check_vma=False,
    )
```

```python
import functools

import jax
import jax.numpy as jnp
from jax import lax
from jax.experimental import pallas as pl
from jax.experimental.pallas import tpu as pltpu
from jax.sharding import PartitionSpec as P

HEADS = 15
KV_HEADS = 5
GROUP = 3
HEAD_DIM = 64
D = 960
ROWS = 256
STRIP = 640
SEQ = 1024
norm_eps = 1e-05
rope_base = 10000.0
masked_score = -1e30
BF = jnp.bfloat16
F32 = jnp.float32


def dot(a, b):
    return jnp.dot(a, b, preferred_element_type=F32)


def dot_nt(a, b):
    return lax.dot_general(a, b, (((1,), (1,)), ((), ())), preferred_element_type=F32)


def lanes(rows=ROWS):
    return lax.broadcasted_iota(jnp.int32, (rows, 128), 1)


def turn(tile, cosine, signed, low_half):
    partner = jnp.where(low_half, pltpu.roll(tile, 96, 1), pltpu.roll(tile, 32, 1))
    return tile * cosine + partner * signed


def whole(shape):
    return pl.BlockSpec(shape, lambda *_: (0,) * len(shape))


def params(limit=56):
    return pltpu.CompilerParams(vmem_limit_bytes=limit * 2**20)


def linked(collective_id, limit=56):
    return pltpu.CompilerParams(collective_id=collective_id, has_side_effects=True, vmem_limit_bytes=limit * 2**20)


VM = pl.BlockSpec(memory_space=pltpu.VMEM)
HBM = pl.BlockSpec(memory_space=pl.ANY)
SM = pl.BlockSpec(memory_space=pltpu.SMEM)


def shape(dims, kind):
    return jax.ShapeDtypeStruct(dims, kind)


def gain_row(gains, i):
    return jnp.concatenate([gains[f].astype(F32)[i : i + 1, :240] for f in range(4)], axis=1)


class Several:
    def __init__(self, copies):
        self.copies = copies

    def wait(self):
        for copy in self.copies:
            copy.wait()


class Streams:
    def __init__(self, sems):
        self.sems, self.count, self.open = sems, 0, []

    def start(self, src, dst):
        copy = pltpu.make_async_copy(src, dst, self.sems.at[self.count])
        self.count += 1
        copy.start()
        return copy

    def emit(self, src, dst):
        self.open.append(self.start(src, dst))

    def finish(self):
        for copy in self.open:
            copy.wait()


def unpack_body(summed, gains, *refs):
    layer_outs, grads = refs[:3], refs[3:6]
    q, k_t, v_t, out, gain_a, gain_b, gate, up, down_t, layer_out, input_grad = refs[6:17]
    raw, gate_s, up_s, down_s, layer_s, grad_s, q_s, k_s, v_s, out_s, sems = refs[17:]
    gain_a[...] = gains[0:1, 0:240]
    gain_b[...] = gains[1:2, 0:240]
    streams = Streams(sems)
    loads = [streams.start(summed.at[m, pl.ds(0, 240)], raw.at[m]) for m in range(4)]
    section = lax.axis_index("section")
    for i in range(2):
        for sources, slot in ((layer_outs, layer_s), (grads, grad_s)):
            first, second = (i, i + 1) if slot is layer_s else (2 - i, 1 - i)
            sem = sems.at[streams.count]
            streams.count += 1
            copies = [pltpu.make_async_copy(sources[k], slot.at[i], sem) for k in (first, second)]
            pl.when(section == 0)(copies[0].start)
            pl.when(section == 1)(copies[1].start)
            loads.append(copies[0])
    for m, slot, place in ((1, gate_s, gate), (2, up_s, up)):
        loads[m].wait()
        slot[...] = raw[m].astype(F32)
        streams.emit(slot, place)
    loads[3].wait()
    for j in range(4):
        down_s[240 * j : 240 * j + 240] = raw[3, :, STRIP * j : STRIP * j + STRIP].astype(F32)
    streams.emit(down_s, down_t)
    for load in loads[4:]:
        load.wait()
    streams.emit(layer_s, layer_out)
    streams.emit(grad_s, input_grad)
    loads[0].wait()
    attn = raw[0].astype(F32)
    keys = attn[:, :STRIP].T
    for value, slot, place in (
        (attn[:, STRIP:1600], q_s, q), (attn[:, 1600:], out_s, out), (keys[:320], k_s, k_t), (keys[320:], v_s, v_t)
    ):
        slot[...] = value
        streams.emit(slot, place)
    streams.finish()


def unpack(summed, gains, layer_outs, grads):
    dims = ((240, D), (320, 240), (320, 240), (240, D), (1, 240), (1, 240), (240, 2560), (240, 2560), (D, STRIP))
    return pl.pallas_call(
        unpack_body,
        out_shape=tuple(shape(s, F32) for s in dims) + (shape((2, D, ROWS), BF), shape((2, D, ROWS), F32)),
        in_specs=[HBM, VM] + [HBM] * 6,
        out_specs=[HBM] * 4 + [VM] * 2 + [HBM] * 5,
        scratch_shapes=[
            pltpu.VMEM((4, 240, 2560), BF), pltpu.VMEM((240, 2560), F32), pltpu.VMEM((240, 2560), F32),
            pltpu.VMEM((D, STRIP), F32), pltpu.VMEM((2, D, ROWS), BF), pltpu.VMEM((2, D, ROWS), F32),
            pltpu.VMEM((240, D), F32), pltpu.VMEM((320, 240), F32), pltpu.VMEM((320, 240), F32), pltpu.VMEM((240, D), F32),
            pltpu.SemaphoreType.DMA((17,)),
        ],
        compiler_params=params(),
        name="unpack",
    )(summed, gains, *layer_outs, *grads)


def fill_bias(bias, lens, slot, f):
    key = lax.broadcasted_iota(jnp.int32, (SEQ, ROWS), 0)
    place = lax.broadcasted_iota(jnp.int32, (SEQ, ROWS), 1) + f * ROWS
    one = jnp.where((key <= place) & (key < lens[0, slot]), 0.0, masked_score)
    for r in range(GROUP):
        bias[:, r * ROWS : (r + 1) * ROWS] = one


HEADS_SHAPE = (KV_HEADS, GROUP * ROWS, 128)
KEYS_SHAPE = (KV_HEADS, SEQ, 128)
WIDE, NARROW = (ROWS, 2560), (ROWS, D)


def head_rows(h):
    return slice(h % GROUP * ROWS, (h % GROUP + 1) * ROWS)


def front_part(step, spot, mover, streams, lens, hid, gains, load_w, w, cosine, signed, n1, q, kv, att, lse, bias, outs,
               between=None):
    section = lax.axis_index("section")
    slot = step // 2 if step != 1 else 1 - section
    h = hid[...].astype(F32)
    inverse = lax.rsqrt(jnp.mean(h * h, axis=-1, keepdims=True) + norm_eps)
    n = (h * inverse * gain_row(gains, 0)).astype(BF)
    n1[...] = n
    streams.emit(hid, outs[0])
    streams.emit(n1, outs[1])
    low = lanes() < 64
    half = lax.rem(lanes(), 64) < 32
    cos, sin = cosine[...], signed[...]
    load_w.wait()
    proj = dot(n, w[:, :STRIP])
    tile = [proj[:, 128 * i : 128 * i + 128] for i in range(5)]
    turned = [turn(tile[i], cos, sin, half) for i in range(3)]
    mine = pl.ds(pl.multiple_of(spot.f * ROWS, ROWS), ROWS)
    other = pl.ds(pl.multiple_of(((1 - spot.zl) * 2 + spot.c) * ROWS, ROWS), ROWS)
    across, near, far = [], [], []
    for g in range(KV_HEADS):
        k_tile, v_tile = turned[g // 2], tile[(5 + g) // 2]
        if g % 2 == 0:
            both = jnp.where(low, k_tile, v_tile)
        else:
            both = pltpu.roll(jnp.where(low, v_tile, k_tile), 64, 1)
        kv[g, mine] = both.astype(BF)
        block = kv.at[g, mine]
        across.append(mover.push(block, block, spot.z))
        near.append(mover.push(block, block, spot.core))
    proj = dot(n, w[:, STRIP:])
    for i in range(8):
        t = turn(proj[:, 128 * i : 128 * i + 128], cos, sin, half) * (HEAD_DIM**-0.5)
        for h in (2 * i, 2 * i + 1):
            if h < HEADS:
                part = pltpu.roll(t, 64, 1) if h % 2 else t
                q[h // GROUP, head_rows(h)] = jnp.where(low, part, 0.0).astype(BF)
    streams.emit(q, outs[2])
    fill_bias(bias, lens, slot, spot.f)

    def onward(g):
        across[g].wait_recv()
        block = kv.at[g, other]
        far.append(mover.push(block, block, spot.core))

    onward(0)
    for g in range(KV_HEADS):
        if g + 1 < KV_HEADS:
            onward(g + 1)
        near[g].wait_recv()
        far[g].wait_recv()
        if g + 1 == KV_HEADS:
            streams.emit(kv, outs[3])
        keys = kv[g]
        keys_t = keys.astype(F32).T.astype(BF)
        s = dot_nt(keys, q[g]) + bias[...]
        top = jnp.max(s, axis=0, keepdims=True)
        e = jnp.exp(s - top)
        total = jnp.sum(e, axis=0, keepdims=True)
        att[g] = (dot(keys_t, e.astype(BF)) / total).T.astype(BF)
        log_total = top + jnp.log(total)
        for r in range(GROUP):
            lse[g, r : r + 1] = log_total[:, r * ROWS : (r + 1) * ROWS]
        if between and g in between:
            between[g]()


FRONT_OUTS = (
    shape(NARROW, BF), shape(NARROW, BF), shape(HEADS_SHAPE, BF), shape(KEYS_SHAPE, BF),
    shape(HEADS_SHAPE, BF), shape((KV_HEADS, 8, ROWS), F32),
)
FRONT_SPECS = [HBM] * 4 + [VM] * 2
FRONT_SLOTS = [
    pltpu.VMEM((D, 1664), BF), pltpu.VMEM(NARROW, BF), pltpu.VMEM(NARROW, BF), pltpu.VMEM(HEADS_SHAPE, BF),
    pltpu.VMEM(KEYS_SHAPE, BF), pltpu.VMEM((SEQ, GROUP * ROWS), F32),
]


def load_columns(streams, attn, start, dst, flat=True):
    size = dst.shape[1]
    if not flat:
        return Several([
            streams.start(
                attn.at[f, i, pl.ds(0, 64 if i < 3 else 48), pl.ds(start, size)],
                dst.at[pl.ds(240 * f + 64 * i, 64 if i < 3 else 48)],
            )
            for f in range(4) for i in range(4)
        ])
    return Several([
        streams.start(attn.at[f, pl.ds(0, 240), pl.ds(start, size)], dst.at[pl.ds(240 * f, 240)]) for f in range(4)
    ])


def load_weights(streams, attn, ff, wo, wg, wu, wd, order):
    def load(k):
        if k == "o":
            return load_columns(streams, attn, 1536, wo)
        if k == "d":
            return Several([
                streams.start(
                    ff.at[2, f, pl.ds(0, 240), pl.ds(STRIP * j, STRIP)], wd.at[pl.ds(240 * j, 240), pl.ds(STRIP * f, STRIP)]
                )
                for f in range(4) for j in range(4)
            ])
        m, dst = (0, wg) if k == "g" else (1, wu)
        return Several([streams.start(ff.at[m, f, pl.ds(0, 240)], dst.at[pl.ds(240 * f, 240)]) for f in range(4)])

    return {k: load(k) for k in order}


def rest_part(streams, loads, att, hid, gains, wo, wg, wu, wd, mid_s, n2_s, gate_s, up_s, mixed_s, compact_s, out_s, outs):
    low = lanes() < 64

    def head(h):
        return att[h // GROUP, head_rows(h)].astype(F32)

    for h in range(0, HEADS - 1, 2):
        pair = jnp.where(low, pltpu.roll(head(h), 64, 1), head(h + 1))
        compact_s[:, 64 * h : 64 * h + 128] = pair.astype(BF)
    compact_s[:, 896:960] = pltpu.roll(head(HEADS - 1), 64, 1)[:, :64].astype(BF)
    streams.emit(compact_s, outs[5])
    loads["o"].wait()
    mid = hid[...].astype(F32) + dot(compact_s[...], wo[...])[:, 64:]
    mid_s[...] = mid
    inverse = lax.rsqrt(jnp.mean(mid * mid, axis=-1, keepdims=True) + norm_eps)
    n2_s[...] = (mid * inverse * gain_row(gains, 1)).astype(BF)
    if outs[0] is not None:
        streams.emit(mid_s, outs[0])
    streams.emit(n2_s, outs[1])
    loads["g"].wait()
    loads["u"].wait()
    for i in range(2):
        cols = slice(1280 * i, 1280 * i + 1280)
        n = n2_s[...]
        g = dot(n, wg[:, cols])
        u = dot(n, wu[:, cols])
        gate_s[:, cols] = g.astype(BF)
        up_s[:, cols] = u.astype(BF)
        mixed_s[:, cols] = (g * jax.nn.sigmoid(g) * u).astype(BF)
    if outs[2] is not None:
        streams.emit(gate_s, outs[2])
        streams.emit(up_s, outs[3])
    streams.emit(mixed_s, outs[4])
    loads["d"].wait()
    y = mid_s[...] + dot_nt(mixed_s[...], wd[...])
    out_s[...] = y.astype(BF)
    return y


WEIGHT_SLOTS = [pltpu.VMEM((D, 1024), BF)] + [pltpu.VMEM((D, 2560), BF)] * 3
REST_SLOTS = [
    pltpu.VMEM(NARROW, F32), pltpu.VMEM(NARROW, BF), pltpu.VMEM(WIDE, BF), pltpu.VMEM(WIDE, BF),
    pltpu.VMEM(WIDE, BF), pltpu.VMEM(NARROW, BF), pltpu.VMEM(NARROW, BF),
]


def forward_body(step, lens, att, hid, own_t, gains, attn_w, ff_w, cosine, signed,
                 out_t, o_mid, o_n2, o_gate, o_up, o_mixed, o_compact, o_hid, o_n1, o_q, o_kv, att_next, lse,
                 wo, wg, wu, wd, mid_s, n2_s, gate_s, up_s, mixed_s, compact_s, out_s,
                 w, hid_s, n1, q, kv, bias, passed_on, sems, front_sems, send, recv, ready):
    streams = Streams(sems)
    loads = load_weights(streams, attn_w, ff_w, wo, wg, wu, wd, "ogud")
    load_w = load_columns(streams, attn_w, 0, w)
    spot = Spot()
    section = lax.axis_index("section")
    pair_greet(spot, (section, 0, ready))
    y = rest_part(streams, loads, att, hid, gains, wo, wg, wu, wd, mid_s, n2_s, gate_s, up_s, mixed_s, compact_s, out_s,
                  (o_mid, o_n2, o_gate, o_up, o_mixed, o_compact))

    @pl.when(section == 0)
    def _():
        pl.semaphore_wait(ready, 1)
        relay_copy(section, out_s, passed_on, send.at[15], recv.at[15]).start()
        hid_s[...] = own_t[1].astype(F32).T.astype(BF)

    out_t[...] = y.T.astype(BF)

    @pl.when(section == 1)
    def _():
        relay_copy(section, out_s, passed_on, send.at[15], recv.at[15]).wait_recv()
        hid_s[...] = passed_on[...]

    def attention():
        mover = Mover(send, recv)
        inner = Streams(front_sems)
        front_part(step + 1, spot, mover, inner, lens, hid_s, gains, load_w, w, cosine, signed, n1, q, kv, att_next, lse, bias,
                   (o_hid, o_n1, o_q, o_kv))
        mover.finish()
        inner.finish()

    if step == 0:
        attention()
    else:
        pl.when(section == 1)(attention)

        @pl.when(section == 0)
        def _():
            inner = Streams(front_sems)
            load_w.wait()
            for slot, place in ((hid_s, o_hid), (n1, o_n1), (q, o_q), (kv, o_kv)):
                slot[...] = jnp.zeros(slot.shape, slot.dtype)
                inner.emit(slot, place)
            att_next[...] = jnp.zeros(att_next.shape, BF)
            lse[...] = jnp.zeros(lse.shape, F32)
            inner.finish()

    @pl.when(section == 0)
    def _():
        relay_copy(section, out_s, passed_on, send.at[15], recv.at[15]).wait_send()

    streams.finish()


def forward(step, lens, att, hid, own_t, gains, attn_w, ff_w, cosine, signed):
    rest_outs = (shape((D, ROWS), BF), shape(NARROW, F32), shape(NARROW, BF)) + (shape(WIDE, BF),) * 3 + (shape(NARROW, BF),)
    return pl.pallas_call(
        functools.partial(forward_body, step),
        out_shape=rest_outs + FRONT_OUTS,
        in_specs=[SM, VM, VM, VM, VM, HBM, HBM, VM, VM],
        out_specs=[VM] + [HBM] * 6 + FRONT_SPECS,
        scratch_shapes=WEIGHT_SLOTS + REST_SLOTS + FRONT_SLOTS + [
            pltpu.VMEM(NARROW, BF), pltpu.SemaphoreType.DMA((42,)), pltpu.SemaphoreType.DMA((4,)), pltpu.SemaphoreType.DMA((16,)),
            pltpu.SemaphoreType.DMA((16,)), pltpu.SemaphoreType.REGULAR,
        ],
        compiler_params=linked(4 + step, 60),
        name="forward",
    )(lens, att, hid, own_t, gains, attn_w, ff_w, cosine, signed)


def back_rest_part(streams, loads, g_out, gains, mid_ref, gate_s, up_s, gg_s, gu_s, gm_s, wo, wg, wu, wd, gao_out, part, da, outs):
    loads["d"].wait()
    for i in range(2):
        cols = slice(1280 * i, 1280 * i + 1280)
        grad_mixed = dot(g_out[...], wd[:, cols])
        ga = gate_s[:, cols].astype(F32)
        sg = jax.nn.sigmoid(ga)
        scaled = grad_mixed * sg
        gg_s[:, cols] = (scaled * up_s[:, cols].astype(F32) * (1.0 + ga * (1.0 - sg))).astype(BF)
        gu_s[:, cols] = (scaled * ga).astype(BF)
    streams.emit(gg_s, outs[0])
    streams.emit(gu_s, outs[1])
    loads["g"].wait()
    loads["u"].wait()
    grad_normed = dot_nt(gg_s[...], wg[...]) + dot_nt(gu_s[...], wu[...])
    mid = mid_ref[...]
    inverse = lax.rsqrt(jnp.mean(mid * mid, axis=-1, keepdims=True) + norm_eps)
    unit = mid * inverse
    part[...] = jnp.sum(grad_normed * unit, axis=0, keepdims=True)
    scaled_two = grad_normed * gain_row(gains, 1)
    gm = g_out[...].astype(F32) + inverse * (
        scaled_two - unit * jnp.mean(scaled_two * unit, axis=-1, keepdims=True)
    )
    gm_s[...] = gm
    streams.emit(gm_s, outs[2])
    gao_out[...] = gm.astype(BF)
    shifted = jnp.concatenate([jnp.zeros((ROWS, 64), F32), gm], axis=1).astype(BF)
    loads["o"].wait()
    att = jnp.concatenate([dot_nt(shifted, wo[...]), jnp.zeros((ROWS, 64), F32)], axis=1)
    low = lanes() < 64
    for h in range(HEADS):
        tile = att[:, 128 * (h // 2) : 128 * (h // 2) + 128]
        if h % 2 == 0:
            tile = pltpu.roll(tile, 64, 1)
        da[h // GROUP, head_rows(h)] = jnp.where(low, 0.0, tile).astype(BF)


def live_cotangent(step, lens, cot_t):
    place = lax.broadcasted_iota(jnp.int32, (D, ROWS), 1) + lax.axis_index("fsdp") * ROWS
    return jnp.where(place < lens[0, 1 - step], cot_t[1 - step].astype(F32), 0.0).T.astype(BF)


BACK_OUTS = (
    shape(WIDE, BF), shape(WIDE, BF), shape(NARROW, F32), shape(NARROW, BF), shape((1, D), F32),
    shape(HEADS_SHAPE, BF), shape(NARROW, BF),
)
BACK_SPECS = [HBM] * 3 + [VM] * 4


def turn_back_body(lens, att, hid, cot_t, gains, attn_w, ff_w,
                   out_t, o_n2, o_mixed, o_compact, o_gg, o_gu, o_gm, gao, part, da, g_out,
                   wo, wg, wu, wd, mid_s, n2_s, gate_s, up_s, mixed_s, compact_s, out_s, gg_s, gu_s, gm_s, sems):
    streams = Streams(sems)
    loads = load_weights(streams, attn_w, ff_w, wo, wg, wu, wd, "ogud")
    y = rest_part(streams, loads, att, hid, gains, wo, wg, wu, wd, mid_s, n2_s, gate_s, up_s, mixed_s, compact_s, out_s,
                  (None, o_n2, None, None, o_mixed, o_compact))
    out_t[...] = y.T.astype(BF)
    g_out[...] = jnp.where(lax.axis_index("section") == 1, live_cotangent(0, lens, cot_t), 0.0).astype(BF)

    class Done:
        def wait(self):
            pass

    back_rest_part(streams, {k: Done() for k in "ogud"}, g_out, gains, mid_s, gate_s, up_s, gg_s, gu_s, gm_s,
                   wo, wg, wu, wd, gao, part, da, (o_gg, o_gu, o_gm))
    streams.finish()


def turn_back(lens, att, hid, cot_t, gains, attn_w, ff_w):
    return pl.pallas_call(
        turn_back_body,
        out_shape=(shape((D, ROWS), BF), shape(NARROW, BF), shape(WIDE, BF), shape(NARROW, BF)) + BACK_OUTS,
        in_specs=[SM, VM, VM, VM, VM, HBM, HBM],
        out_specs=[VM] + [HBM] * 3 + BACK_SPECS,
        scratch_shapes=WEIGHT_SLOTS + REST_SLOTS + [
            pltpu.VMEM(WIDE, BF), pltpu.VMEM(WIDE, BF), pltpu.VMEM(NARROW, F32), pltpu.SemaphoreType.DMA((36,)),
        ],
        compiler_params=params(60),
        name="turn_back",
    )(lens, att, hid, cot_t, gains, attn_w, ff_w)


def back_attend_part(step, spot, mover, lens, q, kv, lse, da, cosine, signed, hid, gains, load_w, w, gm, packed, gain_part,
                     bias, part, near, passed, far, own, dq, between=None):
    section = lax.axis_index("section")
    slot = 1 - section if step == 1 else 1 - step // 2
    fill_bias(bias, lens, slot, spot.f)
    low = lanes() < 64
    half = lax.rem(lanes(), 64) < 32
    cos, sin = cosine[...], -signed[...]

    def rows_of(zl, c):
        return pl.ds(pl.multiple_of((zl * 2 + c) * ROWS, ROWS), ROWS)

    there, here = 1 - spot.zl, spot.zl
    core, across = {}, {}

    def stage_one(g):
        core[g][0].wait_recv()
        passed[g] = (part[g, rows_of(there, spot.c)].astype(F32) + near[g, 0].astype(F32)).astype(BF)
        across[g] = mover.push(passed.at[g], far.at[g], spot.z)
        core[g][1].wait_recv()
        own[g] = part[g, rows_of(here, spot.c)].astype(F32) + near[g, 1].astype(F32)

    def stage_two(g):
        across[g].wait_recv()
        own[g] = own[g] + far[g].astype(F32)

    for g in range(KV_HEADS):
        keys = kv[g]
        keys_t = keys.astype(F32).T.astype(BF)
        logs = jnp.concatenate([lse[g, r : r + 1] for r in range(GROUP)], axis=1)
        p = jnp.exp(dot_nt(keys, q[g]) + bias[...] - logs)
        dp = dot_nt(keys, da[g])
        delta = jnp.sum(p * dp, axis=0, keepdims=True)
        ds = (p * (dp - delta)).astype(BF)
        part[g] = (dot(ds, q[g]) + dot(p.astype(BF), da[g])).astype(BF)
        core[g] = (
            mover.push(part.at[g, rows_of(there, 1 - spot.c)], near.at[g, 0], spot.core),
            mover.push(part.at[g, rows_of(here, 1 - spot.c)], near.at[g, 1], spot.core),
        )
        grad_q = (dot(keys_t, ds) * (HEAD_DIM**-0.5)).T
        for r in range(GROUP):
            rows = slice(r * ROWS, (r + 1) * ROWS)
            dq[g, rows] = turn(grad_q[rows], cos, sin, half).astype(BF)
        if g > 0:
            stage_one(g - 1)
        if g > 1:
            stage_two(g - 2)
        if between and g in between:
            between[g]()

    def merged(left, right):
        return jnp.where(low, left, right)

    def flip(v):
        return pltpu.roll(v, 64, 1)

    def head(h):
        return dq[h // GROUP, head_rows(h)].astype(F32)

    stage_one(KV_HEADS - 1)
    for h in range(0, HEADS, 2):
        tile = merged(head(h), flip(head(h + 1)) if h + 1 < HEADS else 0.0)
        packed[:, STRIP + 64 * h : STRIP + 64 * h + 128] = tile.astype(BF)
    load_w.wait()
    grad_normed = dot_nt(packed[:, STRIP:], w[:, STRIP:])
    hidden = hid[...].astype(F32)
    inverse = lax.rsqrt(jnp.mean(hidden * hidden, axis=-1, keepdims=True) + norm_eps)
    unit = hidden * inverse
    stage_two(KV_HEADS - 2)
    stage_two(KV_HEADS - 1)
    both = [own[g] for g in range(KV_HEADS)]
    turned = [turn(b, cos, sin, half) for b in both]
    tiles = [
        merged(turned[0], flip(turned[1])),
        merged(turned[2], flip(turned[3])),
        merged(turned[4], both[0]),
        merged(flip(both[1]), both[2]),
        merged(flip(both[3]), both[4]),
    ]
    for i, tile in enumerate(tiles):
        packed[:, 128 * i : 128 * i + 128] = tile.astype(BF)
    grad_normed = grad_normed + dot_nt(packed[:, :STRIP], w[:, :STRIP])
    gain_part[...] = jnp.sum(grad_normed * unit, axis=0, keepdims=True)
    scaled = grad_normed * gain_row(gains, 0)
    return gm[...] + inverse * (scaled - unit * jnp.mean(scaled * unit, axis=-1, keepdims=True))


OWN_SHAPE = (KV_HEADS, ROWS, 128)
ATTEND_SLOTS = [
    pltpu.VMEM((SEQ, GROUP * ROWS), F32), pltpu.VMEM(KEYS_SHAPE, BF), pltpu.VMEM((KV_HEADS, 2, ROWS, 128), BF),
    pltpu.VMEM(OWN_SHAPE, BF), pltpu.VMEM(OWN_SHAPE, BF), pltpu.VMEM(OWN_SHAPE, F32), pltpu.VMEM(HEADS_SHAPE, BF),
    pltpu.VMEM((D, 1664), BF),
]
ATTEND_OUTS = (shape((D, ROWS), F32), shape((ROWS, 1664), BF), shape((1, D), F32))


def backward_body(step, lens, q, kv, lse, da, cosine, signed, hid, gains, attn_w, ff_w, gm, cot_t, mid, gate, up,
                  grad_t, packed, gain_part, o_gg, o_gu, o_gm, gao, part_two, da_next, g_out,
                  bias, part, near, passed, far, own, dq, w, wo, wg, wu, wd, gate_s, up_s, gg_s, gu_s, gm_s,
                  out_s, passed_on, sems, send, recv, ready):
    streams = Streams(sems)
    load_w = load_columns(streams, attn_w, 0, w)
    loads = load_weights(streams, attn_w, ff_w, wo, wg, wu, wd, "dguo")
    load_gate = streams.start(gate, gate_s)
    load_up = streams.start(up, up_s)
    spot = Spot()
    section = lax.axis_index("section")
    pair_greet(spot, (section, 1, ready))
    mover = Mover(send, recv)
    grad_in = back_attend_part(step, spot, mover, lens, q, kv, lse, da, cosine, signed, hid, gains, load_w, w, gm,
                               packed, gain_part, bias, part, near, passed, far, own, dq)
    out_s[...] = grad_in.astype(BF)

    @pl.when(section == 1)
    def _():
        pl.semaphore_wait(ready, 1)
        relay_copy(section, out_s, passed_on, send.at[15], recv.at[15]).start()
        if step == 0:
            g_out[...] = live_cotangent(1, lens, cot_t)
        else:
            g_out[...] = jnp.zeros(NARROW, BF)

    grad_t[...] = grad_in.T

    @pl.when(section == 0)
    def _():
        relay_copy(section, out_s, passed_on, send.at[15], recv.at[15]).wait_recv()
        g_out[...] = passed_on[...]

    load_gate.wait()
    load_up.wait()
    back_rest_part(streams, loads, g_out, gains, mid, gate_s, up_s, gg_s, gu_s, gm_s, wo, wg, wu, wd, gao, part_two, da_next,
                   (o_gg, o_gu, o_gm))
    mover.finish()

    @pl.when(section == 1)
    def _():
        relay_copy(section, out_s, passed_on, send.at[15], recv.at[15]).wait_send()

    streams.finish()


def backward(step, lens, q, kv, lse, da, cosine, signed, hid, gains, attn_w, ff_w, gm, cot_t, mid, gate, up):
    return pl.pallas_call(
        functools.partial(backward_body, step),
        out_shape=ATTEND_OUTS + BACK_OUTS,
        in_specs=[SM] + [VM] * 8 + [HBM, HBM, VM, VM, VM, HBM, HBM],
        out_specs=[VM] * 3 + BACK_SPECS,
        scratch_shapes=ATTEND_SLOTS + WEIGHT_SLOTS + [pltpu.VMEM(WIDE, BF)] * 4 + [
            pltpu.VMEM(NARROW, F32), pltpu.VMEM(NARROW, BF), pltpu.VMEM(NARROW, BF), pltpu.SemaphoreType.DMA((40,)),
            pltpu.SemaphoreType.DMA((16,)), pltpu.SemaphoreType.DMA((16,)), pltpu.SemaphoreType.REGULAR,
        ],
        compiler_params=linked(6 + step, 62),
        name="backward",
    )(lens, q, kv, lse, da, cosine, signed, hid, gains, attn_w, ff_w, gm, cot_t, mid, gate, up)


MESH = pl.DeviceIdType.MESH
SIDE = 4
OFFSETS = (1, 3, 2)
HALVES = ((0, 128), (128, 112))


class Spot:
    def __init__(self):
        d = lax.axis_index("dp")
        f = lax.axis_index("fsdp")
        self.x, self.y = d // SIDE, lax.rem(d, SIDE)
        self.zl, self.c = f // 2, lax.rem(f, 2)
        self.f = f
        self.core = {"fsdp": self.zl * 2 + 1 - self.c}
        self.z = {"fsdp": (1 - self.zl) * 2 + self.c}
        self.across = {"fsdp": (1 - self.zl) * 2 + 1 - self.c}

    def along_x(self, k):
        return {"dp": lax.rem(self.x + k, SIDE) * SIDE + self.y}

    def along_y(self, k):
        return {"dp": self.x * SIDE + lax.rem(self.y + k, SIDE)}

    def greet(self):
        self.call()
        self.hear()

    def call(self):
        barrier = pltpu.get_barrier_semaphore()
        ids = [self.core, self.z, self.across]
        for k in range(1, SIDE):
            ids += [self.along_x(k), self.along_y(k)]
        for who in ids:
            pl.semaphore_signal(barrier, inc=1, device_id=who, device_id_type=MESH)

    def hear(self):
        pl.semaphore_wait(pltpu.get_barrier_semaphore(), 9)


class Mover:
    def __init__(self, send, recv):
        self.send, self.recv, self.pending, self.count = send, recv, [], 0

    def push(self, src, dst, who):
        i = self.count
        self.count += 1
        copy = pltpu.make_async_remote_copy(
            src_ref=src, dst_ref=dst, send_sem=self.send.at[i], recv_sem=self.recv.at[i],
            device_id=who, device_id_type=MESH,
        )
        copy.start()
        self.pending.append(copy)
        return copy

    def finish(self):
        for copy in self.pending:
            copy.wait_send()


def ring_axes(spot, which, view):
    if which == 0:
        return spot.along_x, spot.along_y, view
    return spot.along_y, spot.along_x, lambda part, a, b: view(part, b, a)


def ring_inner(mover, spot, which, rows, view):
    inner, outer, at = ring_axes(spot, which, view)
    lo, size = rows
    both, one, two = rows, (lo, size // 2), (lo + size // 2, size // 2)
    own = at(both, 0, 0)
    near = [mover.push(own, own, inner(k)) for k in (1, 3)]
    yield
    for copy in near:
        copy.wait_recv()
    far = [mover.push(at(one, 3, 0), at(one, 3, 0), inner(1)), mover.push(at(two, 1, 0), at(two, 1, 0), inner(3))]
    yield
    for copy in far:
        copy.wait_recv()
    yield


def ring_outer(mover, spot, which, rows, view, onward, direct=()):
    inner, outer, at = ring_axes(spot, which, view)
    lo, size = rows
    both, one, two = rows, (lo, size // 2), (lo + size // 2, size // 2)
    line = at(both, None, 0)
    near = [mover.push(line, line, outer(k)) for k in (1, 3)]
    onward(line)
    yield
    for copy in near:
        copy.wait_recv()
    line = LATE if direct else None
    far = list(direct)
    far.append(mover.push(at(one, line, 3), at(one, line, 3), outer(1)))
    far.append(mover.push(at(two, line, 1), at(two, line, 1), outer(3)))
    onward(at(both, None, 3))
    onward(at(both, None, 1))
    yield
    for copy in far:
        copy.wait_recv()
    onward(at(both, None, 2))
    yield


LATE = "late"


def chunk_at(p, part):
    if p is None or p is LATE:
        return pl.ds(0, 4) if p is None else pl.ds(2, 2), pl.ds(*part)
    return pl.ds(lax.rem(p, SIDE), 1), pl.ds(*part)


def strip_at(p):
    if p is None or p is LATE:
        return pl.ds(0, 2560) if p is None else pl.ds(1280, 1280)
    return pl.ds(pl.multiple_of(lax.rem(p, SIDE) * STRIP, 128), STRIP)


def moved(p, a):
    return a if a is None or a is LATE else p + a


def chunk_rows(p, lo=0, size=64):
    return pl.ds(pl.multiple_of(lax.rem(p, SIDE) * 64 + lo, 16), size)


def strip_cols(p):
    return pl.ds(pl.multiple_of(lax.rem(p, SIDE) * STRIP, 128), STRIP)


def first_body(lens, k_t, v_t, wq, wo, gain_a, gain_b, own_t, cosine, signed, gate, up, down_t,
               attn_full, ff_full, gains_full, o_hid, o_n1, o_q, o_kv, att, lse,
               own, ff, gains, w, hid, n1, q, kv, bias, sems, send, recv):
    streams = Streams(sems)
    loads = [
        streams.start(gate, ff.at[0, pl.ds(0, 240)]),
        streams.start(up, ff.at[1, pl.ds(0, 240)]),
    ]
    for j in range(4):
        loads.append(streams.start(down_t.at[pl.ds(240 * j, 240)], ff.at[2, pl.ds(0, 240), pl.ds(STRIP * j, STRIP)]))
    spot = Spot()
    x, y, f = spot.x, spot.y, spot.f
    fz = (1 - spot.zl) * 2 + spot.c
    spot.call()
    keys = jnp.concatenate([k_t[...].astype(F32), v_t[...].astype(F32)], axis=0).T
    both = jnp.concatenate([wq[...].astype(F32), wo[...].astype(F32)], axis=1)
    for i in range(4):
        size = 64 if i < 3 else 48
        own[i, :size, :STRIP] = keys[64 * i : 64 * i + size].astype(BF)
        own[i, :size, STRIP:] = both[64 * i : 64 * i + size].astype(BF)
    own[3, 48:64] = jnp.zeros((16, 2560), BF)
    ff[:, pl.ds(240, 16)] = jnp.zeros((3, 16, 2560), BF)
    gains[...] = jnp.zeros((8, 256), F32)
    gains[0:1, 0:240] = gain_a[...].astype(F32)
    gains[1:2, 0:240] = gain_b[...].astype(F32)
    spot.hear()
    mover = Mover(send, recv)
    here = chunk_at(x, (0, 64)) + (strip_at(y),)
    first = mover.push(own.at[here], attn_full.at[(f,) + here], spot.z)
    for load in loads:
        load.wait()
    every = pl.ds(0, 3)
    there = (every, f, lax.rem(x, SIDE), pl.ds(0, 64), strip_at(y))
    second = mover.push(ff.at[every, chunk_rows(x), strip_at(y)], ff_full.at[there], spot.z)
    waits = [mover.push(gains, gains_full.at[f], {"fsdp": lax.rem(f + k, 4)}) for k in range(1, 4)]
    waits.append(mover.push(own, attn_full.at[f], spot.core))
    streams.emit(own, attn_full.at[f])
    gains_full[f] = gains[...]
    late = []

    def view(part, a, b):
        return attn_full.at[(fz,) + chunk_at(moved(x, a), part) + (strip_at(moved(y, b)),)]

    def ff_view(part, a, b):
        return ff_full.at[(every, fz) + chunk_at(moved(x, a), part) + (strip_at(moved(y, b)),)]

    def onward(ref):
        waits.append(mover.push(ref, ref, spot.core))

    def ff_onward(ref):
        late.append(mover.push(ref, ref, spot.core))

    parts = (0, (0, 32)), (1, (32, 32))
    sides = [ring_inner(mover, spot, *part, view) for part in parts]
    hid[...] = jnp.where(lax.axis_index("section") == 0, own_t[0].astype(F32).T, 0.0).astype(BF)
    first.wait_recv()
    for side in sides:
        next(side)
    direct = (
        [mover.push(ff.at[every, pl.ds(64 * i, 32), strip_at(y + 2)], ff_full.at[every, f, i, pl.ds(0, 32), strip_at(y + 2)], spot.z)
         for i in range(2)],
        [mover.push(ff.at[every, chunk_rows(x + 2, 32, 32), pl.ds(0, 1280)],
                    ff_full.at[every, f, lax.rem(x + 2, SIDE), pl.ds(32, 32), pl.ds(0, 1280)], spot.z)],
    )
    for i in range(4):
        late.append(mover.push(ff.at[every, pl.ds(64 * i, 64)], ff_full.at[every, f, i], spot.core))
        streams.emit(ff.at[every, pl.ds(64 * i, 64)], ff_full.at[every, f, i])
    for _ in range(2):
        for side in sides:
            next(side)
    sides = [ring_outer(mover, spot, *part, view, onward) for part in parts]
    for side in sides:
        next(side)
    second.wait_recv()
    ff_sides = [ring_inner(mover, spot, *part, ff_view) for part in parts]
    for _ in range(2):
        for side in ff_sides:
            next(side)
        for side in sides:
            next(side)
    for copy in waits:
        copy.wait_recv()
    for copy in streams.open[:1]:
        copy.wait()
    streams.open = streams.open[1:]
    load_w = load_columns(streams, attn_full, 0, w, flat=False)

    def inner_done():
        for side in ff_sides:
            next(side)
        outers.extend(ring_outer(mover, spot, *part, ff_view, ff_onward, direct[part[0]]) for part in parts)
        progress()

    outers = []

    def progress():
        for side in outers:
            next(side)

    inner_done()
    front_part(0, spot, mover, streams, lens, hid, gains_full, load_w, w, cosine, signed, n1, q, kv, att, lse, bias,
               (o_hid, o_n1, o_q, o_kv), {2: progress})
    progress()
    for copy in late:
        copy.wait_recv()
    mover.finish()
    streams.finish()


def first_attention(*operands):
    n = 112
    return pl.pallas_call(
        first_body,
        out_shape=(shape((4, 4, 64, 2560), BF), shape((3, 4, 4, 64, 2560), BF), shape((4, 8, 256), F32)) + FRONT_OUTS,
        in_specs=[SM] + [VM] * 9 + [HBM] * 3,
        out_specs=[HBM, HBM, VM] + FRONT_SPECS,
        scratch_shapes=[pltpu.VMEM((4, 64, 2560), BF), pltpu.VMEM((3, 256, 2560), BF), pltpu.VMEM((8, 256), F32)] + FRONT_SLOTS + [
            pltpu.SemaphoreType.DMA((32,)), pltpu.SemaphoreType.DMA((n,)), pltpu.SemaphoreType.DMA((n,)),
        ],
        compiler_params=linked(1),
        name="first_attention",
    )(*operands)


STEP = 16


def add_rows(out, rows, terms):
    def body(i, carry):
        sl = pl.ds(pl.multiple_of(i * STEP, STEP), STEP)
        total = terms[0](sl).astype(F32)
        for term in terms[1:]:
            total = total + term(sl).astype(F32)
        out(sl, total.astype(BF))
        return carry

    lax.fori_loop(0, rows // STEP, body, 0)


def dot_tn(a, b):
    return lax.dot_general(a, b, (((0,), (0,)), ((), ())), preferred_element_type=F32)


class Sums:
    def __init__(self, spot, mover, **slots):
        self.spot, self.mover, self.flights = spot, mover, {}
        self.__dict__.update(slots)

    def land(self, *key):
        for copy in self.flights[key]:
            copy.wait_recv()

    def chunk(self, k, lo=0, size=64):
        return chunk_rows(self.spot.x + k, lo, size)

    def strip(self, k):
        return strip_cols(self.spot.y + k)

    def to_core(self, m, cols=pl.ds(0, 2560)):
        spot, rows = self.spot, pl.ds(0, 256)
        flight = self.flights.setdefault(("core", m), [])
        for i, f in enumerate((spot.zl * 2 + 1 - spot.c, (1 - spot.zl) * 2 + 1 - spot.c)):
            flight.append(self.mover.push(self.stage.at[f, rows, cols], self.own.at[m, i, rows, cols], spot.core))

    def core_sent(self, m):
        for copy in self.flights["core", m]:
            copy.wait_send()
            self.mover.pending = [item for item in self.mover.pending if item is not copy]

    def one(self, m):
        self.land("core", m)
        spot, push, own = self.spot, self.mover.push, self.own
        for i, f in enumerate((spot.zl * 2 + spot.c, (1 - spot.zl) * 2 + spot.c)):
            def put(sl, v, i=i):
                own[m, i, sl] = v
            add_rows(put, 256, [lambda sl, i=i: own[m, i, sl], lambda sl, f=f: self.stage[f, sl]])
        self.flights["half", m] = (
            push(own.at[m, 0, self.chunk(2, 0, 32)], self.hx.at[0, m], spot.along_x(1)),
            push(own.at[m, 0, self.chunk(2, 32, 32)], self.hx.at[1, m], spot.along_x(3)),
            push(own.at[m, 1, pl.ds(0, 128), self.strip(2)], self.hy.at[0, m], spot.along_y(1)),
            push(own.at[m, 1, pl.ds(128, 128), self.strip(2)], self.hy.at[1, m], spot.along_y(3)),
        )

    def two(self, m):
        self.land("half", m)
        spot, own = self.spot, self.own
        for i, k in ((0, 1), (1, 3)):
            base = lax.rem(spot.x + k, SIDE) * 64 + 32 * i

            def rows(sl, base=base):
                return pl.ds(pl.multiple_of(base + sl.start, 16), STEP)

            def put(sl, v, rows=rows):
                own[m, 0, rows(sl)] = v
            add_rows(put, 32, [lambda sl, rows=rows: own[m, 0, rows(sl)], lambda sl, i=i: self.hx[i, m, sl]])

            def low(sl, i=i):
                return pl.ds(pl.multiple_of(128 * i + sl.start, 16), STEP)

            def put(sl, v, low=low, k=k):
                own[m, 1, low(sl), self.strip(k)] = v
            add_rows(put, 128, [lambda sl, low=low, k=k: own[m, 1, low(sl), self.strip(k)], lambda sl, i=i: self.hy[i, m, sl]])

    def next(self, m):
        spot, push, own = self.spot, self.mover.push, self.own
        self.flights["next", m] = tuple(
            copy
            for i, k in ((0, 1), (1, 3))
            for copy in (
                push(own.at[m, 0, self.chunk(k)], self.rx.at[i, m], spot.along_x(k)),
                push(own.at[m, 1, :, self.strip(k)], self.ry.at[i, m], spot.along_y(k)),
            )
        )

    def three(self, m, ta, tb):
        self.land("next", m)
        own, base = self.own, self.spot.x * 64

        def put(sl, v):
            ta[sl] = v
        first = lambda sl: own[m, 0, pl.ds(pl.multiple_of(base + sl.start, 16), STEP)]
        add_rows(put, 64, [first, lambda sl: self.rx[0, m, sl], lambda sl: self.rx[1, m, sl]])

        def put(sl, v):
            tb[sl] = v
        add_rows(put, 256, [lambda sl: own[m, 1, sl, self.strip(0)], lambda sl: self.ry[0, m, sl], lambda sl: self.ry[1, m, sl]])

    def cross(self, m):
        spot, push = self.spot, self.mover.push
        self.flights["second", m] = tuple(
            copy
            for i, k in enumerate(OFFSETS)
            for copy in (
                push(self.ta.at[m, :, self.strip(k)], self.ry2.at[i, m], spot.along_y(k)),
                push(self.tb.at[m, self.chunk(k)], self.rx2.at[i, m], spot.along_x(k)),
            )
        )

    def four(self, m):
        self.land("second", m)
        ta, tb, ua, ub, base = self.ta, self.tb, self.ua, self.ub, self.spot.x * 64

        def put(sl, v):
            ub[m, sl] = v
        first = lambda sl: tb[m, pl.ds(pl.multiple_of(base + sl.start, 16), STEP)]
        add_rows(put, 64, [first] + [lambda sl, i=i: self.rx2[i, m, sl] for i in range(3)])

        def put(sl, v):
            ua[m, sl] = v
        add_rows(put, 64, [lambda sl: ta[m, sl, self.strip(0)]] + [lambda sl, i=i: self.ry2[i, m, sl] for i in range(3)])

    def to_z(self, m):
        self.flights["z", m] = (self.mover.push(self.ub.at[m], self.rz.at[m], self.spot.z),)

    def five(self, m):
        self.land("z", m)
        ua = self.ua

        def put(sl, v):
            ua[m, sl] = v
        add_rows(put, 64, [lambda sl: ua[m, sl], lambda sl: self.rz[m, sl]])


class Live:
    def __init__(self, sems):
        self.sems, self.count = sems, 0

    def load(self, trio, dst):
        i = self.count
        self.count += 2
        section = lax.axis_index("section")
        fixed = pltpu.make_async_copy(trio[1], dst.at[pl.ds(ROWS, ROWS)], self.sems.at[i])
        fixed.start()
        early = pltpu.make_async_copy(trio[0], dst.at[pl.ds(0, ROWS)], self.sems.at[i + 1])
        late = pltpu.make_async_copy(trio[2], dst.at[pl.ds(0, ROWS)], self.sems.at[i + 1])
        pl.when(section == 1)(early.start)
        pl.when(section == 0)(late.start)

        def wait():
            fixed.wait()
            pl.when(section == 1)(early.wait)
            pl.when(section == 0)(late.wait)

        return wait


def wide_gradient(stage, tall, left, right):
    for i in range(2):
        v = dot_tn(left[...], right[:, pl.ds(1280 * i, 1280)])
        for f in range(4):
            if not tall:
                stage[f, pl.ds(0, 240), pl.ds(1280 * i, 1280)] = v[240 * f : 240 * f + 240].astype(BF)
            elif f // 2 == i:
                for j in range(4):
                    cols = slice(STRIP * (f % 2), STRIP * (f % 2) + STRIP)
                    stage[f, pl.ds(0, 240), pl.ds(STRIP * j, STRIP)] = v[240 * j : 240 * j + 240, cols].astype(BF)


def back_last_body(lens, q, kv, lse, da, cosine, signed, hid, gains, attn_w, gm, *refs):
    gd, mixed, n2, gu, gg = (refs[3 * i : 3 * i + 3] for i in range(5))
    (grad_t, packed, gain_part, ta_out, tb_out, own_out, ua_out, ub_out, bias, part, near, passed, far, own_keys, dq, w,
     stage, own, hx, hy, rx, ry, ta, tb, rx2, ry2, ua, ub, left, right, sems, live_sems, send, recv) = refs[15:]
    spot = Spot()
    spot.call()
    streams = Streams(sems)
    live = Live(live_sems)
    waits = {0: [live.load(gd, left.at[0]), live.load(mixed, right.at[0])]}
    load_w = load_columns(streams, attn_w, 0, w)
    waits[1] = [live.load(n2, left.at[1]), live.load(gu, right.at[1])]
    stage[:, pl.ds(240, 16)] = jnp.zeros((4, 16, 2560), BF)
    spot.hear()
    mover = Mover(send, recv)
    sums = Sums(spot, mover, stage=stage, own=own, hx=hx, hy=hy, rx=rx, ry=ry, ta=ta, tb=tb, rx2=rx2, ry2=ry2, ua=ua, ub=ub)

    def compute(k):
        for wait in waits[k]:
            wait()
        wide_gradient(stage, k == 0, left.at[min(k, 1)], right.at[k % 2])
        if k == 0:
            waits[2] = [live.load(gg, right.at[0])]
        sums.to_core(k)

    def after_one():
        sums.one(0)
        sums.core_sent(0)
        compute(1)

    def after_two():
        sums.one(1)
        sums.two(0)
        sums.next(0)
        sums.core_sent(1)
        compute(2)

    def after_three():
        sums.one(2)
        sums.two(1)
        sums.next(1)

    def after_four():
        sums.three(0, ta.at[0], tb.at[0])
        sums.cross(0)

    compute(0)
    grad_in = back_attend_part(2, spot, mover, lens, q, kv, lse, da, cosine, signed, hid, gains, load_w, w, gm,
                               packed, gain_part, bias, part, near, passed, far, own_keys, dq,
                               {1: after_one, 2: after_two, 3: after_three, 4: after_four})
    sums.two(2)
    streams.emit(own.at[2], own_out)
    grad_t[...] = grad_in.T
    sums.three(1, ta.at[1], tb.at[1])
    streams.emit(ta.at[1], ta_out)
    streams.emit(tb.at[1], tb_out)
    sums.four(0)
    streams.emit(ua.at[0], ua_out)
    streams.emit(ub.at[0], ub_out)
    mover.finish()
    streams.finish()


def back_last(lens, q, kv, lse, da, cosine, signed, hid, gains, attn_w, gm, sets):
    vm, n = pltpu.VMEM, 64
    return pl.pallas_call(
        back_last_body,
        out_shape=ATTEND_OUTS + (
            shape((64, 2560), BF), shape((256, STRIP), BF), shape((2, 256, 2560), BF), shape((64, STRIP), BF), shape((64, STRIP), BF),
        ),
        in_specs=[SM] + [VM] * 8 + [HBM, VM] + [HBM] * 15,
        out_specs=[VM] * 3 + [HBM] * 5,
        scratch_shapes=ATTEND_SLOTS + [
            vm((4, 256, 2560), BF), vm((3, 2, 256, 2560), BF), vm((2, 3, 32, 2560), BF), vm((2, 3, 128, STRIP), BF),
            vm((2, 2, 64, 2560), BF), vm((2, 2, 256, STRIP), BF), vm((2, 64, 2560), BF), vm((2, 256, STRIP), BF),
            vm((3, 1, 64, STRIP), BF), vm((3, 1, 64, STRIP), BF), vm((1, 64, STRIP), BF), vm((1, 64, STRIP), BF),
            vm((2, 2 * ROWS, D), BF), vm((2, 2 * ROWS, 2560), BF),
            pltpu.SemaphoreType.DMA((10,)), pltpu.SemaphoreType.DMA((10,)), pltpu.SemaphoreType.DMA((n,)), pltpu.SemaphoreType.DMA((n,)),
        ],
        compiler_params=linked(8, 63),
        name="back_last",
    )(lens, q, kv, lse, da, cosine, signed, hid, gains, attn_w, gm, *[a for trio in sets for a in trio])


def finish_body(*refs):
    n1, att, packed, gao = (refs[3 * i : 3 * i + 3] for i in range(4))
    ta_in, tb_in, own_in, ua_in, ub_in = refs[12:17]
    parts = refs[17:23]
    (out, gains_out, gains, stage, own, left, left_b, right_p, right_q, hx, hy, rx, ry, ta, tb, rx2, ry2,
     ua, ub, rz, g_core, g_mine, g_x, g_y, send, recv, local, live_sems) = refs[23:]
    spot = Spot()
    spot.call()
    x, y = spot.x, spot.y
    live = Live(live_sems)
    brought = [
        pltpu.make_async_copy(src, dst, local.at[1 + i])
        for i, (src, dst) in enumerate(
            ((ub_in, ub.at[3]), (own_in, own.at[1]), (ta_in, ta.at[2]), (tb_in, tb.at[2]), (ua_in, ua.at[3]))
        )
    ]
    for copy in brought:
        copy.start()
    waits = [live.load(n1, left), live.load(packed, right_p), live.load(att, left_b), live.load(gao, right_q)]
    stage[:, pl.ds(240, 16)] = jnp.zeros((4, 16, 2560), BF)
    gains[...] = jnp.zeros((4, 8, 256), F32)
    for i in range(2):
        total = parts[i][...] + parts[2 + i][...] + parts[4 + i][...]
        for f in range(4):
            gains[f, i : i + 1, 0:240] = total[:, 240 * f : 240 * f + 240]
    spot.hear()
    mover = Mover(send, recv)
    sums = Sums(spot, mover, stage=stage, own=own, hx=hx, hy=hy, rx=rx, ry=ry, ta=ta, tb=tb, rx2=rx2, ry2=ry2, ua=ua, ub=ub, rz=rz)
    pa, pb = spot.zl * 2 + 1 - spot.c, (1 - spot.zl) * 2 + 1 - spot.c
    small = [mover.push(gains.at[p], g_core.at[i], spot.core) for i, p in enumerate((pa, pb))]
    for copy in brought:
        copy.wait()
    sums.to_z(3)
    sums.next(1)
    sums.cross(2)
    for wait in waits:
        wait()
    for i in range(2):
        if i == 0:
            value = dot_tn(left[...], right_p[:, :1280])
        else:
            value = jnp.concatenate([dot_tn(left[...], right_p[:, 1280:1600]), dot_tn(left_b[...], right_q[...])], axis=1)
        for f in range(4):
            stage[f, pl.ds(0, 240), pl.ds(1280 * i, 1280)] = value[240 * f : 240 * f + 240].astype(BF)
        sums.to_core(0, pl.ds(1280 * i, 1280))
    for i, f in enumerate((spot.zl * 2 + spot.c, (1 - spot.zl) * 2 + spot.c)):
        small[i].wait_recv()
        g_mine[0, i] = gains[f] + g_core[i]
    gx = [mover.push(g_mine.at[0], g_x.at[i], spot.along_x(k)) for i, k in enumerate(OFFSETS)]

    rows = (0, (0, 32)), (1, (32, 32))

    def view_of(ms):
        def view(part, a, b):
            return out.at[(ms,) + chunk_at(moved(x, a), part) + (strip_at(moved(y, b)),)]

        return view

    def begin(ms):
        keep = pltpu.make_async_copy(ua.at[ms], out.at[ms, x, :, strip_at(y)], local.at[0])
        keep.start()
        keep.wait()
        return [ring_inner(mover, spot, *part, view_of(ms)) for part in rows]

    def go_on(ms):
        return [ring_outer(mover, spot, *part, view_of(ms), lambda ref: None) for part in rows]

    def step(*sides):
        for pair in sides:
            for side in pair:
                next(side)

    sums.one(0)
    sums.four(2)
    sums.to_z(2)
    sums.three(1, ta.at[1], tb.at[1])
    sums.cross(1)
    for copy in gx:
        copy.wait_recv()
    g_mine[1] = g_mine[0] + g_x[0] + g_x[1] + g_x[2]
    gy = [mover.push(g_mine.at[1], g_y.at[i], spot.along_y(k)) for i, k in enumerate(OFFSETS)]
    sums.two(0)
    sums.next(0)
    sums.five(3)
    sums.five(2)
    sums.four(1)
    sums.to_z(1)
    for copy in gy:
        copy.wait_recv()
    g_mine[2] = g_mine[1] + g_y[0] + g_y[1] + g_y[2]
    gz = mover.push(g_mine.at[2, 1], g_core.at[2], spot.z)
    sums.five(1)
    wide = begin(pl.ds(1, 3))
    step(wide)
    sums.three(0, ta.at[0], tb.at[0])
    sums.cross(0)
    step(wide)
    sums.four(0)
    sums.to_z(0)
    step(wide)
    third, second, first = (go_on(pl.ds(m, 1)) for m in (3, 2, 1))
    step(third)
    sums.five(0)
    last = begin(pl.ds(0, 1))
    step(last)
    step(second)
    gz.wait_recv()
    gains_out[...] = g_mine[2, 0] + g_core[2]
    step(last)
    step(first)
    step(last)
    last = go_on(pl.ds(0, 1))
    step(last)
    step(third, second, first)
    step(last)
    step(third, second, first)
    step(last)
    mover.finish()


def finish(sets, begun, parts):
    vm, n = pltpu.VMEM, 128
    return pl.pallas_call(
        finish_body,
        out_shape=(shape((4, 4, 64, 2560), BF), shape((8, 256), F32)),
        in_specs=[HBM] * 17 + [VM] * 6,
        out_specs=[HBM, VM],
        scratch_shapes=[
            vm((4, 8, 256), F32), vm((4, 256, 2560), BF), vm((2, 2, 256, 2560), BF),
            vm((2 * ROWS, D), BF), vm((2 * ROWS, D), BF), vm((2 * ROWS, 1664), BF), vm((2 * ROWS, D), BF),
            vm((2, 1, 32, 2560), BF), vm((2, 1, 128, STRIP), BF), vm((2, 2, 64, 2560), BF), vm((2, 2, 256, STRIP), BF),
            vm((4, 64, 2560), BF), vm((4, 256, STRIP), BF), vm((3, 4, 64, STRIP), BF), vm((3, 4, 64, STRIP), BF),
            vm((4, 64, STRIP), BF), vm((4, 64, STRIP), BF), vm((4, 64, STRIP), BF),
            vm((3, 8, 256), F32), vm((3, 2, 8, 256), F32), vm((3, 2, 8, 256), F32), vm((3, 2, 8, 256), F32),
            pltpu.SemaphoreType.DMA((n,)), pltpu.SemaphoreType.DMA((n,)), pltpu.SemaphoreType.DMA((7,)), pltpu.SemaphoreType.DMA((8,)),
        ],
        compiler_params=linked(2, 60),
        name="finish",
    )(*[a for trio in sets for a in trio], *begun, *[v for pair in parts for v in pair])


def pair_greet(spot, relay):
    barrier = pltpu.get_barrier_semaphore()
    for who in (spot.core, spot.z):
        pl.semaphore_signal(barrier, inc=1, device_id=who, device_id_type=MESH)
    if relay is None:
        pl.semaphore_wait(barrier, 2)
        return
    section, sender, ready = relay
    beyond = {"section": 1 - section}

    @pl.when(section == sender)
    def _():
        pl.semaphore_signal(barrier, inc=1, device_id=beyond, device_id_type=MESH)
        pl.semaphore_wait(barrier, 2)

    @pl.when(section != sender)
    def _():
        pl.semaphore_wait(barrier, 3)
        pl.semaphore_signal(ready, inc=1, device_id=beyond, device_id_type=MESH)


def relay_copy(section, src, dst, send, recv):
    return pltpu.make_async_remote_copy(
        src_ref=src, dst_ref=dst, send_sem=send, recv_sem=recv,
        device_id={"section": 1 - section}, device_id_type=MESH,
    )


def rope_tables(place):
    lane = lax.broadcasted_iota(jnp.int32, (ROWS, 128), 1)
    rows = lax.broadcasted_iota(jnp.int32, (ROWS, 128), 0) + place * ROWS
    frequencies = rope_base ** (-((lane % 32).astype(F32) * 2.0) / HEAD_DIM)
    angles = rows.astype(F32) * frequencies
    return jnp.cos(angles), jnp.sin(angles) * jnp.where(lane % 64 < 32, -1.0, 1.0)


def shards(
    block_input, cotangent, lengths, w_query, w_key, w_value, w_out, w_gate, w_up, w_down, gain_attn, gain_mlp
):
    cosine, signed = rope_tables(lax.axis_index("fsdp"))
    inputs_t = block_input.transpose(0, 2, 1)
    cot_t = cotangent.transpose(0, 2, 1)
    kept, outs = [], []
    attn_w, ff_w, gains, hid, n1, q, kv, att, lse = first_attention(
        lengths, w_key[0].T, w_value[0].T, w_query[0], w_out[0], gain_attn, gain_mlp, inputs_t, cosine, signed,
        w_gate[0], w_up[0], w_down[0].T,
    )
    attn_w, ff_w = attn_w.reshape(4, 256, 2560), ff_w.reshape(3, 4, 256, 2560)
    for step in range(2):
        here = (hid, n1, q, kv, lse)
        out_t, mid, n2, gate, up, mixed, compact, hid, n1, q, kv, att, lse = forward(
            step, lengths, att, hid, inputs_t, gains, attn_w, ff_w, cosine, signed
        )
        outs.append(out_t)
        kept.append(here + (mid, n2, gate, up, mixed, compact))
    out_t, n2, mixed, compact, gg, gu, gm, gao, part_two, da, g_out = turn_back(
        lengths, att, hid, cot_t, gains, attn_w, ff_w
    )
    outs.append(out_t)
    kept.append((hid, n1, q, kv, lse, None, n2, None, None, mixed, compact))
    grads, parts, terms = [], [], []
    for step in range(3):
        hid, n1, q, kv, lse, _, n2, _, _, mixed, compact = kept[2 - step]
        before = (n1, compact, n2, g_out)
        after = (gao, gg, gu, mixed)
        if step < 2:
            mid, gate, up = (kept[1 - step][i] for i in (5, 7, 8))
            grad_t, packed, part_one, gg, gu, gm, gao, next_two, da, g_out = backward(
                step, lengths, q, kv, lse, da, cosine, signed, hid, gains, attn_w, ff_w, gm, cot_t, mid, gate, up
            )
        else:
            live = [(*(terms[k][i] for k in (0, 1)), (before + (None,) + after)[i]) for i in (3, 8, 2, 7, 6)]
            grad_t, packed, part_one, *begun = back_last(
                lengths, q, kv, lse, da, cosine, signed, hid, gains, attn_w, gm, live
            )
        grads.append(grad_t)
        parts.append((part_one, part_two))
        part_two = next_two
        terms.append(before + (packed,) + after)
    live = list(zip(*terms))
    summed, gain_sums = finish([live[i] for i in (0, 1, 4, 5)], begun, parts)
    query, key_t, value_t, out, gain_a, gain_b, gate, up, down_t, layer_out, input_grad = unpack(
        summed.reshape(4, 256, 2560), gain_sums, outs, grads
    )
    return (
        layer_out.transpose(0, 2, 1)[None],
        input_grad.transpose(0, 2, 1)[None],
        query[None],
        key_t.T[None],
        value_t.T[None],
        out[None],
        gate[None],
        up[None],
        down_t.T[None],
        gain_a,
        gain_b,
    )


def solution(mesh):
    tokens, two = ("dp", "fsdp"), P("section", "fsdp", None)
    return jax.shard_map(
        shards,
        mesh=mesh,
        in_specs=(P(None, tokens, None), P(None, tokens, None), P("dp", None)) + (two,) * 7 + (P("section", "fsdp"),) * 2,
        out_specs=(P("section", None, tokens, None),) * 2 + (two,) * 7 + (P("section", "fsdp"),) * 2,
        check_vma=False,
    )
```

```python
import functools

import jax
import jax.numpy as jnp
from jax import lax
from jax.experimental import pallas as pl
from jax.experimental.pallas import tpu as pltpu
from jax.sharding import PartitionSpec as P

HEADS = 15
KV_HEADS = 5
GROUP = 3
HEAD_DIM = 64
D = 960
ROWS = 256
STRIP = 640
SEQ = 1024
norm_eps = 1e-05
rope_base = 10000.0
masked_score = -1e30
BF = jnp.bfloat16
F32 = jnp.float32


def dot(a, b):
    return jnp.dot(a, b, preferred_element_type=F32)


def dot_nt(a, b):
    return lax.dot_general(a, b, (((1,), (1,)), ((), ())), preferred_element_type=F32)


def lanes(rows=ROWS):
    return lax.broadcasted_iota(jnp.int32, (rows, 128), 1)


def turn(tile, cosine, signed, low_half):
    partner = jnp.where(low_half, pltpu.roll(tile, 96, 1), pltpu.roll(tile, 32, 1))
    return tile * cosine + partner * signed


def whole(shape):
    return pl.BlockSpec(shape, lambda *_: (0,) * len(shape))


def params(limit=56):
    return pltpu.CompilerParams(vmem_limit_bytes=limit * 2**20)


def linked(collective_id, limit=56):
    return pltpu.CompilerParams(collective_id=collective_id, has_side_effects=True, vmem_limit_bytes=limit * 2**20)


VM = pl.BlockSpec(memory_space=pltpu.VMEM)
HBM = pl.BlockSpec(memory_space=pl.ANY)
SM = pl.BlockSpec(memory_space=pltpu.SMEM)


def shape(dims, kind):
    return jax.ShapeDtypeStruct(dims, kind)


def gain_row(gains, i):
    return jnp.concatenate([gains[f].astype(F32)[i : i + 1, :240] for f in range(4)], axis=1)


class Several:
    def __init__(self, copies):
        self.copies = copies

    def wait(self):
        for copy in self.copies:
            copy.wait()


class Streams:
    def __init__(self, sems):
        self.sems, self.count, self.open = sems, 0, []

    def start(self, src, dst):
        copy = pltpu.make_async_copy(src, dst, self.sems.at[self.count])
        self.count += 1
        copy.start()
        return copy

    def emit(self, src, dst):
        self.open.append(self.start(src, dst))

    def finish(self):
        for copy in self.open:
            copy.wait()


def unpack_body(summed, gains, *refs):
    layer_outs, grads = refs[:3], refs[3:6]
    q, k_t, v_t, out, gain_a, gain_b, gate, up, down_t, layer_out, input_grad = refs[6:17]
    raw, gate_s, up_s, down_s, layer_s, grad_s, q_s, k_s, v_s, out_s, sems = refs[17:]
    gain_a[...] = gains[0:1, 0:240]
    gain_b[...] = gains[1:2, 0:240]
    streams = Streams(sems)
    loads = [streams.start(summed.at[m, pl.ds(0, 240)], raw.at[m]) for m in range(4)]
    section = lax.axis_index("section")
    for i in range(2):
        for sources, slot in ((layer_outs, layer_s), (grads, grad_s)):
            first, second = (i, i + 1) if slot is layer_s else (2 - i, 1 - i)
            sem = sems.at[streams.count]
            streams.count += 1
            copies = [pltpu.make_async_copy(sources[k], slot.at[i], sem) for k in (first, second)]
            pl.when(section == 0)(copies[0].start)
            pl.when(section == 1)(copies[1].start)
            loads.append(copies[0])
    for m, slot, place in ((1, gate_s, gate), (2, up_s, up)):
        loads[m].wait()
        slot[...] = raw[m].astype(F32)
        streams.emit(slot, place)
    loads[3].wait()
    for j in range(4):
        down_s[240 * j : 240 * j + 240] = raw[3, :, STRIP * j : STRIP * j + STRIP].astype(F32)
    streams.emit(down_s, down_t)
    for load in loads[4:]:
        load.wait()
    streams.emit(layer_s, layer_out)
    streams.emit(grad_s, input_grad)
    loads[0].wait()
    attn = raw[0].astype(F32)
    keys = attn[:, :STRIP].T
    for value, slot, place in (
        (attn[:, STRIP:1600], q_s, q), (attn[:, 1600:], out_s, out), (keys[:320], k_s, k_t), (keys[320:], v_s, v_t)
    ):
        slot[...] = value
        streams.emit(slot, place)
    streams.finish()


def unpack(summed, gains, layer_outs, grads):
    dims = ((240, D), (320, 240), (320, 240), (240, D), (1, 240), (1, 240), (240, 2560), (240, 2560), (D, STRIP))
    return pl.pallas_call(
        unpack_body,
        out_shape=tuple(shape(s, F32) for s in dims) + (shape((2, D, ROWS), BF), shape((2, D, ROWS), F32)),
        in_specs=[HBM, VM] + [HBM] * 6,
        out_specs=[HBM] * 4 + [VM] * 2 + [HBM] * 5,
        scratch_shapes=[
            pltpu.VMEM((4, 240, 2560), BF), pltpu.VMEM((240, 2560), F32), pltpu.VMEM((240, 2560), F32),
            pltpu.VMEM((D, STRIP), F32), pltpu.VMEM((2, D, ROWS), BF), pltpu.VMEM((2, D, ROWS), F32),
            pltpu.VMEM((240, D), F32), pltpu.VMEM((320, 240), F32), pltpu.VMEM((320, 240), F32), pltpu.VMEM((240, D), F32),
            pltpu.SemaphoreType.DMA((17,)),
        ],
        compiler_params=params(),
        name="unpack",
    )(summed, gains, *layer_outs, *grads)


def fill_bias(bias, lens, slot, f):
    key = lax.broadcasted_iota(jnp.int32, (SEQ, ROWS), 0)
    place = lax.broadcasted_iota(jnp.int32, (SEQ, ROWS), 1) + f * ROWS
    one = jnp.where((key <= place) & (key < lens[0, slot]), 0.0, masked_score)
    for r in range(GROUP):
        bias[:, r * ROWS : (r + 1) * ROWS] = one


HEADS_SHAPE = (KV_HEADS, GROUP * ROWS, 128)
KEYS_SHAPE = (KV_HEADS, SEQ, 128)
WIDE, NARROW = (ROWS, 2560), (ROWS, D)


def head_rows(h):
    return slice(h % GROUP * ROWS, (h % GROUP + 1) * ROWS)


def front_part(step, spot, mover, streams, lens, hid, gains, load_w, w, cosine, signed, n1, q, kv, att, lse, bias, outs,
               between=None):
    section = lax.axis_index("section")
    slot = step // 2 if step != 1 else 1 - section
    h = hid[...].astype(F32)
    inverse = lax.rsqrt(jnp.mean(h * h, axis=-1, keepdims=True) + norm_eps)
    n = (h * inverse * gain_row(gains, 0)).astype(BF)
    n1[...] = n
    streams.emit(hid, outs[0])
    streams.emit(n1, outs[1])
    low = lanes() < 64
    half = lax.rem(lanes(), 64) < 32
    cos, sin = cosine[...], signed[...]
    load_w.wait()
    proj = dot(n, w[:, :STRIP])
    tile = [proj[:, 128 * i : 128 * i + 128] for i in range(5)]
    turned = [turn(tile[i], cos, sin, half) for i in range(3)]
    mine = pl.ds(pl.multiple_of(spot.f * ROWS, ROWS), ROWS)
    other = pl.ds(pl.multiple_of(((1 - spot.zl) * 2 + spot.c) * ROWS, ROWS), ROWS)
    across, near, far = [], [], []
    for g in range(KV_HEADS):
        k_tile, v_tile = turned[g // 2], tile[(5 + g) // 2]
        if g % 2 == 0:
            both = jnp.where(low, k_tile, v_tile)
        else:
            both = pltpu.roll(jnp.where(low, v_tile, k_tile), 64, 1)
        kv[g, mine] = both.astype(BF)
        block = kv.at[g, mine]
        across.append(mover.push(block, block, spot.z))
        near.append(mover.push(block, block, spot.core))
    proj = dot(n, w[:, STRIP:])
    for i in range(8):
        t = turn(proj[:, 128 * i : 128 * i + 128], cos, sin, half) * (HEAD_DIM**-0.5)
        for h in (2 * i, 2 * i + 1):
            if h < HEADS:
                part = pltpu.roll(t, 64, 1) if h % 2 else t
                q[h // GROUP, head_rows(h)] = jnp.where(low, part, 0.0).astype(BF)
    streams.emit(q, outs[2])
    fill_bias(bias, lens, slot, spot.f)

    def onward(g):
        across[g].wait_recv()
        block = kv.at[g, other]
        far.append(mover.push(block, block, spot.core))

    onward(0)
    for g in range(KV_HEADS):
        if g + 1 < KV_HEADS:
            onward(g + 1)
        near[g].wait_recv()
        far[g].wait_recv()
        if g + 1 == KV_HEADS:
            streams.emit(kv, outs[3])
        keys = kv[g]
        keys_t = keys.astype(F32).T.astype(BF)
        s = dot_nt(keys, q[g]) + bias[...]
        top = jnp.max(s, axis=0, keepdims=True)
        e = jnp.exp(s - top)
        total = jnp.sum(e, axis=0, keepdims=True)
        att[g] = (dot(keys_t, e.astype(BF)) / total).T.astype(BF)
        log_total = top + jnp.log(total)
        for r in range(GROUP):
            lse[g, r : r + 1] = log_total[:, r * ROWS : (r + 1) * ROWS]
        if between and g in between:
            between[g]()


FRONT_OUTS = (
    shape(NARROW, BF), shape(NARROW, BF), shape(HEADS_SHAPE, BF), shape(KEYS_SHAPE, BF),
    shape(HEADS_SHAPE, BF), shape((KV_HEADS, 8, ROWS), F32),
)
FRONT_SPECS = [HBM] * 4 + [VM] * 2
FRONT_SLOTS = [
    pltpu.VMEM((D, 1664), BF), pltpu.VMEM(NARROW, BF), pltpu.VMEM(NARROW, BF), pltpu.VMEM(HEADS_SHAPE, BF),
    pltpu.VMEM(KEYS_SHAPE, BF), pltpu.VMEM((SEQ, GROUP * ROWS), F32),
]


def load_columns(streams, attn, start, dst, flat=True):
    size = dst.shape[1]
    if not flat:
        return Several([
            streams.start(
                attn.at[f, i, pl.ds(0, 64 if i < 3 else 48), pl.ds(start, size)],
                dst.at[pl.ds(240 * f + 64 * i, 64 if i < 3 else 48)],
            )
            for f in range(4) for i in range(4)
        ])
    return Several([
        streams.start(attn.at[f, pl.ds(0, 240), pl.ds(start, size)], dst.at[pl.ds(240 * f, 240)]) for f in range(4)
    ])


def load_weights(streams, attn, ff, wo, wg, wu, wd, order):
    def load(k):
        if k == "o":
            return load_columns(streams, attn, 1536, wo)
        if k == "d":
            return Several([
                streams.start(
                    ff.at[2, f, pl.ds(0, 240), pl.ds(STRIP * j, STRIP)], wd.at[pl.ds(240 * j, 240), pl.ds(STRIP * f, STRIP)]
                )
                for f in range(4) for j in range(4)
            ])
        m, dst = (0, wg) if k == "g" else (1, wu)
        return Several([streams.start(ff.at[m, f, pl.ds(0, 240)], dst.at[pl.ds(240 * f, 240)]) for f in range(4)])

    return {k: load(k) for k in order}


def rest_part(streams, loads, att, hid, gains, wo, wg, wu, wd, mid_s, n2_s, gate_s, up_s, mixed_s, compact_s, out_s, outs):
    low = lanes() < 64

    def head(h):
        return att[h // GROUP, head_rows(h)].astype(F32)

    for h in range(0, HEADS - 1, 2):
        pair = jnp.where(low, pltpu.roll(head(h), 64, 1), head(h + 1))
        compact_s[:, 64 * h : 64 * h + 128] = pair.astype(BF)
    compact_s[:, 896:960] = pltpu.roll(head(HEADS - 1), 64, 1)[:, :64].astype(BF)
    streams.emit(compact_s, outs[5])
    loads["o"].wait()
    mid = hid[...].astype(F32) + dot(compact_s[...], wo[...])[:, 64:]
    mid_s[...] = mid
    inverse = lax.rsqrt(jnp.mean(mid * mid, axis=-1, keepdims=True) + norm_eps)
    n2_s[...] = (mid * inverse * gain_row(gains, 1)).astype(BF)
    if outs[0] is not None:
        streams.emit(mid_s, outs[0])
    streams.emit(n2_s, outs[1])
    loads["g"].wait()
    loads["u"].wait()
    for i in range(2):
        cols = slice(1280 * i, 1280 * i + 1280)
        n = n2_s[...]
        g = dot(n, wg[:, cols])
        u = dot(n, wu[:, cols])
        gate_s[:, cols] = g.astype(BF)
        up_s[:, cols] = u.astype(BF)
        mixed_s[:, cols] = (g * jax.nn.sigmoid(g) * u).astype(BF)
    if outs[2] is not None:
        streams.emit(gate_s, outs[2])
        streams.emit(up_s, outs[3])
    streams.emit(mixed_s, outs[4])
    loads["d"].wait()
    y = mid_s[...] + dot_nt(mixed_s[...], wd[...])
    out_s[...] = y.astype(BF)
    return y


WEIGHT_SLOTS = [pltpu.VMEM((D, 1024), BF)] + [pltpu.VMEM((D, 2560), BF)] * 3
REST_SLOTS = [
    pltpu.VMEM(NARROW, F32), pltpu.VMEM(NARROW, BF), pltpu.VMEM(WIDE, BF), pltpu.VMEM(WIDE, BF),
    pltpu.VMEM(WIDE, BF), pltpu.VMEM(NARROW, BF), pltpu.VMEM(NARROW, BF),
]


def forward_body(step, lens, att, hid, own_t, gains, attn_w, ff_w, cosine, signed,
                 out_t, o_mid, o_n2, o_gate, o_up, o_mixed, o_compact, o_hid, o_n1, o_q, o_kv, att_next, lse,
                 wo, wg, wu, wd, mid_s, n2_s, gate_s, up_s, mixed_s, compact_s, out_s,
                 w, hid_s, n1, q, kv, bias, passed_on, sems, front_sems, send, recv, ready):
    streams = Streams(sems)
    loads = load_weights(streams, attn_w, ff_w, wo, wg, wu, wd, "ogud")
    load_w = load_columns(streams, attn_w, 0, w)
    spot = Spot()
    section = lax.axis_index("section")
    pair_greet(spot, (section, 0, ready))
    y = rest_part(streams, loads, att, hid, gains, wo, wg, wu, wd, mid_s, n2_s, gate_s, up_s, mixed_s, compact_s, out_s,
                  (o_mid, o_n2, o_gate, o_up, o_mixed, o_compact))

    @pl.when(section == 0)
    def _():
        pl.semaphore_wait(ready, 1)
        relay_copy(section, out_s, passed_on, send.at[15], recv.at[15]).start()
        hid_s[...] = own_t[1].astype(F32).T.astype(BF)

    out_t[...] = y.T.astype(BF)

    @pl.when(section == 1)
    def _():
        relay_copy(section, out_s, passed_on, send.at[15], recv.at[15]).wait_recv()
        hid_s[...] = passed_on[...]

    def attention():
        mover = Mover(send, recv)
        inner = Streams(front_sems)
        front_part(step + 1, spot, mover, inner, lens, hid_s, gains, load_w, w, cosine, signed, n1, q, kv, att_next, lse, bias,
                   (o_hid, o_n1, o_q, o_kv))
        mover.finish()
        inner.finish()

    if step == 0:
        attention()
    else:
        pl.when(section == 1)(attention)

        @pl.when(section == 0)
        def _():
            inner = Streams(front_sems)
            load_w.wait()
            for slot, place in ((hid_s, o_hid), (n1, o_n1), (q, o_q), (kv, o_kv)):
                slot[...] = jnp.zeros(slot.shape, slot.dtype)
                inner.emit(slot, place)
            att_next[...] = jnp.zeros(att_next.shape, BF)
            lse[...] = jnp.zeros(lse.shape, F32)
            inner.finish()

    @pl.when(section == 0)
    def _():
        relay_copy(section, out_s, passed_on, send.at[15], recv.at[15]).wait_send()

    streams.finish()


def forward(step, lens, att, hid, own_t, gains, attn_w, ff_w, cosine, signed):
    rest_outs = (shape((D, ROWS), BF), shape(NARROW, F32), shape(NARROW, BF)) + (shape(WIDE, BF),) * 3 + (shape(NARROW, BF),)
    return pl.pallas_call(
        functools.partial(forward_body, step),
        out_shape=rest_outs + FRONT_OUTS,
        in_specs=[SM, VM, VM, VM, VM, HBM, HBM, VM, VM],
        out_specs=[VM] + [HBM] * 6 + FRONT_SPECS,
        scratch_shapes=WEIGHT_SLOTS + REST_SLOTS + FRONT_SLOTS + [
            pltpu.VMEM(NARROW, BF), pltpu.SemaphoreType.DMA((42,)), pltpu.SemaphoreType.DMA((4,)), pltpu.SemaphoreType.DMA((16,)),
            pltpu.SemaphoreType.DMA((16,)), pltpu.SemaphoreType.REGULAR,
        ],
        compiler_params=linked(4 + step, 60),
        name="forward",
    )(lens, att, hid, own_t, gains, attn_w, ff_w, cosine, signed)


def back_rest_part(streams, loads, g_out, gains, mid_ref, gate_s, up_s, gg_s, gu_s, gm_s, wo, wg, wu, wd, gao_out, part, da, outs):
    loads["d"].wait()
    for i in range(2):
        cols = slice(1280 * i, 1280 * i + 1280)
        grad_mixed = dot(g_out[...], wd[:, cols])
        ga = gate_s[:, cols].astype(F32)
        sg = jax.nn.sigmoid(ga)
        scaled = grad_mixed * sg
        gg_s[:, cols] = (scaled * up_s[:, cols].astype(F32) * (1.0 + ga * (1.0 - sg))).astype(BF)
        gu_s[:, cols] = (scaled * ga).astype(BF)
    streams.emit(gg_s, outs[0])
    streams.emit(gu_s, outs[1])
    loads["g"].wait()
    loads["u"].wait()
    grad_normed = dot_nt(gg_s[...], wg[...]) + dot_nt(gu_s[...], wu[...])
    mid = mid_ref[...]
    inverse = lax.rsqrt(jnp.mean(mid * mid, axis=-1, keepdims=True) + norm_eps)
    unit = mid * inverse
    part[...] = jnp.sum(grad_normed * unit, axis=0, keepdims=True)
    scaled_two = grad_normed * gain_row(gains, 1)
    gm = g_out[...].astype(F32) + inverse * (
        scaled_two - unit * jnp.mean(scaled_two * unit, axis=-1, keepdims=True)
    )
    gm_s[...] = gm
    streams.emit(gm_s, outs[2])
    gao_out[...] = gm.astype(BF)
    shifted = jnp.concatenate([jnp.zeros((ROWS, 64), F32), gm], axis=1).astype(BF)
    loads["o"].wait()
    att = jnp.concatenate([dot_nt(shifted, wo[...]), jnp.zeros((ROWS, 64), F32)], axis=1)
    low = lanes() < 64
    for h in range(HEADS):
        tile = att[:, 128 * (h // 2) : 128 * (h // 2) + 128]
        if h % 2 == 0:
            tile = pltpu.roll(tile, 64, 1)
        da[h // GROUP, head_rows(h)] = jnp.where(low, 0.0, tile).astype(BF)


def live_cotangent(step, lens, cot_t):
    place = lax.broadcasted_iota(jnp.int32, (D, ROWS), 1) + lax.axis_index("fsdp") * ROWS
    return jnp.where(place < lens[0, 1 - step], cot_t[1 - step].astype(F32), 0.0).T.astype(BF)


BACK_OUTS = (
    shape(WIDE, BF), shape(WIDE, BF), shape(NARROW, F32), shape(NARROW, BF), shape((1, D), F32),
    shape(HEADS_SHAPE, BF), shape(NARROW, BF),
)
BACK_SPECS = [HBM] * 3 + [VM] * 4


class Done:
    def wait(self):
        pass


def forward_turn_body(lens, att, hid, own_t, gains, attn_w, ff_w, cosine, signed, cot_t,
                      out_t, o_mid, o_n2, o_gate, o_up, o_mixed, o_compact, o_hid, o_n1, o_q, o_kv, lse,
                      last_t, t_n2, t_mixed, t_compact, o_gg, o_gu, o_gm, gao, part, da, g_out,
                      wo, wg, wu, wd, mid_s, n2_s, gate_s, up_s, mixed_s, compact_s, out_s,
                      w, hid_s, n1, q, kv, bias, att_next, gg_s, gu_s, gm_s,
                      passed_on, sems, front_sems, turn_sems, send, recv, ready):
    forward_body(1, lens, att, hid, own_t, gains, attn_w, ff_w, cosine, signed,
                 out_t, o_mid, o_n2, o_gate, o_up, o_mixed, o_compact, o_hid, o_n1, o_q, o_kv, att_next, lse,
                 wo, wg, wu, wd, mid_s, n2_s, gate_s, up_s, mixed_s, compact_s, out_s,
                 w, hid_s, n1, q, kv, bias, passed_on, sems, front_sems, send, recv, ready)
    streams = Streams(turn_sems)
    loads = {k: Done() for k in "ogud"}
    y = rest_part(streams, loads, att_next, hid_s, gains, wo, wg, wu, wd, mid_s, n2_s, gate_s, up_s, mixed_s, compact_s, out_s,
                  (None, t_n2, None, None, t_mixed, t_compact))
    last_t[...] = y.T.astype(BF)
    g_out[...] = jnp.where(lax.axis_index("section") == 1, live_cotangent(0, lens, cot_t), 0.0).astype(BF)
    back_rest_part(streams, loads, g_out, gains, mid_s, gate_s, up_s, gg_s, gu_s, gm_s, wo, wg, wu, wd, gao, part, da,
                   (o_gg, o_gu, o_gm))
    streams.finish()


def forward_turn(lens, att, hid, own_t, gains, attn_w, ff_w, cosine, signed, cot_t):
    rest_outs = (shape((D, ROWS), BF), shape(NARROW, F32), shape(NARROW, BF)) + (shape(WIDE, BF),) * 3 + (shape(NARROW, BF),)
    turn_outs = (shape((D, ROWS), BF), shape(NARROW, BF), shape(WIDE, BF), shape(NARROW, BF)) + BACK_OUTS
    return pl.pallas_call(
        forward_turn_body,
        out_shape=rest_outs + FRONT_OUTS[:4] + FRONT_OUTS[5:] + turn_outs,
        in_specs=[SM, VM, VM, VM, VM, HBM, HBM, VM, VM, VM],
        out_specs=[VM] + [HBM] * 6 + [HBM] * 4 + [VM] + [VM] + [HBM] * 3 + BACK_SPECS,
        scratch_shapes=WEIGHT_SLOTS + REST_SLOTS + FRONT_SLOTS + [
            pltpu.VMEM(HEADS_SHAPE, BF), pltpu.VMEM(WIDE, BF), pltpu.VMEM(WIDE, BF), pltpu.VMEM(NARROW, F32),
            pltpu.VMEM(NARROW, BF), pltpu.SemaphoreType.DMA((42,)), pltpu.SemaphoreType.DMA((4,)), pltpu.SemaphoreType.DMA((6,)),
            pltpu.SemaphoreType.DMA((16,)), pltpu.SemaphoreType.DMA((16,)), pltpu.SemaphoreType.REGULAR,
        ],
        compiler_params=linked(5, 62),
        name="forward_turn",
    )(lens, att, hid, own_t, gains, attn_w, ff_w, cosine, signed, cot_t)


def back_attend_part(step, spot, mover, lens, q, kv, lse, da, cosine, signed, hid, gains, load_w, w, gm, packed, gain_part,
                     bias, part, near, passed, far, own, dq, between=None):
    section = lax.axis_index("section")
    slot = 1 - section if step == 1 else 1 - step // 2
    fill_bias(bias, lens, slot, spot.f)
    low = lanes() < 64
    half = lax.rem(lanes(), 64) < 32
    cos, sin = cosine[...], -signed[...]

    def rows_of(zl, c):
        return pl.ds(pl.multiple_of((zl * 2 + c) * ROWS, ROWS), ROWS)

    there, here = 1 - spot.zl, spot.zl
    core, across = {}, {}

    def stage_one(g):
        core[g][0].wait_recv()
        passed[g] = (part[g, rows_of(there, spot.c)].astype(F32) + near[g, 0].astype(F32)).astype(BF)
        across[g] = mover.push(passed.at[g], far.at[g], spot.z)
        core[g][1].wait_recv()
        own[g] = part[g, rows_of(here, spot.c)].astype(F32) + near[g, 1].astype(F32)

    def stage_two(g):
        across[g].wait_recv()
        own[g] = own[g] + far[g].astype(F32)

    for g in range(KV_HEADS):
        keys = kv[g]
        keys_t = keys.astype(F32).T.astype(BF)
        logs = jnp.concatenate([lse[g, r : r + 1] for r in range(GROUP)], axis=1)
        p = jnp.exp(dot_nt(keys, q[g]) + bias[...] - logs)
        dp = dot_nt(keys, da[g])
        delta = jnp.sum(p * dp, axis=0, keepdims=True)
        ds = (p * (dp - delta)).astype(BF)
        both = jnp.concatenate([ds, p.astype(BF)], axis=1)
        part[g] = dot(both, jnp.concatenate([q[g], da[g]], axis=0)).astype(BF)
        core[g] = (
            mover.push(part.at[g, rows_of(there, 1 - spot.c)], near.at[g, 0], spot.core),
            mover.push(part.at[g, rows_of(here, 1 - spot.c)], near.at[g, 1], spot.core),
        )
        grad_q = (dot(keys_t, ds) * (HEAD_DIM**-0.5)).T
        for r in range(GROUP):
            rows = slice(r * ROWS, (r + 1) * ROWS)
            dq[g, rows] = turn(grad_q[rows], cos, sin, half).astype(BF)
        if g > 0:
            stage_one(g - 1)
        if g > 1:
            stage_two(g - 2)
        if between and g in between:
            between[g]()

    def merged(left, right):
        return jnp.where(low, left, right)

    def flip(v):
        return pltpu.roll(v, 64, 1)

    def head(h):
        return dq[h // GROUP, head_rows(h)].astype(F32)

    stage_one(KV_HEADS - 1)
    for h in range(0, HEADS, 2):
        tile = merged(head(h), flip(head(h + 1)) if h + 1 < HEADS else 0.0)
        packed[:, STRIP + 64 * h : STRIP + 64 * h + 128] = tile.astype(BF)
    load_w.wait()
    grad_normed = dot_nt(packed[:, STRIP:], w[:, STRIP:])
    hidden = hid[...].astype(F32)
    inverse = lax.rsqrt(jnp.mean(hidden * hidden, axis=-1, keepdims=True) + norm_eps)
    unit = hidden * inverse
    stage_two(KV_HEADS - 2)
    stage_two(KV_HEADS - 1)
    both = [own[g] for g in range(KV_HEADS)]
    turned = [turn(b, cos, sin, half) for b in both]
    tiles = [
        merged(turned[0], flip(turned[1])),
        merged(turned[2], flip(turned[3])),
        merged(turned[4], both[0]),
        merged(flip(both[1]), both[2]),
        merged(flip(both[3]), both[4]),
    ]
    for i, tile in enumerate(tiles):
        packed[:, 128 * i : 128 * i + 128] = tile.astype(BF)
    grad_normed = grad_normed + dot_nt(packed[:, :STRIP], w[:, :STRIP])
    gain_part[...] = jnp.sum(grad_normed * unit, axis=0, keepdims=True)
    scaled = grad_normed * gain_row(gains, 0)
    return gm[...] + inverse * (scaled - unit * jnp.mean(scaled * unit, axis=-1, keepdims=True))


OWN_SHAPE = (KV_HEADS, ROWS, 128)
ATTEND_SLOTS = [
    pltpu.VMEM((SEQ, GROUP * ROWS), F32), pltpu.VMEM(KEYS_SHAPE, BF), pltpu.VMEM((KV_HEADS, 2, ROWS, 128), BF),
    pltpu.VMEM(OWN_SHAPE, BF), pltpu.VMEM(OWN_SHAPE, BF), pltpu.VMEM(OWN_SHAPE, F32), pltpu.VMEM(HEADS_SHAPE, BF),
    pltpu.VMEM((D, 1664), BF),
]
ATTEND_OUTS = (shape((D, ROWS), F32), shape((ROWS, 1664), BF), shape((1, D), F32))


def backward_body(step, lens, q, kv, lse, da, cosine, signed, hid, gains, attn_w, ff_w, gm, cot_t, mid, gate, up,
                  grad_t, packed, gain_part, o_gg, o_gu, o_gm, gao, part_two, da_next, g_out,
                  bias, part, near, passed, far, own, dq, w, wo, wg, wu, wd, gate_s, up_s, gg_s, gu_s, gm_s,
                  out_s, passed_on, sems, send, recv, ready):
    streams = Streams(sems)
    load_w = load_columns(streams, attn_w, 0, w)
    loads = load_weights(streams, attn_w, ff_w, wo, wg, wu, wd, "dguo")
    load_gate = streams.start(gate, gate_s)
    load_up = streams.start(up, up_s)
    spot = Spot()
    section = lax.axis_index("section")
    pair_greet(spot, (section, 1, ready))
    mover = Mover(send, recv)
    grad_in = back_attend_part(step, spot, mover, lens, q, kv, lse, da, cosine, signed, hid, gains, load_w, w, gm,
                               packed, gain_part, bias, part, near, passed, far, own, dq)
    out_s[...] = grad_in.astype(BF)

    @pl.when(section == 1)
    def _():
        pl.semaphore_wait(ready, 1)
        relay_copy(section, out_s, passed_on, send.at[15], recv.at[15]).start()
        if step == 0:
            g_out[...] = live_cotangent(1, lens, cot_t)
        else:
            g_out[...] = jnp.zeros(NARROW, BF)

    grad_t[...] = grad_in.T

    @pl.when(section == 0)
    def _():
        relay_copy(section, out_s, passed_on, send.at[15], recv.at[15]).wait_recv()
        g_out[...] = passed_on[...]

    load_gate.wait()
    load_up.wait()
    back_rest_part(streams, loads, g_out, gains, mid, gate_s, up_s, gg_s, gu_s, gm_s, wo, wg, wu, wd, gao, part_two, da_next,
                   (o_gg, o_gu, o_gm))
    mover.finish()

    @pl.when(section == 1)
    def _():
        relay_copy(section, out_s, passed_on, send.at[15], recv.at[15]).wait_send()

    streams.finish()


def backward(step, lens, q, kv, lse, da, cosine, signed, hid, gains, attn_w, ff_w, gm, cot_t, mid, gate, up):
    return pl.pallas_call(
        functools.partial(backward_body, step),
        out_shape=ATTEND_OUTS + BACK_OUTS,
        in_specs=[SM] + [VM] * 8 + [HBM, HBM, VM, VM, VM, HBM, HBM],
        out_specs=[VM] * 3 + BACK_SPECS,
        scratch_shapes=ATTEND_SLOTS + WEIGHT_SLOTS + [pltpu.VMEM(WIDE, BF)] * 4 + [
            pltpu.VMEM(NARROW, F32), pltpu.VMEM(NARROW, BF), pltpu.VMEM(NARROW, BF), pltpu.SemaphoreType.DMA((40,)),
            pltpu.SemaphoreType.DMA((16,)), pltpu.SemaphoreType.DMA((16,)), pltpu.SemaphoreType.REGULAR,
        ],
        compiler_params=linked(6 + step, 62),
        name="backward",
    )(lens, q, kv, lse, da, cosine, signed, hid, gains, attn_w, ff_w, gm, cot_t, mid, gate, up)


MESH = pl.DeviceIdType.MESH
SIDE = 4
OFFSETS = (1, 3, 2)
HALVES = ((0, 128), (128, 112))


class Spot:
    def __init__(self):
        d = lax.axis_index("dp")
        f = lax.axis_index("fsdp")
        self.x, self.y = d // SIDE, lax.rem(d, SIDE)
        self.zl, self.c = f // 2, lax.rem(f, 2)
        self.f = f
        self.core = {"fsdp": self.zl * 2 + 1 - self.c}
        self.z = {"fsdp": (1 - self.zl) * 2 + self.c}
        self.across = {"fsdp": (1 - self.zl) * 2 + 1 - self.c}

    def along_x(self, k):
        return {"dp": lax.rem(self.x + k, SIDE) * SIDE + self.y}

    def along_y(self, k):
        return {"dp": self.x * SIDE + lax.rem(self.y + k, SIDE)}

    def greet(self):
        self.call()
        self.hear()

    def call(self):
        barrier = pltpu.get_barrier_semaphore()
        ids = [self.core, self.z, self.across]
        for k in range(1, SIDE):
            ids += [self.along_x(k), self.along_y(k)]
        for who in ids:
            pl.semaphore_signal(barrier, inc=1, device_id=who, device_id_type=MESH)

    def hear(self):
        pl.semaphore_wait(pltpu.get_barrier_semaphore(), 9)


class Mover:
    def __init__(self, send, recv):
        self.send, self.recv, self.pending, self.count = send, recv, [], 0

    def push(self, src, dst, who):
        i = self.count
        self.count += 1
        copy = pltpu.make_async_remote_copy(
            src_ref=src, dst_ref=dst, send_sem=self.send.at[i], recv_sem=self.recv.at[i],
            device_id=who, device_id_type=MESH,
        )
        copy.start()
        self.pending.append(copy)
        return copy

    def finish(self):
        for copy in self.pending:
            copy.wait_send()


def ring_axes(spot, which, view):
    if which == 0:
        return spot.along_x, spot.along_y, view
    return spot.along_y, spot.along_x, lambda part, a, b: view(part, b, a)


def ring_inner(mover, spot, which, rows, view):
    inner, outer, at = ring_axes(spot, which, view)
    lo, size = rows
    both, one, two = rows, (lo, size // 2), (lo + size // 2, size // 2)
    own = at(both, 0, 0)
    near = [mover.push(own, own, inner(k)) for k in (1, 3)]
    yield
    for copy in near:
        copy.wait_recv()
    far = [mover.push(at(one, 3, 0), at(one, 3, 0), inner(1)), mover.push(at(two, 1, 0), at(two, 1, 0), inner(3))]
    yield
    for copy in far:
        copy.wait_recv()
    yield


def ring_outer(mover, spot, which, rows, view, onward, direct=()):
    inner, outer, at = ring_axes(spot, which, view)
    lo, size = rows
    both, one, two = rows, (lo, size // 2), (lo + size // 2, size // 2)
    line = at(both, None, 0)
    near = [mover.push(line, line, outer(k)) for k in (1, 3)]
    onward(line)
    yield
    for copy in near:
        copy.wait_recv()
    line = LATE if direct else None
    far = list(direct)
    far.append(mover.push(at(one, line, 3), at(one, line, 3), outer(1)))
    far.append(mover.push(at(two, line, 1), at(two, line, 1), outer(3)))
    onward(at(both, None, 3))
    onward(at(both, None, 1))
    yield
    for copy in far:
        copy.wait_recv()
    onward(at(both, None, 2))
    yield


LATE = "late"


def chunk_at(p, part):
    if p is None or p is LATE:
        return pl.ds(0, 4) if p is None else pl.ds(2, 2), pl.ds(*part)
    return pl.ds(lax.rem(p, SIDE), 1), pl.ds(*part)


def strip_at(p):
    if p is None or p is LATE:
        return pl.ds(0, 2560) if p is None else pl.ds(1280, 1280)
    return pl.ds(pl.multiple_of(lax.rem(p, SIDE) * STRIP, 128), STRIP)


def moved(p, a):
    return a if a is None or a is LATE else p + a


def chunk_rows(p, lo=0, size=64):
    return pl.ds(pl.multiple_of(lax.rem(p, SIDE) * 64 + lo, 16), size)


def strip_cols(p):
    return pl.ds(pl.multiple_of(lax.rem(p, SIDE) * STRIP, 128), STRIP)


def first_body(lens, k_t, v_t, wq, wo, gain_a, gain_b, own_t, cosine, signed, gate, up, down_t,
               attn_full, ff_full, gains_full, o_hid, o_n1, o_q, o_kv, att, lse,
               own, ff, gains, w, hid, n1, q, kv, bias, sems, send, recv):
    streams = Streams(sems)
    loads = [
        streams.start(gate, ff.at[0, pl.ds(0, 240)]),
        streams.start(up, ff.at[1, pl.ds(0, 240)]),
    ]
    for j in range(4):
        loads.append(streams.start(down_t.at[pl.ds(240 * j, 240)], ff.at[2, pl.ds(0, 240), pl.ds(STRIP * j, STRIP)]))
    spot = Spot()
    x, y, f = spot.x, spot.y, spot.f
    fz = (1 - spot.zl) * 2 + spot.c
    spot.call()
    keys = jnp.concatenate([k_t[...].astype(F32), v_t[...].astype(F32)], axis=0).T
    both = jnp.concatenate([wq[...].astype(F32), wo[...].astype(F32)], axis=1)
    for i in range(4):
        size = 64 if i < 3 else 48
        own[i, :size, :STRIP] = keys[64 * i : 64 * i + size].astype(BF)
        own[i, :size, STRIP:] = both[64 * i : 64 * i + size].astype(BF)
    own[3, 48:64] = jnp.zeros((16, 2560), BF)
    ff[:, pl.ds(240, 16)] = jnp.zeros((3, 16, 2560), BF)
    gains[...] = jnp.zeros((8, 256), F32)
    gains[0:1, 0:240] = gain_a[...].astype(F32)
    gains[1:2, 0:240] = gain_b[...].astype(F32)
    spot.hear()
    mover = Mover(send, recv)
    here = chunk_at(x, (0, 64)) + (strip_at(y),)
    first = mover.push(own.at[here], attn_full.at[(f,) + here], spot.z)
    for load in loads:
        load.wait()
    every = pl.ds(0, 3)
    there = (every, f, lax.rem(x, SIDE), pl.ds(0, 64), strip_at(y))
    second = mover.push(ff.at[every, chunk_rows(x), strip_at(y)], ff_full.at[there], spot.z)
    waits = [mover.push(gains, gains_full.at[f], {"fsdp": lax.rem(f + k, 4)}) for k in range(1, 4)]
    waits.append(mover.push(own, attn_full.at[f], spot.core))
    streams.emit(own, attn_full.at[f])
    gains_full[f] = gains[...]
    late = []

    def view(part, a, b):
        return attn_full.at[(fz,) + chunk_at(moved(x, a), part) + (strip_at(moved(y, b)),)]

    def ff_view(part, a, b):
        return ff_full.at[(every, fz) + chunk_at(moved(x, a), part) + (strip_at(moved(y, b)),)]

    def onward(ref):
        waits.append(mover.push(ref, ref, spot.core))

    def ff_onward(ref):
        late.append(mover.push(ref, ref, spot.core))

    parts = (0, (0, 32)), (1, (32, 32))
    sides = [ring_inner(mover, spot, *part, view) for part in parts]
    hid[...] = jnp.where(lax.axis_index("section") == 0, own_t[0].astype(F32).T, 0.0).astype(BF)
    first.wait_recv()
    for side in sides:
        next(side)
    direct = (
        [mover.push(ff.at[every, pl.ds(64 * i, 32), strip_at(y + 2)], ff_full.at[every, f, i, pl.ds(0, 32), strip_at(y + 2)], spot.z)
         for i in range(2)],
        [mover.push(ff.at[every, chunk_rows(x + 2, 32, 32), pl.ds(0, 1280)],
                    ff_full.at[every, f, lax.rem(x + 2, SIDE), pl.ds(32, 32), pl.ds(0, 1280)], spot.z)],
    )
    for i in range(4):
        late.append(mover.push(ff.at[every, pl.ds(64 * i, 64)], ff_full.at[every, f, i], spot.core))
        streams.emit(ff.at[every, pl.ds(64 * i, 64)], ff_full.at[every, f, i])
    for _ in range(2):
        for side in sides:
            next(side)
    sides = [ring_outer(mover, spot, *part, view, onward) for part in parts]
    for side in sides:
        next(side)
    second.wait_recv()
    ff_sides = [ring_inner(mover, spot, *part, ff_view) for part in parts]
    for _ in range(2):
        for side in ff_sides:
            next(side)
        for side in sides:
            next(side)
    for copy in waits:
        copy.wait_recv()
    for copy in streams.open[:1]:
        copy.wait()
    streams.open = streams.open[1:]
    load_w = load_columns(streams, attn_full, 0, w, flat=False)

    def inner_done():
        for side in ff_sides:
            next(side)
        outers.extend(ring_outer(mover, spot, *part, ff_view, ff_onward, direct[part[0]]) for part in parts)
        progress()

    outers = []

    def progress():
        for side in outers:
            next(side)

    inner_done()
    front_part(0, spot, mover, streams, lens, hid, gains_full, load_w, w, cosine, signed, n1, q, kv, att, lse, bias,
               (o_hid, o_n1, o_q, o_kv), {2: progress})
    progress()
    for copy in late:
        copy.wait_recv()
    mover.finish()
    streams.finish()


def first_attention(*operands):
    n = 112
    return pl.pallas_call(
        first_body,
        out_shape=(shape((4, 4, 64, 2560), BF), shape((3, 4, 4, 64, 2560), BF), shape((4, 8, 256), F32)) + FRONT_OUTS,
        in_specs=[SM] + [VM] * 9 + [HBM] * 3,
        out_specs=[HBM, HBM, VM] + FRONT_SPECS,
        scratch_shapes=[pltpu.VMEM((4, 64, 2560), BF), pltpu.VMEM((3, 256, 2560), BF), pltpu.VMEM((8, 256), F32)] + FRONT_SLOTS + [
            pltpu.SemaphoreType.DMA((32,)), pltpu.SemaphoreType.DMA((n,)), pltpu.SemaphoreType.DMA((n,)),
        ],
        compiler_params=linked(1),
        name="first_attention",
    )(*operands)


STEP = 16


def add_rows(out, rows, terms):
    def body(i, carry):
        sl = pl.ds(pl.multiple_of(i * STEP, STEP), STEP)
        total = terms[0](sl).astype(F32)
        for term in terms[1:]:
            total = total + term(sl).astype(F32)
        out(sl, total.astype(BF))
        return carry

    lax.fori_loop(0, rows // STEP, body, 0)


def dot_tn(a, b):
    return lax.dot_general(a, b, (((0,), (0,)), ((), ())), preferred_element_type=F32)


class Sums:
    def __init__(self, spot, mover, **slots):
        self.spot, self.mover, self.flights = spot, mover, {}
        self.__dict__.update(slots)

    def land(self, *key):
        for copy in self.flights[key]:
            copy.wait_recv()

    def chunk(self, k, lo=0, size=64):
        return chunk_rows(self.spot.x + k, lo, size)

    def strip(self, k):
        return strip_cols(self.spot.y + k)

    def to_core(self, m, cols=pl.ds(0, 2560)):
        spot, rows = self.spot, pl.ds(0, 256)
        flight = self.flights.setdefault(("core", m), [])
        for i, f in enumerate((spot.zl * 2 + 1 - spot.c, (1 - spot.zl) * 2 + 1 - spot.c)):
            flight.append(self.mover.push(self.stage.at[f, rows, cols], self.own.at[m, i, rows, cols], spot.core))

    def core_sent(self, m):
        for copy in self.flights["core", m]:
            copy.wait_send()
            self.mover.pending = [item for item in self.mover.pending if item is not copy]

    def one(self, m):
        self.land("core", m)
        spot, push, own = self.spot, self.mover.push, self.own
        for i, f in enumerate((spot.zl * 2 + spot.c, (1 - spot.zl) * 2 + spot.c)):
            def put(sl, v, i=i):
                own[m, i, sl] = v
            add_rows(put, 256, [lambda sl, i=i: own[m, i, sl], lambda sl, f=f: self.stage[f, sl]])
        self.flights["half", m] = (
            push(own.at[m, 0, self.chunk(2, 0, 32)], self.hx.at[0, m], spot.along_x(1)),
            push(own.at[m, 0, self.chunk(2, 32, 32)], self.hx.at[1, m], spot.along_x(3)),
            push(own.at[m, 1, pl.ds(0, 128), self.strip(2)], self.hy.at[0, m], spot.along_y(1)),
            push(own.at[m, 1, pl.ds(128, 128), self.strip(2)], self.hy.at[1, m], spot.along_y(3)),
        )

    def two(self, m):
        self.land("half", m)
        spot, own = self.spot, self.own
        for i, k in ((0, 1), (1, 3)):
            base = lax.rem(spot.x + k, SIDE) * 64 + 32 * i

            def rows(sl, base=base):
                return pl.ds(pl.multiple_of(base + sl.start, 16), STEP)

            def put(sl, v, rows=rows):
                own[m, 0, rows(sl)] = v
            add_rows(put, 32, [lambda sl, rows=rows: own[m, 0, rows(sl)], lambda sl, i=i: self.hx[i, m, sl]])

            def low(sl, i=i):
                return pl.ds(pl.multiple_of(128 * i + sl.start, 16), STEP)

            def put(sl, v, low=low, k=k):
                own[m, 1, low(sl), self.strip(k)] = v
            add_rows(put, 128, [lambda sl, low=low, k=k: own[m, 1, low(sl), self.strip(k)], lambda sl, i=i: self.hy[i, m, sl]])

    def next(self, m):
        spot, push, own = self.spot, self.mover.push, self.own
        self.flights["next", m] = tuple(
            copy
            for i, k in ((0, 1), (1, 3))
            for copy in (
                push(own.at[m, 0, self.chunk(k)], self.rx.at[i, m], spot.along_x(k)),
                push(own.at[m, 1, :, self.strip(k)], self.ry.at[i, m], spot.along_y(k)),
            )
        )

    def three(self, m, ta, tb):
        self.land("next", m)
        own, base = self.own, self.spot.x * 64

        def put(sl, v):
            ta[sl] = v
        first = lambda sl: own[m, 0, pl.ds(pl.multiple_of(base + sl.start, 16), STEP)]
        add_rows(put, 64, [first, lambda sl: self.rx[0, m, sl], lambda sl: self.rx[1, m, sl]])

        def put(sl, v):
            tb[sl] = v
        add_rows(put, 256, [lambda sl: own[m, 1, sl, self.strip(0)], lambda sl: self.ry[0, m, sl], lambda sl: self.ry[1, m, sl]])

    def cross(self, m):
        spot, push = self.spot, self.mover.push
        self.flights["second", m] = tuple(
            copy
            for i, k in enumerate(OFFSETS)
            for copy in (
                push(self.ta.at[m, :, self.strip(k)], self.ry2.at[i, m], spot.along_y(k)),
                push(self.tb.at[m, self.chunk(k)], self.rx2.at[i, m], spot.along_x(k)),
            )
        )

    def four(self, m):
        self.land("second", m)
        ta, tb, ua, ub, base = self.ta, self.tb, self.ua, self.ub, self.spot.x * 64

        def put(sl, v):
            ub[m, sl] = v
        first = lambda sl: tb[m, pl.ds(pl.multiple_of(base + sl.start, 16), STEP)]
        add_rows(put, 64, [first] + [lambda sl, i=i: self.rx2[i, m, sl] for i in range(3)])

        def put(sl, v):
            ua[m, sl] = v
        add_rows(put, 64, [lambda sl: ta[m, sl, self.strip(0)]] + [lambda sl, i=i: self.ry2[i, m, sl] for i in range(3)])

    def to_z(self, m):
        self.flights["z", m] = (self.mover.push(self.ub.at[m], self.rz.at[m], self.spot.z),)

    def five(self, m):
        self.land("z", m)
        ua = self.ua

        def put(sl, v):
            ua[m, sl] = v
        add_rows(put, 64, [lambda sl: ua[m, sl], lambda sl: self.rz[m, sl]])


class Live:
    def __init__(self, sems):
        self.sems, self.count = sems, 0

    def load(self, trio, dst):
        i = self.count
        self.count += 2
        section = lax.axis_index("section")
        fixed = pltpu.make_async_copy(trio[1], dst.at[pl.ds(ROWS, ROWS)], self.sems.at[i])
        fixed.start()
        early = pltpu.make_async_copy(trio[0], dst.at[pl.ds(0, ROWS)], self.sems.at[i + 1])
        late = pltpu.make_async_copy(trio[2], dst.at[pl.ds(0, ROWS)], self.sems.at[i + 1])
        pl.when(section == 1)(early.start)
        pl.when(section == 0)(late.start)

        def wait():
            fixed.wait()
            pl.when(section == 1)(early.wait)
            pl.when(section == 0)(late.wait)

        return wait


def wide_gradient(stage, tall, left, right):
    for i in range(2):
        v = dot_tn(left[...], right[:, pl.ds(1280 * i, 1280)])
        for f in range(4):
            if not tall:
                stage[f, pl.ds(0, 240), pl.ds(1280 * i, 1280)] = v[240 * f : 240 * f + 240].astype(BF)
            elif f // 2 == i:
                for j in range(4):
                    cols = slice(STRIP * (f % 2), STRIP * (f % 2) + STRIP)
                    stage[f, pl.ds(0, 240), pl.ds(STRIP * j, STRIP)] = v[240 * j : 240 * j + 240, cols].astype(BF)


def back_last_body(lens, q, kv, lse, da, cosine, signed, hid, gains, attn_w, gm, *refs):
    gd, mixed, n2, gu, gg = (refs[3 * i : 3 * i + 3] for i in range(5))
    (grad_t, packed, gain_part, ta_out, tb_out, own_out, ua_out, ub_out, bias, part, near, passed, far, own_keys, dq, w,
     stage, own, hx, hy, rx, ry, ta, tb, rx2, ry2, ua, ub, left, right, sems, live_sems, send, recv) = refs[15:]
    spot = Spot()
    spot.call()
    streams = Streams(sems)
    live = Live(live_sems)
    waits = {0: [live.load(gd, left.at[0]), live.load(mixed, right.at[0])]}
    load_w = load_columns(streams, attn_w, 0, w)
    waits[1] = [live.load(n2, left.at[1]), live.load(gu, right.at[1])]
    stage[:, pl.ds(240, 16)] = jnp.zeros((4, 16, 2560), BF)
    spot.hear()
    mover = Mover(send, recv)
    sums = Sums(spot, mover, stage=stage, own=own, hx=hx, hy=hy, rx=rx, ry=ry, ta=ta, tb=tb, rx2=rx2, ry2=ry2, ua=ua, ub=ub)

    def compute(k):
        for wait in waits[k]:
            wait()
        wide_gradient(stage, k == 0, left.at[min(k, 1)], right.at[k % 2])
        if k == 0:
            waits[2] = [live.load(gg, right.at[0])]
        sums.to_core(k)

    def after_one():
        sums.one(0)
        sums.core_sent(0)
        compute(1)

    def after_two():
        sums.one(1)
        sums.two(0)
        sums.next(0)
        sums.core_sent(1)
        compute(2)

    def after_three():
        sums.one(2)
        sums.two(1)
        sums.next(1)

    def after_four():
        sums.three(0, ta.at[0], tb.at[0])
        sums.cross(0)

    compute(0)
    grad_in = back_attend_part(2, spot, mover, lens, q, kv, lse, da, cosine, signed, hid, gains, load_w, w, gm,
                               packed, gain_part, bias, part, near, passed, far, own_keys, dq,
                               {1: after_one, 2: after_two, 3: after_three, 4: after_four})
    sums.two(2)
    streams.emit(own.at[2], own_out)
    grad_t[...] = grad_in.T
    sums.three(1, ta.at[1], tb.at[1])
    streams.emit(ta.at[1], ta_out)
    streams.emit(tb.at[1], tb_out)
    sums.four(0)
    streams.emit(ua.at[0], ua_out)
    streams.emit(ub.at[0], ub_out)
    mover.finish()
    streams.finish()


def back_last(lens, q, kv, lse, da, cosine, signed, hid, gains, attn_w, gm, sets):
    vm, n = pltpu.VMEM, 64
    return pl.pallas_call(
        back_last_body,
        out_shape=ATTEND_OUTS + (
            shape((64, 2560), BF), shape((256, STRIP), BF), shape((2, 256, 2560), BF), shape((64, STRIP), BF), shape((64, STRIP), BF),
        ),
        in_specs=[SM] + [VM] * 8 + [HBM, VM] + [HBM] * 15,
        out_specs=[VM] * 3 + [HBM] * 5,
        scratch_shapes=ATTEND_SLOTS + [
            vm((4, 256, 2560), BF), vm((3, 2, 256, 2560), BF), vm((2, 3, 32, 2560), BF), vm((2, 3, 128, STRIP), BF),
            vm((2, 2, 64, 2560), BF), vm((2, 2, 256, STRIP), BF), vm((2, 64, 2560), BF), vm((2, 256, STRIP), BF),
            vm((3, 1, 64, STRIP), BF), vm((3, 1, 64, STRIP), BF), vm((1, 64, STRIP), BF), vm((1, 64, STRIP), BF),
            vm((2, 2 * ROWS, D), BF), vm((2, 2 * ROWS, 2560), BF),
            pltpu.SemaphoreType.DMA((10,)), pltpu.SemaphoreType.DMA((10,)), pltpu.SemaphoreType.DMA((n,)), pltpu.SemaphoreType.DMA((n,)),
        ],
        compiler_params=linked(8, 63),
        name="back_last",
    )(lens, q, kv, lse, da, cosine, signed, hid, gains, attn_w, gm, *[a for trio in sets for a in trio])


def finish_body(*refs):
    n1, att, packed, gao = (refs[3 * i : 3 * i + 3] for i in range(4))
    ta_in, tb_in, own_in, ua_in, ub_in = refs[12:17]
    parts = refs[17:23]
    (out, gains_out, gains, stage, own, left, left_b, right_p, right_q, hx, hy, rx, ry, ta, tb, rx2, ry2,
     ua, ub, rz, g_core, g_mine, g_x, g_y, send, recv, local, live_sems) = refs[23:]
    spot = Spot()
    spot.call()
    x, y = spot.x, spot.y
    live = Live(live_sems)
    brought = [
        pltpu.make_async_copy(src, dst, local.at[1 + i])
        for i, (src, dst) in enumerate(
            ((ub_in, ub.at[3]), (own_in, own.at[1]), (ta_in, ta.at[2]), (tb_in, tb.at[2]), (ua_in, ua.at[3]))
        )
    ]
    for copy in brought:
        copy.start()
    waits = [live.load(n1, left), live.load(packed, right_p), live.load(att, left_b), live.load(gao, right_q)]
    stage[:, pl.ds(240, 16)] = jnp.zeros((4, 16, 2560), BF)
    gains[...] = jnp.zeros((4, 8, 256), F32)
    for i in range(2):
        total = parts[i][...] + parts[2 + i][...] + parts[4 + i][...]
        for f in range(4):
            gains[f, i : i + 1, 0:240] = total[:, 240 * f : 240 * f + 240]
    spot.hear()
    mover = Mover(send, recv)
    sums = Sums(spot, mover, stage=stage, own=own, hx=hx, hy=hy, rx=rx, ry=ry, ta=ta, tb=tb, rx2=rx2, ry2=ry2, ua=ua, ub=ub, rz=rz)
    pa, pb = spot.zl * 2 + 1 - spot.c, (1 - spot.zl) * 2 + 1 - spot.c
    small = [mover.push(gains.at[p], g_core.at[i], spot.core) for i, p in enumerate((pa, pb))]
    for copy in brought:
        copy.wait()
    sums.to_z(3)
    sums.next(1)
    sums.cross(2)
    for wait in waits:
        wait()
    for i in range(2):
        if i == 0:
            value = dot_tn(left[...], right_p[:, :1280])
        else:
            value = jnp.concatenate([dot_tn(left[...], right_p[:, 1280:1600]), dot_tn(left_b[...], right_q[...])], axis=1)
        for f in range(4):
            stage[f, pl.ds(0, 240), pl.ds(1280 * i, 1280)] = value[240 * f : 240 * f + 240].astype(BF)
        sums.to_core(0, pl.ds(1280 * i, 1280))
    for i, f in enumerate((spot.zl * 2 + spot.c, (1 - spot.zl) * 2 + spot.c)):
        small[i].wait_recv()
        g_mine[0, i] = gains[f] + g_core[i]
    gx = [mover.push(g_mine.at[0], g_x.at[i], spot.along_x(k)) for i, k in enumerate(OFFSETS)]

    rows = (0, (0, 32)), (1, (32, 32))

    def view_of(ms):
        def view(part, a, b):
            return out.at[(ms,) + chunk_at(moved(x, a), part) + (strip_at(moved(y, b)),)]

        return view

    def begin(ms):
        keep = pltpu.make_async_copy(ua.at[ms], out.at[ms, x, :, strip_at(y)], local.at[0])
        keep.start()
        keep.wait()
        return [ring_inner(mover, spot, *part, view_of(ms)) for part in rows]

    def go_on(ms):
        return [ring_outer(mover, spot, *part, view_of(ms), lambda ref: None) for part in rows]

    def step(*sides):
        for pair in sides:
            for side in pair:
                next(side)

    sums.one(0)
    sums.four(2)
    sums.to_z(2)
    sums.three(1, ta.at[1], tb.at[1])
    sums.cross(1)
    for copy in gx:
        copy.wait_recv()
    g_mine[1] = g_mine[0] + g_x[0] + g_x[1] + g_x[2]
    gy = [mover.push(g_mine.at[1], g_y.at[i], spot.along_y(k)) for i, k in enumerate(OFFSETS)]
    sums.two(0)
    sums.next(0)
    sums.five(3)
    sums.five(2)
    sums.four(1)
    sums.to_z(1)
    for copy in gy:
        copy.wait_recv()
    g_mine[2] = g_mine[1] + g_y[0] + g_y[1] + g_y[2]
    gz = mover.push(g_mine.at[2, 1], g_core.at[2], spot.z)
    sums.five(1)
    wide = begin(pl.ds(1, 3))
    step(wide)
    sums.three(0, ta.at[0], tb.at[0])
    sums.cross(0)
    step(wide)
    sums.four(0)
    sums.to_z(0)
    step(wide)
    third, second, first = (go_on(pl.ds(m, 1)) for m in (3, 2, 1))
    step(third)
    sums.five(0)
    last = begin(pl.ds(0, 1))
    step(last)
    step(second)
    gz.wait_recv()
    gains_out[...] = g_mine[2, 0] + g_core[2]
    step(last)
    step(first)
    step(last)
    last = go_on(pl.ds(0, 1))
    step(last)
    step(third, second, first)
    step(last)
    step(third, second, first)
    step(last)
    mover.finish()


def finish(sets, begun, parts):
    vm, n = pltpu.VMEM, 128
    return pl.pallas_call(
        finish_body,
        out_shape=(shape((4, 4, 64, 2560), BF), shape((8, 256), F32)),
        in_specs=[HBM] * 17 + [VM] * 6,
        out_specs=[HBM, VM],
        scratch_shapes=[
            vm((4, 8, 256), F32), vm((4, 256, 2560), BF), vm((2, 2, 256, 2560), BF),
            vm((2 * ROWS, D), BF), vm((2 * ROWS, D), BF), vm((2 * ROWS, 1664), BF), vm((2 * ROWS, D), BF),
            vm((2, 1, 32, 2560), BF), vm((2, 1, 128, STRIP), BF), vm((2, 2, 64, 2560), BF), vm((2, 2, 256, STRIP), BF),
            vm((4, 64, 2560), BF), vm((4, 256, STRIP), BF), vm((3, 4, 64, STRIP), BF), vm((3, 4, 64, STRIP), BF),
            vm((4, 64, STRIP), BF), vm((4, 64, STRIP), BF), vm((4, 64, STRIP), BF),
            vm((3, 8, 256), F32), vm((3, 2, 8, 256), F32), vm((3, 2, 8, 256), F32), vm((3, 2, 8, 256), F32),
            pltpu.SemaphoreType.DMA((n,)), pltpu.SemaphoreType.DMA((n,)), pltpu.SemaphoreType.DMA((7,)), pltpu.SemaphoreType.DMA((8,)),
        ],
        compiler_params=linked(2, 60),
        name="finish",
    )(*[a for trio in sets for a in trio], *begun, *[v for pair in parts for v in pair])


def pair_greet(spot, relay):
    barrier = pltpu.get_barrier_semaphore()
    for who in (spot.core, spot.z):
        pl.semaphore_signal(barrier, inc=1, device_id=who, device_id_type=MESH)
    if relay is None:
        pl.semaphore_wait(barrier, 2)
        return
    section, sender, ready = relay
    beyond = {"section": 1 - section}

    @pl.when(section == sender)
    def _():
        pl.semaphore_signal(barrier, inc=1, device_id=beyond, device_id_type=MESH)
        pl.semaphore_wait(barrier, 2)

    @pl.when(section != sender)
    def _():
        pl.semaphore_wait(barrier, 3)
        pl.semaphore_signal(ready, inc=1, device_id=beyond, device_id_type=MESH)


def relay_copy(section, src, dst, send, recv):
    return pltpu.make_async_remote_copy(
        src_ref=src, dst_ref=dst, send_sem=send, recv_sem=recv,
        device_id={"section": 1 - section}, device_id_type=MESH,
    )


def rope_tables(place):
    lane = lax.broadcasted_iota(jnp.int32, (ROWS, 128), 1)
    rows = lax.broadcasted_iota(jnp.int32, (ROWS, 128), 0) + place * ROWS
    frequencies = rope_base ** (-((lane % 32).astype(F32) * 2.0) / HEAD_DIM)
    angles = rows.astype(F32) * frequencies
    return jnp.cos(angles), jnp.sin(angles) * jnp.where(lane % 64 < 32, -1.0, 1.0)


def shards(
    block_input, cotangent, lengths, w_query, w_key, w_value, w_out, w_gate, w_up, w_down, gain_attn, gain_mlp
):
    cosine, signed = rope_tables(lax.axis_index("fsdp"))
    inputs_t = block_input.transpose(0, 2, 1)
    cot_t = cotangent.transpose(0, 2, 1)
    kept, outs = [], []
    attn_w, ff_w, gains, hid, n1, q, kv, att, lse = first_attention(
        lengths, w_key[0].T, w_value[0].T, w_query[0], w_out[0], gain_attn, gain_mlp, inputs_t, cosine, signed,
        w_gate[0], w_up[0], w_down[0].T,
    )
    attn_w, ff_w = attn_w.reshape(4, 256, 2560), ff_w.reshape(3, 4, 256, 2560)
    here = (hid, n1, q, kv, lse)
    out_t, mid, n2, gate, up, mixed, compact, hid, n1, q, kv, att, lse = forward(
        0, lengths, att, hid, inputs_t, gains, attn_w, ff_w, cosine, signed
    )
    outs.append(out_t)
    kept.append(here + (mid, n2, gate, up, mixed, compact))
    here = (hid, n1, q, kv, lse)
    out_t, mid, n2, gate, up, mixed, compact, hid, n1, q, kv, lse, *turned = forward_turn(
        lengths, att, hid, inputs_t, gains, attn_w, ff_w, cosine, signed, cot_t
    )
    outs.append(out_t)
    kept.append(here + (mid, n2, gate, up, mixed, compact))
    out_t, n2, mixed, compact, gg, gu, gm, gao, part_two, da, g_out = turned
    outs.append(out_t)
    kept.append((hid, n1, q, kv, lse, None, n2, None, None, mixed, compact))

    grads, parts, terms = [], [], []
    for step in range(3):
        hid, n1, q, kv, lse, _, n2, _, _, mixed, compact = kept[2 - step]
        before = (n1, compact, n2, g_out)
        after = (gao, gg, gu, mixed)
        if step < 2:
            mid, gate, up = (kept[1 - step][i] for i in (5, 7, 8))
            grad_t, packed, part_one, gg, gu, gm, gao, next_two, da, g_out = backward(
                step, lengths, q, kv, lse, da, cosine, signed, hid, gains, attn_w, ff_w, gm, cot_t, mid, gate, up
            )
        else:
            live = [(*(terms[k][i] for k in (0, 1)), (before + (None,) + after)[i]) for i in (3, 8, 2, 7, 6)]
            grad_t, packed, part_one, *begun = back_last(
                lengths, q, kv, lse, da, cosine, signed, hid, gains, attn_w, gm, live
            )
        grads.append(grad_t)
        parts.append((part_one, part_two))
        part_two = next_two
        terms.append(before + (packed,) + after)
    live = list(zip(*terms))
    summed, gain_sums = finish([live[i] for i in (0, 1, 4, 5)], begun, parts)
    query, key_t, value_t, out, gain_a, gain_b, gate, up, down_t, layer_out, input_grad = unpack(
        summed.reshape(4, 256, 2560), gain_sums, outs, grads
    )
    return (
        layer_out.transpose(0, 2, 1)[None],
        input_grad.transpose(0, 2, 1)[None],
        query[None],
        key_t.T[None],
        value_t.T[None],
        out[None],
        gate[None],
        up[None],
        down_t.T[None],
        gain_a,
        gain_b,
    )


def solution(mesh):
    tokens, two = ("dp", "fsdp"), P("section", "fsdp", None)
    return jax.shard_map(
        shards,
        mesh=mesh,
        in_specs=(P(None, tokens, None), P(None, tokens, None), P("dp", None)) + (two,) * 7 + (P("section", "fsdp"),) * 2,
        out_specs=(P("section", None, tokens, None),) * 2 + (two,) * 7 + (P("section", "fsdp"),) * 2,
        check_vma=False,
    )
```
